32 devices in a mesh: dp: 4 (over z), ctx: 2 (over y), tensor: 4 (over x, core).
Axes of the slice: x: 2, y: 2, z: 4, core: 2. Of those that a mesh axis runs over, the one named last changes fastest.
Arguments:
- tokens: bfloat16 [4, 1024, 1024], P('dp', 'ctx')
- segments: int32 [4, 1024], P('dp', 'ctx'), may hold values from 0 to 767, as said below
- padding: int32 [4, 1024], P('dp', 'ctx'), may hold values from 0 to 1, as said below
- cotangent: bfloat16 [4, 1024, 1024], P('dp', 'ctx'), may hold values from -6 to 6
- norm1_gain: float32 [1024], replicated, may hold values from 0.5 to 1.5
- norm1_shift: float32 [1024], replicated, may hold values from -2 to 2
- norm2_gain: float32 [1024], replicated, may hold values from 0.5 to 1.5
- norm2_shift: float32 [1024], replicated, may hold values from -2 to 2
- qkv_weight: bfloat16 [1024, 3, 1024], P(None, None, 'tensor'), may hold values from -0.1875 to 0.1875
- qkv_bias: float32 [3, 1024], P(None, 'tensor'), may hold values from -3 to 3
- out_weight: bfloat16 [1024, 1024], P('tensor'), may hold values from -1 to 1
- out_bias: float32 [1024], replicated, may hold values from -2 to 2
- up_weight: bfloat16 [1024, 4096], P(None, 'tensor'), may hold values from -0.1875 to 0.1875
- up_bias: float32 [4096], P('tensor'), may hold values from -3 to 3
- down_weight: bfloat16 [4096, 1024], P('tensor'), may hold values from -0.09375 to 0.09375
- down_bias: float32 [1024], replicated, may hold values from -2 to 2
Outputs:
- block_output: bfloat16 [4, 1024, 1024], P('dp', 'ctx')
- input_grad: bfloat16 [4, 1024, 1024], P('dp', 'ctx')
- grad_norm1_gain: float32 [1024], replicated
- grad_norm1_shift: float32 [1024], replicated
- grad_norm2_gain: float32 [1024], replicated
- grad_norm2_shift: float32 [1024], replicated
- grad_qkv: float32 [1024, 3, 1024], P(None, None, 'tensor')
- grad_qkv_bias: float32 [3, 1024], P(None, 'tensor')
- grad_out: float32 [1024, 1024], P('tensor')
- grad_out_bias: float32 [1024], replicated
- grad_up: float32 [1024, 4096], P(None, 'tensor')
- grad_up_bias: float32 [4096], P('tensor')
- grad_down: float32 [4096, 1024], P('tensor')
- grad_down_bias: float32 [1024], replicated
The draws below stay inside these ranges and needn't reach their ends.
Inputs may be any that keep to these rules, and one draw needn't show every extreme that they name: `segments`: within a sequence the ids never fall; a token's id is the position at which its document begins; the first token of a sequence begins a document. Each sequence is real tokens followed by a padding tail of 1 to 256 tokens, which lies inside the sequence's last document after at least one real token of it.
All inputs are finite; a program needn't handle non-finite values.
Results may differ from the reference program's by a relative error of at most 0.018.
Values may be sent and summed in bfloat16 or wider, within the bound.
No kernel may reach another device: no remote copies, remote signals or barrier semaphores. Data moves between devices by JAX's collectives and lax.ppermute only.
A program may use at most 128 MiB of HBM per device.

```python
import jax
import jax.numpy as jnp
from jax import lax

D = 1024
HEADS = 16
HEAD_DIM = 64
ROT = 16
FF = 4096
KBLOCK = 512
SEQ = 1024
SPAN = 512
BATCH = 4


def draw_segments(key, part):
    key = jax.random.fold_in(key, 3)
    keys_split = jax.random.split(key, 4)
    positions = jnp.arange(SEQ, dtype=jnp.int32)[None, :]
    opening = jax.random.randint(keys_split[0], (BATCH, 1), 1, SPAN // 2)
    closing = jax.random.randint(keys_split[1], (BATCH, 1), SEQ - SPAN, SEQ - SPAN // 2)
    chosen = jax.random.randint(keys_split[3], (), 0, BATCH)
    row_ids = jnp.arange(BATCH, dtype=jnp.int32)[:, None]
    closing = jnp.where(row_ids == chosen, SEQ - SPAN // 2 - 1, closing)
    mark_bits = jax.random.randint(keys_split[2], (BATCH, SEQ), 0, 24) == 0
    starts = mark_bits & (positions < opening) | (positions == 0) | (positions == opening) | (positions == closing)
    segment_ids = lax.cummax(jnp.where(starts, positions, 0), axis=1)
    return segment_ids.astype(jnp.int32)


def draw_padding(key, part):
    key = jax.random.fold_in(key, 5)
    positions = jnp.arange(SEQ, dtype=jnp.int32)[None, :]
    tail_len = jax.random.randint(key, (BATCH, 1), 1, SPAN // 2 + 1)
    return (positions < SEQ - tail_len).astype(jnp.int32)


def draw_tokens(key, part):
    key = jax.random.fold_in(key, 11)
    keys_split = jax.random.split(key, 3)
    row_scale = jnp.exp(jax.random.uniform(keys_split[0], (BATCH, SEQ, 1), jnp.float32, jnp.log(0.4), jnp.log(4.0)))
    col_scale = jnp.exp(jax.random.uniform(keys_split[1], (1, 1, D), jnp.float32, jnp.log(0.5), jnp.log(2.0)))
    base = jax.random.normal(keys_split[2], (BATCH, SEQ, D), jnp.float32)
    return (base * row_scale * col_scale).astype(jnp.bfloat16)


def shard_levels(stream_key, extent, cuts, least, high):
    loudness = 1.0
    for position, blocks in cuts:
        steps = jax.random.uniform(jax.random.fold_in(jax.random.fold_in(stream_key, 6), position), (blocks,), jnp.float32, least / len(cuts), high / len(cuts))
        loudness = loudness * jnp.repeat(jnp.exp(steps), extent[position] // blocks).reshape((-1,) + (1,) * (len(extent) - 1 - position))
    return loudness


def bell_draw(own_key, shape, deviation, limit, pieces=(), held_as=jnp.bfloat16):
    level = shard_levels(own_key, shape, pieces, -0.22, 0.18) if pieces else 1.0
    entries = jax.random.normal(own_key, shape, jnp.float32) * deviation * level
    return jnp.minimum(jnp.maximum(entries, -limit), limit).astype(held_as)


def setup_inputs(seed: int = 0) -> dict:
    streams_of = jax.random.split(jax.random.key(seed), 17)
    return {
        "tokens": draw_tokens(jax.random.fold_in(streams_of[16], 71), 0),
        "segments": draw_segments(jax.random.fold_in(streams_of[16], 71), 0),
        "padding": draw_padding(jax.random.fold_in(streams_of[16], 71), 0),
        "cotangent": bell_draw(streams_of[3], (BATCH, SEQ, D), 1.0, 6.0, ((0, 4), (1, 2))),
        "norm1_gain": jnp.clip(1.0 + 0.1 * jax.random.normal(streams_of[4], (D,), jnp.float32), 0.5, 1.5),
        "norm1_shift": bell_draw(streams_of[5], (D,), 0.3, 2.0, (), jnp.float32),
        "norm2_gain": jnp.clip(1.0 + 0.1 * jax.random.normal(streams_of[6], (D,), jnp.float32), 0.5, 1.5),
        "norm2_shift": bell_draw(streams_of[7], (D,), 0.3, 2.0, (), jnp.float32),
        "qkv_weight": bell_draw(streams_of[8], (D, 3, D), D ** -0.5, 0.1875, ((2, 4),)),
        "qkv_bias": bell_draw(streams_of[9], (3, D), 0.5, 3.0, ((1, 4),), jnp.float32),
        "out_weight": bell_draw(streams_of[10], (D, D), (D // 32) ** -0.5, 1.0, ((0, 4),)),
        "out_bias": bell_draw(streams_of[11], (D,), 0.3, 2.0, (), jnp.float32),
        "up_weight": bell_draw(streams_of[12], (D, FF), D ** -0.5, 0.1875, ((1, 4),)),
        "up_bias": bell_draw(streams_of[13], (FF,), 0.5, 3.0, ((0, 4),), jnp.float32),
        "down_weight": bell_draw(streams_of[14], (FF, D), FF ** -0.5, 0.09375, ((0, 4),)),
        "down_bias": bell_draw(streams_of[15], (D,), 0.3, 2.0, (), jnp.float32),
    }


@jax.custom_vjp
def low(v):
    return lax.optimization_barrier(v.astype(jnp.bfloat16)).astype(jnp.float32)

@jax.custom_vjp
def low_back(v):
    return v

def low_keep(v):
    return (low(v), None)

def low_pass(kept, grad):
    return (grad,)

def back_keep(v):
    return (v, None)

def back_low(kept, grad):
    return (low(grad),)
low.defvjp(low_keep, low_pass)
low_back.defvjp(back_keep, back_low)

def layer_norm(values, gain_vec, shift_vec):
    centre = lax.optimization_barrier(jnp.mean(values, axis=-1, keepdims=True))
    centred = values - centre
    spread = lax.optimization_barrier(jnp.mean(centred * centred, axis=-1, keepdims=True))
    return centred * lax.rsqrt(spread + 1e-05) * gain_vec + shift_vec

def rotary_tables(positions):
    half_dims = ROT // 2
    freq_index = jnp.arange(half_dims, dtype=jnp.float32)
    inverse = jnp.exp(freq_index * (-2.0 * jnp.log(10000.0) / ROT))
    angles = positions.astype(jnp.float32)[:, None] * inverse[None, :]
    return (jnp.cos(angles)[:, None, :], jnp.sin(angles)[:, None, :])

def rotate(values, cosine_tab, sine_tab):
    half_dims = ROT // 2
    first_half = values[..., :half_dims]
    second_half = values[..., half_dims:ROT]
    return jnp.concatenate([first_half * cosine_tab - second_half * sine_tab, second_half * cosine_tab + first_half * sine_tab, values[..., ROT:]], axis=-1)

def attend_block(queries, query_at, query_doc, keys_all, values_all, key_doc, key_at):
    scores = jnp.einsum('qhd,khd->hqk', queries, keys_all, precision=lax.Precision.HIGHEST) * HEAD_DIM ** (-0.5)
    scores = low_back(scores)
    visible = (key_at[None, :] <= query_at[:, None]) & ((key_doc[None, :] == query_doc[:, None]) | (key_at[None, :] == query_at[:, None]))
    masked = jnp.where(visible[None], scores, -1e+30)
    row_top = lax.optimization_barrier(jnp.max(masked, axis=-1, keepdims=True))
    weights = jnp.where(visible[None], jnp.exp(masked - row_top), 0.0)
    probs_row = low(weights / lax.optimization_barrier(jnp.sum(weights, axis=-1, keepdims=True)))
    return jnp.einsum('hqk,khd->qhd', probs_row, values_all, precision=lax.Precision.HIGHEST)

def layer(tokens_f, seg_row, pad_row, norm1_gain, norm1_shift, norm2_gain, norm2_shift, qkv_weight, qkv_bias, out_weight, out_bias, up_weight, up_bias, down_weight, down_bias):
    length = tokens_f.shape[0]
    normed1 = low(layer_norm(tokens_f, norm1_gain, norm1_shift))
    normed2 = low(layer_norm(tokens_f, norm2_gain, norm2_shift))
    projected = jnp.einsum('sd,dtf->stf', normed1, qkv_weight, precision=lax.Precision.HIGHEST) + qkv_bias[None]
    projected = low_back(projected).reshape(length, 3, HEADS, HEAD_DIM)
    positions = jnp.arange(length, dtype=jnp.int32)
    cosine_tab, sine_tab = rotary_tables(positions)
    queries = low(rotate(projected[:, 0], cosine_tab, sine_tab))
    keys_all = low(rotate(projected[:, 1], cosine_tab, sine_tab))
    values_all = low(projected[:, 2])
    key_doc = jnp.where(pad_row == 1, seg_row, -1)
    blocks = length // KBLOCK

    def block_fn(block_data):
        return attend_block(block_data[0], block_data[1], block_data[2], keys_all, values_all, key_doc, positions)
    attended = lax.map(jax.checkpoint(block_fn), (queries.reshape(blocks, KBLOCK, HEADS, HEAD_DIM), positions.reshape(blocks, KBLOCK), seg_row.reshape(blocks, KBLOCK)))
    attended = low(low_back(attended.reshape(length, D)))
    upward = low_back(jnp.dot(normed2, up_weight, precision=lax.Precision.HIGHEST) + up_bias)
    activated = low(jax.nn.gelu(upward, approximate=False))
    return tokens_f + jnp.dot(attended, out_weight, precision=lax.Precision.HIGHEST) + out_bias + jnp.dot(activated, down_weight, precision=lax.Precision.HIGHEST) + down_bias

def reference(tokens, segments, padding, cotangent, norm1_gain, norm1_shift, norm2_gain, norm2_shift, qkv_weight, qkv_bias, out_weight, out_bias, up_weight, up_bias, down_weight, down_bias):
    params = tuple((weight_arg.astype(jnp.float32) for weight_arg in (norm1_gain, norm1_shift, norm2_gain, norm2_shift, qkv_weight, qkv_bias, out_weight, out_bias, up_weight, up_bias, down_weight, down_bias)))

    def one_sequence(running, sequence):
        tokens_row, seg_row, pad_row, cot_row = sequence

        def forward(tokens_f, *weight_list):
            return layer(tokens_f, seg_row, pad_row, *weight_list)
        output, pullback = jax.vjp(forward, tokens_row.astype(jnp.float32), *params)
        gradients = pullback(cot_row.astype(jnp.float32))
        running = tuple((old_sum + gradient for old_sum, gradient in zip(running, gradients[1:])))
        return (running, (output.astype(jnp.bfloat16), gradients[0].astype(jnp.bfloat16)))
    zero_grads = tuple((jnp.zeros(weight_arg.shape, jnp.float32) for weight_arg in params))
    totals, outputs = lax.scan(one_sequence, zero_grads, (tokens, segments, padding, cotangent))
    return (outputs[0], outputs[1], totals[0], totals[1], totals[2], totals[3], totals[4], totals[5], totals[6], totals[7], totals[8], totals[9], totals[10], totals[11])
```

```python
import functools

import jax
import jax.numpy as jnp
from jax import lax
from jax.sharding import PartitionSpec as P
from jax.experimental import pallas as pl
from jax.experimental.pallas import tpu as pltpu

HEAD_DIM = 64
ROT = 16
KBLOCK = 512


def layer_norm(values, gain_vec, shift_vec):
    centre = jnp.mean(values, axis=-1, keepdims=True)
    centred = values - centre
    spread = jnp.mean(centred * centred, axis=-1, keepdims=True)
    return centred * lax.rsqrt(spread + 1e-05) * gain_vec + shift_vec


def norm_back(values, gain_vec, shift_vec, upstream):
    outcome, pullback = jax.vjp(layer_norm, values, gain_vec, shift_vec)
    return pullback(upstream)


def gelu_exact(values):
    return jax.nn.gelu(values, approximate=False)


def rotary_tables(positions):
    half_dims = ROT // 2
    freq_index = jnp.arange(half_dims, dtype=jnp.float32)
    inverse = jnp.exp(freq_index * (-2.0 * jnp.log(10000.0) / ROT))
    angles = positions.astype(jnp.float32)[:, None] * inverse[None, :]
    return (jnp.cos(angles)[:, None, :], jnp.sin(angles)[:, None, :])


def rotate(values, cosine_tab, sine_tab):
    half_dims = ROT // 2
    first_half = values[..., :half_dims]
    second_half = values[..., half_dims:ROT]
    return jnp.concatenate(
        [
            first_half * cosine_tab - second_half * sine_tab,
            second_half * cosine_tab + first_half * sine_tab,
            values[..., ROT:],
        ],
        axis=-1,
    )


def score_block(query_block, key_block, query_at, query_doc, key_at, key_doc):
    scores = jnp.einsum(
        "qhd,khd->hqk", query_block, key_block, preferred_element_type=jnp.float32
    ) * HEAD_DIM ** (-0.5)
    visible = (key_at[None, :] <= query_at[:, None]) & (
        (key_doc[None, :] == query_doc[:, None]) | (key_at[None, :] == query_at[:, None])
    )
    return (scores, visible[None])


def grad_scores(
    query_block,
    grad_block,
    query_at,
    query_doc,
    top_block,
    delta_block,
    key_block,
    value_block,
    key_at,
    key_doc,
):
    scores, visible = score_block(query_block, key_block, query_at, query_doc, key_at, key_doc)
    probs_full = jnp.where(
        visible, jnp.exp(jnp.where(visible, scores, -1e30) - top_block[..., None]), 0.0
    )
    probs_grad = jnp.einsum(
        "qhd,khd->hqk", grad_block, value_block, preferred_element_type=jnp.float32
    )
    score_grad = (probs_full * (probs_grad - delta_block[..., None])).astype(jnp.bfloat16)
    return (probs_full.astype(jnp.bfloat16), score_grad)


def on_device(
    tokens,
    segments,
    padding,
    cotangent,
    norm1_gain,
    norm1_shift,
    norm2_gain,
    norm2_shift,
    qkv_weight,
    qkv_bias,
    out_weight,
    out_bias,
    up_weight,
    up_bias,
    down_weight,
    down_bias,
):
    inputs = tokens[0].astype(jnp.float32)
    seg_own = segments[0]
    pad_own = padding[0]
    span_rows = inputs.shape[0]
    local_width = qkv_weight.shape[2]
    heads_loc = local_width // HEAD_DIM
    score_scale = HEAD_DIM ** (-0.5)
    query_pos = lax.axis_index("ctx") * span_rows + jnp.arange(span_rows, dtype=jnp.int32)
    normed1 = layer_norm(inputs, norm1_gain, norm1_shift).astype(jnp.bfloat16)
    normed2 = layer_norm(inputs, norm2_gain, norm2_shift).astype(jnp.bfloat16)
    projected = (
        jnp.einsum("cd,dtf->ctf", normed1, qkv_weight, preferred_element_type=jnp.float32)
        + qkv_bias[None]
    )
    projected = projected.reshape(span_rows, 3, heads_loc, HEAD_DIM)
    cosine_tab, sine_tab = rotary_tables(query_pos)
    queries = rotate(projected[:, 0], cosine_tab, sine_tab).astype(jnp.bfloat16)
    keys_own = rotate(projected[:, 1], cosine_tab, sine_tab).astype(jnp.bfloat16)
    values_own = projected[:, 2].astype(jnp.bfloat16)
    code_own = jnp.where(pad_own == 1, seg_own, -1)
    keys_all, values_all, codes_all = (
        lax.all_gather(keys_own.reshape(span_rows, local_width), "ctx", axis=0, tiled=True),
        lax.all_gather(values_own.reshape(span_rows, local_width), "ctx", axis=0, tiled=True),
        lax.all_gather(code_own, "ctx", axis=0, tiled=True),
    )
    seq_len = keys_all.shape[0]
    block_count = seq_len // KBLOCK
    key_pos = jnp.arange(seq_len, dtype=jnp.int32)
    key_blocks = keys_all.reshape(block_count, KBLOCK, heads_loc, HEAD_DIM)
    value_blocks = values_all.reshape(block_count, KBLOCK, heads_loc, HEAD_DIM)
    code_blocks = codes_all.reshape(block_count, KBLOCK)
    pos_blocks = key_pos.reshape(block_count, KBLOCK)

    def total_step(state_pair, block_data):
        run_top, run_sum = state_pair
        key_block, code_block, pos_block = block_data
        scores, visible = score_block(queries, key_block, query_pos, seg_own, pos_block, code_block)
        masked = jnp.where(visible, scores, -1e30)
        new_top = jnp.maximum(run_top, jnp.max(masked, axis=-1))
        fresh_sum = jnp.sum(jnp.where(visible, jnp.exp(masked - new_top[..., None]), 0.0), axis=-1)
        return ((new_top, run_sum * jnp.exp(run_top - new_top) + fresh_sum), None)

    start_state = (
        jnp.full((heads_loc, span_rows), -1e30, jnp.float32),
        jnp.zeros((heads_loc, span_rows), jnp.float32),
    )
    final_pair, unused = lax.scan(total_step, start_state, (key_blocks, code_blocks, pos_blocks))
    log_total = final_pair[0] + jnp.log(final_pair[1])

    def attend_step(running, block_data):
        key_block, value_block, code_block, pos_block = block_data
        scores, visible = score_block(queries, key_block, query_pos, seg_own, pos_block, code_block)
        weights_low = jnp.where(
            visible, jnp.exp(jnp.where(visible, scores, -1e30) - log_total[..., None]), 0.0
        ).astype(jnp.bfloat16)
        return (
            running
            + jnp.einsum(
                "hqk,khd->qhd", weights_low, value_block, preferred_element_type=jnp.float32
            ),
            None,
        )

    zero_heads = jnp.zeros((span_rows, heads_loc, HEAD_DIM), jnp.float32)
    attended, unused = lax.scan(
        attend_step, zero_heads, (key_blocks, value_blocks, code_blocks, pos_blocks)
    )
    attended_b = attended.reshape(span_rows, local_width).astype(jnp.bfloat16)
    upward = jnp.dot(normed2, up_weight, preferred_element_type=jnp.float32) + up_bias
    activated = gelu_exact(upward).astype(jnp.bfloat16)
    partial_sum = jnp.dot(attended_b, out_weight, preferred_element_type=jnp.float32) + jnp.dot(
        activated, down_weight, preferred_element_type=jnp.float32
    )
    bias_sum = out_bias + down_bias
    summed = lax.psum(partial_sum.astype(jnp.bfloat16), "tensor").astype(jnp.float32)
    block_output = (inputs + summed + bias_sum).astype(jnp.bfloat16)
    grad_in = cotangent[0]
    grad_att_b = jnp.einsum(
        "cd,fd->cf", grad_in, out_weight, preferred_element_type=jnp.float32
    ).astype(jnp.bfloat16)
    grad_act = jnp.einsum("cd,fd->cf", grad_in, down_weight, preferred_element_type=jnp.float32)
    unused, gelu_pull = jax.vjp(gelu_exact, upward)
    grad_up_b = gelu_pull(grad_act)[0].astype(jnp.bfloat16)
    grad_heads = grad_att_b.reshape(span_rows, heads_loc, HEAD_DIM)
    delta_t = jnp.sum(grad_heads.astype(jnp.float32) * attended, axis=-1).T

    def both_step(query_grad, block_data):
        key_block, value_block, code_block, pos_block = block_data
        probs_low, score_grad = grad_scores(
            queries,
            grad_heads,
            query_pos,
            seg_own,
            log_total,
            delta_t,
            key_block,
            value_block,
            pos_block,
            code_block,
        )
        query_grad = query_grad + jnp.einsum(
            "hqk,khd->qhd", score_grad, key_block, preferred_element_type=jnp.float32
        )
        key_grad = jnp.einsum(
            "hqk,qhd->khd", score_grad, queries, preferred_element_type=jnp.float32
        )
        value_grad = jnp.einsum(
            "hqk,qhd->khd", probs_low, grad_heads, preferred_element_type=jnp.float32
        )
        return (query_grad, (key_grad, value_grad))

    query_grad, stacked = lax.scan(
        both_step, zero_heads, (key_blocks, value_blocks, code_blocks, pos_blocks)
    )
    key_grad, value_grad = (
        lax.psum_scatter(
            stacked[0].reshape(seq_len, local_width).astype(jnp.bfloat16),
            "ctx",
            scatter_dimension=0,
            tiled=True,
        ).astype(jnp.float32),
        lax.psum_scatter(
            stacked[1].reshape(seq_len, local_width).astype(jnp.bfloat16),
            "ctx",
            scatter_dimension=0,
            tiled=True,
        ).astype(jnp.float32),
    )
    key_grad = key_grad.reshape(span_rows, heads_loc, HEAD_DIM)
    value_grad = value_grad.reshape(span_rows, heads_loc, HEAD_DIM)
    query_pre = rotate(query_grad * score_scale, cosine_tab, -sine_tab)
    key_pre = rotate(key_grad * score_scale, cosine_tab, -sine_tab)
    grad_proj = (
        jnp.stack([query_pre, key_pre, value_grad], axis=1)
        .reshape(span_rows, 3, local_width)
        .astype(jnp.bfloat16)
    )
    grad_qkv_w = jnp.einsum("cd,ctf->dtf", normed1, grad_proj, preferred_element_type=jnp.float32)
    grad_qkv_b = jnp.sum(grad_proj.astype(jnp.float32), axis=0)
    grad_out_w = jnp.einsum("cf,cd->fd", attended_b, grad_in, preferred_element_type=jnp.float32)
    grad_bias_shared = jnp.sum(grad_in.astype(jnp.float32), axis=0)
    grad_up_w = jnp.einsum("cd,cf->df", normed2, grad_up_b, preferred_element_type=jnp.float32)
    grad_up_bias = jnp.sum(grad_up_b.astype(jnp.float32), axis=0)
    grad_down_w = jnp.einsum("cf,cd->fd", activated, grad_in, preferred_element_type=jnp.float32)
    norm_in1 = jnp.einsum("ctf,dtf->cd", grad_proj, qkv_weight, preferred_element_type=jnp.float32)
    norm_in2 = jnp.einsum("cf,df->cd", grad_up_b, up_weight, preferred_element_type=jnp.float32)
    full_one, full_two = (
        lax.psum(norm_in1.astype(jnp.bfloat16), "tensor").astype(jnp.float32),
        lax.psum(norm_in2.astype(jnp.bfloat16), "tensor").astype(jnp.float32),
    )
    input_one, gain_one, shift_one = norm_back(inputs, norm1_gain, norm1_shift, full_one)
    input_two, gain_two, shift_two = norm_back(inputs, norm2_gain, norm2_shift, full_two)
    input_grad = (grad_in.astype(jnp.float32) + input_one + input_two).astype(jnp.bfloat16)
    summed_grads = lax.psum(
        (
            gain_one,
            shift_one,
            gain_two,
            shift_two,
            grad_qkv_w,
            grad_qkv_b,
            grad_out_w,
            grad_bias_shared,
            grad_up_w,
            grad_up_bias,
            grad_down_w,
        ),
        ("dp", "ctx"),
    )
    return (
        block_output[None],
        input_grad[None],
        summed_grads[0],
        summed_grads[1],
        summed_grads[2],
        summed_grads[3],
        summed_grads[4],
        summed_grads[5],
        summed_grads[6],
        summed_grads[7],
        summed_grads[8],
        summed_grads[9],
        summed_grads[10],
        summed_grads[7],
    )


F32 = jnp.float32
BF16 = jnp.bfloat16
NEG = -1e30
MIB = 1 << 20
CHUNKS = 4


def params(mib=40):
    return pltpu.CompilerParams(vmem_limit_bytes=mib * MIB)


def cost(flops, moved):
    return pl.CostEstimate(flops=int(flops), bytes_accessed=int(moved), transcendentals=0)


def dot(a, b):
    return lax.dot_general(a, b, (((1,), (0,)), ((), ())), preferred_element_type=F32)


def dot_nt(a, b):
    return lax.dot_general(a, b, (((1,), (1,)), ((), ())), preferred_element_type=F32)


def dot_tn(a, b):
    return lax.dot_general(a, b, (((0,), (0,)), ((), ())), preferred_element_type=F32)


def whole(shape):
    return pl.BlockSpec(shape, lambda *_: (0,) * len(shape))


def struct(shape, dtype):
    return jax.ShapeDtypeStruct(shape, dtype)


def standard(values):
    centre = jnp.mean(values, axis=-1, keepdims=True)
    centred = values - centre
    spread = jnp.mean(centred * centred, axis=-1, keepdims=True)
    inverse = lax.rsqrt(spread + 1e-05)
    return centred * inverse, inverse


def ctx_flag():
    return lax.axis_index("ctx")


def inner_flag():
    z = lax.axis_index("dp")
    return ((z == 1) | (z == 2)).astype(jnp.int32)


def core_flag():
    return lax.axis_index("tensor") % 2


def halves(flag, values):
    rows = values.shape[0] // 2
    top, low = values[:rows], values[rows:]
    return jnp.where(flag == 0, top, low), jnp.where(flag == 0, low, top)


def resident():
    return pl.BlockSpec(memory_space=pltpu.VMEM)


def small(kernel, arrays, outs, name, mib=16, flops=0):
    return pl.pallas_call(
        kernel,
        in_specs=[resident()] * len(arrays),
        out_specs=[resident()] * len(outs),
        out_shape=list(outs),
        compiler_params=params(mib),
        cost_estimate=cost(flops, 1024),
        name=name,
    )(*arrays)


def fetched(kernel, arrays, outs, name, flops, later=0, scratch=(), mib=48):
    now = len(arrays) - later
    return pl.pallas_call(
        kernel,
        grid=(1,),
        in_specs=[whole(a.shape) for a in arrays[:now]] + [pl.BlockSpec(memory_space=pl.ANY)] * later,
        out_specs=[whole(o.shape) for o in outs],
        out_shape=list(outs),
        scratch_shapes=list(scratch),
        compiler_params=params(mib),
        cost_estimate=cost(flops, 1024),
        name=name,
    )(*arrays)


def add_kernel(a_ref, b_ref, o_ref):
    o_ref[...] = (a_ref[...].astype(F32) + b_ref[...].astype(F32)).astype(o_ref.dtype)


def add(a, b):
    return small(add_kernel, (a, b), [struct(a.shape, a.dtype)], "add")[0]


def choose_kernel(a_ref, b_ref, o_ref):
    o_ref[...] = jnp.where(inner_flag() == 1, a_ref[...], b_ref[...])


def choose(a, b):
    return small(choose_kernel, (a, b), [struct(a.shape, a.dtype)], "choose")[0]


def place_halves_kernel(mine_ref, other_ref, *refs):
    o_ref = refs[-1]
    rows = o_ref.shape[0]
    o_ref[...] = jnp.where(ctx_flag() == pl.program_id(0), mine_ref[:rows], other_ref[:rows]).astype(F32)


def turn_lanes(table):
    half, lanes = ROT // 2, 2 * HEAD_DIM
    row = lax.broadcasted_iota(jnp.int32, (2 * half, lanes), 0)
    lane = lax.broadcasted_iota(jnp.int32, (2 * half, lanes), 1) % HEAD_DIM
    turned = (lane < ROT) & (lane % half == row % half)
    pick_cos = jnp.where(turned & (row < half), 1.0, 0.0)
    pick_sin = jnp.where(turned & (row >= half), jnp.where(lane < half, -1.0, 1.0), 0.0)
    exact = functools.partial(
        lax.dot_general, dimension_numbers=(((0,), (0,)), ((), ())), precision=lax.Precision.HIGHEST,
        preferred_element_type=F32,
    )
    return exact(table, pick_cos) + jnp.where(lane[0:1] < ROT, 0.0, 1.0), exact(table, pick_sin)


def partner(values):
    lane = lax.broadcasted_iota(jnp.int32, values.shape, 1) % HEAD_DIM
    half = ROT // 2
    width = values.shape[1]
    return jnp.where(lane < half, pltpu.roll(values, width - half, 1), pltpu.roll(values, half, 1))


def turn(values, cosine, sine):
    return values * cosine + partner(values) * sine


def activation(up):
    phi = 0.5 * (1.0 + lax.erf(up * 0.7071067811865476))
    return (up * phi).astype(BF16), phi + up * (0.3989422804014327 * jnp.exp(up * up * -0.5))


def own_kernel(x_ref, dy_ref, up_ref, down_ref, pack_ref, n1_ref, n2_ref, act_ref, gu_ref, gub_ref):
    step = pl.program_id(0)

    @pl.when(step == 0)
    def _():
        xhat, _ = standard(x_ref[...].astype(F32))
        n1_ref[...] = (xhat * pack_ref[0:1] + pack_ref[1:2]).astype(BF16)
        n2_ref[...] = (xhat * pack_ref[2:3] + pack_ref[3:4]).astype(BF16)

    size = act_ref.shape[1]
    dy = dy_ref[...]
    act, slope = activation(dot(n2_ref[...], up_ref[...]) + pack_ref[4:5, pl.ds(pl.multiple_of(step * size, size), size)])
    grad = (dot_nt(dy, down_ref[...]) * slope).astype(BF16)
    act_ref[...] = act
    gu_ref[...] = grad
    gub_ref[...] = jnp.sum(grad.astype(F32), axis=0, keepdims=True)


def own_call(x, dy, up_w, down_w, pack):
    rows, width = x.shape
    hidden = up_w.shape[1]
    size = hidden // CHUNKS
    cols = pl.BlockSpec((rows, size), lambda i: (0, i))
    return pl.pallas_call(
        own_kernel,
        grid=(CHUNKS,),
        in_specs=[
            whole(x.shape), whole(x.shape),
            pl.BlockSpec((width, size), lambda i: (0, i)), pl.BlockSpec((size, width), lambda i: (i, 0)),
            whole(pack.shape),
        ],
        out_specs=[whole(x.shape)] * 2 + [cols, cols, pl.BlockSpec((1, size), lambda i: (0, i))],
        out_shape=[struct(x.shape, BF16)] * 2 + [struct((rows, hidden), BF16)] * 2 + [struct((1, hidden), F32)],
        compiler_params=params(48),
        cost_estimate=cost(8e9, 1024),
        name="own",
    )(x, dy, up_w, down_w, pack)


def half_at(flag, size):
    return pl.ds(pl.multiple_of(flag * size, size), size)


def project(n1, span, w_ref, b_ref, table_ref, q_ref, k_ref, v_ref):
    lanes = q_ref.shape[1]
    mine = half_at(ctx_flag(), lanes)
    cosine, sine = turn_lanes(table_ref[:, half_at(span, n1.shape[0])])
    q_ref[...] = turn(dot(n1, w_ref[0, :, mine]) + b_ref[0:1, mine], cosine, sine).astype(BF16)
    k_ref[...] = turn(dot(n1, w_ref[1, :, mine]) + b_ref[1:2, mine], cosine, sine).astype(BF16)
    v_ref[...] = (dot(n1, w_ref[2, :, mine]) + b_ref[2:3, mine]).astype(BF16)


def pieces(near_ref, pair_ref, step):
    core, size = core_flag(), near_ref.shape[0]
    step(half_at(core, size), near_ref[...])
    step(half_at(1 - core, size), pair_ref[...])


def other_kernel(near_ref, pair_ref, n1_o_ref, pack_ref, w_ref, b_ref, table_ref, up_ref,
                 n1_ref, n2_ref, q_o_ref, k_o_ref, v_o_ref, q_ref, k_ref, v_ref, act_ref, slope_ref):
    def norm(at, x):
        xhat, _ = standard(x.astype(F32))
        n1_ref[at] = (xhat * pack_ref[0:1] + pack_ref[1:2]).astype(BF16)
        n2_ref[at] = (xhat * pack_ref[2:3] + pack_ref[3:4]).astype(BF16)

    pieces(near_ref, pair_ref, norm)
    project(n1_o_ref[...], ctx_flag(), w_ref, b_ref, table_ref, q_o_ref, k_o_ref, v_o_ref)
    project(n1_ref[...], 1 - ctx_flag(), w_ref, b_ref, table_ref, q_ref, k_ref, v_ref)
    size = slope_ref.shape[1] // 2
    for j in range(2):
        mine = pl.ds(pl.multiple_of(ctx_flag() * 2 * size + j * size, size), size)
        at = slice(j * size, (j + 1) * size)
        act_ref[:, at], slope_ref[:, at] = activation(dot(n2_ref[...], up_ref[:, mine]) + pack_ref[4:5, mine])


def other_call(near, pair, n1, pack, w3, bias, table, up_w):
    rows, width = 2 * near.shape[0], near.shape[1]
    half = up_w.shape[1] // 2
    head = struct((rows, 2 * HEAD_DIM), BF16)
    outs = [struct((rows, width), BF16)] * 2 + [head] * 6 + [struct((rows, half), BF16), struct((rows, half), F32)]
    return fetched(other_kernel, (near, pair, n1, pack, w3, bias, table, up_w), outs, "other", 5e9)


EXTRA = 16


def unit_struct(rows, cols):
    return struct((rows + EXTRA, cols), BF16)


def fill(ref, *values):
    rows = ref.shape[0] - EXTRA
    at = 0
    for value in values:
        for first in range(0, value.shape[0], rows):
            ref[:rows, at : at + value.shape[1]] = value[first : first + rows]
            at += value.shape[1]
    ref[rows:] = jnp.zeros((EXTRA, ref.shape[1]), ref.dtype)


def unfold(value, lanes, index, count):
    rows = value.shape[0] - EXTRA
    folds = [value[:rows, (index * count + i) * lanes : (index * count + i + 1) * lanes] for i in range(count)]
    return jnp.concatenate(folds, axis=0)


def weights_kernel(near_ref, pair_ref, act_o_ref, dy_o_ref, act_ref, slope_ref, down_ref, ow_ref,
                   dy_ref, gu_ref, ga_ref, *grad_refs):
    hidden = slope_ref.shape[1]

    def put(at, dy):
        dy_ref[at] = dy

    pieces(near_ref, pair_ref, put)
    dy, dy_o = dy_ref[...], dy_o_ref[...]
    rows, lanes = dy.shape[0], ga_ref.shape[1]
    act_o, act = act_o_ref[:, half_at(ctx_flag(), hidden)], act_ref[...]
    for i, ref in enumerate(grad_refs):
        cols = slice(i * ref.shape[1], (i + 1) * ref.shape[1])
        fill(ref, (dot_tn(act_o, dy_o[:, cols]) + dot_tn(act, dy[:, cols])).astype(BF16))
    gu_ref[...] = (dot_nt(dy, down_ref[half_at(ctx_flag(), hidden)]) * slope_ref[...]).astype(BF16)
    out_w = ow_ref[half_at(ctx_flag(), lanes)]
    ga_ref[half_at(ctx_flag(), rows)] = dot_nt(dy_o, out_w).astype(BF16)
    ga_ref[half_at(1 - ctx_flag(), rows)] = dot_nt(dy, out_w).astype(BF16)


def weights_call(near, pair, act_o, dy_o, act, slope, down_w, out_w):
    rows, width = dy_o.shape
    hidden = slope.shape[1]
    outs = [struct((rows, width), BF16), struct((rows, hidden), BF16), struct((2 * rows, 2 * HEAD_DIM), BF16)]
    outs += [unit_struct(hidden, width // 2)] * 2
    arrays = (near, pair, act_o, dy_o, act, slope, down_w, out_w)
    return fetched(weights_kernel, arrays, outs, "weights", 4e9)


def in_order(own, other, axis=0):
    first = ctx_flag() == 0
    return jnp.concatenate([jnp.where(first, own, other), jnp.where(first, other, own)], axis=axis)


def attend_kernel(q_o_ref, k_o_ref, v_o_ref, q_x_ref, k_x_ref, v_x_ref, ga_ref, ids_o_ref, ids_x_ref, table_ref,
                  n1_o_hbm, n1_x_hbm, dy_o_hbm, dy_x_hbm, n2_o_hbm, n2_x_hbm, gu_o_hbm, gu_x_hbm,
                  keep_ref, send_ref, qk_grad_ref, vo_grad_ref, *refs):
    up_refs, refs = refs[:2], refs[2:]
    q_ref, k_ref, v_ref, dk_ref, dv_ref, att_ref, gp_ref, *held, sems = refs
    n1_o_ref, n1_x_ref, dy_o_ref, dy_x_ref, n2_o_ref, n2_x_ref, gu_o_ref, gu_x_ref = held
    rows, lanes = q_ref.shape
    span = rows // 2
    mine, theirs = half_at(ctx_flag(), span), half_at(1 - ctx_flag(), span)
    copies = [
        pltpu.make_async_copy(src, dst, sems.at[i])
        for i, (src, dst) in enumerate((
            (n1_o_hbm, n1_o_ref), (n1_x_hbm, n1_x_ref), (dy_o_hbm, dy_o_ref), (dy_x_hbm, dy_x_ref),
            (n2_o_hbm, n2_o_ref), (n2_x_hbm, n2_x_ref),
            (gu_o_hbm.at[:, half_at(ctx_flag(), gu_x_ref.shape[1])], gu_o_ref), (gu_x_hbm, gu_x_ref),
        ))
    ]
    for copy in copies:
        copy.start()
    cosine, sine = turn_lanes(table_ref[...])
    step = 256
    zero = jnp.zeros((), BF16)
    scale = HEAD_DIM ** (-0.5)
    q_ref[...] = in_order(q_o_ref[...], q_x_ref[...]) * jnp.asarray(scale, BF16)
    k_ref[...], v_ref[...] = in_order(k_o_ref[...], k_x_ref[...]), in_order(v_o_ref[...], v_x_ref[...])
    dk_ref[...] = jnp.zeros(dk_ref.shape, F32)
    dv_ref[...] = jnp.zeros(dv_ref.shape, F32)
    ids = in_order(ids_o_ref[...], ids_x_ref[...], axis=1)
    code = jnp.where(ids[1:2] == 1, ids[0:1], -1).astype(F32)
    doc = jnp.broadcast_to(ids[0:1].astype(F32), (8, rows)).T[:, 0:1]
    lane = lax.broadcasted_iota(jnp.int32, (1, lanes), 1)
    heads = [(lane // HEAD_DIM) == h for h in range(lanes // HEAD_DIM)]
    for i in range(rows // step):
        at, upto = slice(i * step, (i + 1) * step), (i + 1) * step
        k, v = k_ref[:upto], v_ref[:upto]
        row = lax.broadcasted_iota(jnp.int32, (step, upto), 0) + i * step
        col = lax.broadcasted_iota(jnp.int32, (step, upto), 1)
        seen = ((col <= row) & (code[:, :upto] == doc[at])) | (col == row)
        bias = jnp.where(seen, 0.0, NEG)
        q, ga = q_ref[at], ga_ref[at]
        sums = None
        for head in heads:
            qh, gh = jnp.where(head, q, zero), jnp.where(head, ga, zero)
            scores = dot_nt(qh, k) + bias
            e = jnp.exp(scores - jnp.max(scores, axis=1, keepdims=True))
            p = e * (1.0 / jnp.sum(e, axis=1, keepdims=True))
            low = p.astype(BF16)
            att = jnp.where(head, dot(low, v), 0.0)
            delta = jnp.sum(att * gh.astype(F32), axis=1, keepdims=True)
            g = (p * (dot_nt(gh, v) - delta)).astype(BF16)
            terms = att, jnp.where(head, dot(g, k), 0.0), dot_tn(g, qh), dot_tn(low, gh)
            sums = terms if sums is None else [a + b for a, b in zip(sums, terms)]
        att_ref[at] = sums[0].astype(BF16)
        gp_ref[0, at] = turn(sums[1] * scale, cosine[at], -sine[at]).astype(BF16)
        dk_ref[:upto] += sums[2]
        dv_ref[:upto] += sums[3]
    gp_ref[1] = turn(dk_ref[...], cosine, -sine).astype(BF16)
    gp_ref[2] = dv_ref[...].astype(BF16)
    keep_ref[0], send_ref[0] = att_ref[mine], att_ref[theirs]
    for t in range(3):
        keep_ref[t + 1], send_ref[t + 1] = gp_ref[t, mine], gp_ref[t, theirs]
    for copy in copies:
        copy.wait()
    q_grad, k_grad, v_grad = [
        (dot_tn(n1_o_ref[...], keep_ref[t]) + dot_tn(n1_x_ref[...], send_ref[t])).astype(BF16) for t in (1, 2, 3)
    ]
    o_grad = (dot_tn(dy_o_ref[...], keep_ref[0]) + dot_tn(dy_x_ref[...], send_ref[0])).astype(BF16)
    fill(qk_grad_ref, q_grad, k_grad)
    fill(vo_grad_ref, v_grad, o_grad)
    gu_o, gu_x = gu_o_ref[...], gu_x_ref[...]
    for i, ref in enumerate(up_refs):
        at = slice(i * (ref.shape[0] - EXTRA), (i + 1) * (ref.shape[0] - EXTRA))
        fill(ref, (dot_tn(n2_o_ref[:, at], gu_o) + dot_tn(n2_x_ref[:, at], gu_x)).astype(BF16))


def attend_call(own, other, ga, ids, ids_x, table, *later):
    arrays = (*own, *other, ga, ids, ids_x, table, *later)
    rows, lanes = ga.shape
    span, width = later[0].shape
    hidden = later[-1].shape[1]
    outs = [struct((4, span, lanes), BF16)] * 2 + [unit_struct(width // 2, 4 * lanes)] * 2 + [unit_struct(width // 2, hidden)] * 2
    scratch = [pltpu.VMEM((rows, lanes), BF16)] * 3 + [pltpu.VMEM((rows, lanes), F32)] * 2
    scratch += [pltpu.VMEM((rows, lanes), BF16), pltpu.VMEM((3, rows, lanes), BF16)]
    scratch += [pltpu.VMEM((span, width), BF16)] * 6 + [pltpu.VMEM((span, hidden), BF16)] * 2
    scratch.append(pltpu.SemaphoreType.DMA((len(later),)))
    return fetched(attend_kernel, arrays, outs, "attend", 1024, len(later), scratch)


def sums_kernel(mine_ref, recv_ref, act_ref, gu_ref, dy_ref, x_ref, pack_ref, w_ref, ow_ref, up_ref, down_ref,
                gub_ref, keep_ref, send_ref, vec_ref, gb_ref):
    lanes = mine_ref.shape[2]
    heads = [(mine_ref, half_at(ctx_flag(), lanes)), (recv_ref, half_at(1 - ctx_flag(), lanes))]
    out = dot(act_ref[...], down_ref[...])
    two = dot_nt(gu_ref[...], up_ref[...])
    one = None
    for ref, at in heads:
        out = out + dot(ref[0], ow_ref[at])
        for t in range(3):
            term = dot_nt(ref[t + 1], w_ref[t, :, at])
            one = term if one is None else one + term
            gb_ref[t : t + 1, at] = jnp.sum(ref[t + 1].astype(F32), axis=0, keepdims=True)
    xhat, _ = standard(x_ref[...].astype(F32))
    sums = [jnp.sum(v, axis=0, keepdims=True) for v in (one * xhat, one, two * xhat, two)]
    heads_bias = jnp.concatenate([gb_ref[t : t + 1] for t in range(3)], axis=1)
    heads_bias = jnp.concatenate([heads_bias, jnp.zeros((1, xhat.shape[1] - heads_bias.shape[1]), F32)], axis=1)
    sums += [jnp.sum(dy_ref[...].astype(F32), axis=0, keepdims=True), gub_ref[...], heads_bias, jnp.zeros_like(heads_bias)]
    vec = jnp.concatenate(sums, axis=0)
    cols = vec_ref.shape[1]
    vec_ref[...] = jnp.concatenate([vec[:, :cols], vec[:, cols:]], axis=0).astype(BF16)
    rows = x_ref.shape[0] // 2
    for at, value in ((0, out), (rows, one * pack_ref[0:1] + two * pack_ref[2:3])):
        keep_ref[at : at + rows], send_ref[at : at + rows] = halves(core_flag(), value.astype(BF16))


def sums_call(mine, recv, act, gu, dy, x, pack, w3, out_w, up_w, down_w, gub):
    rows, width = x.shape
    both = struct((rows, width), BF16)
    outs = [both, both, struct((EXTRA, width // 2), BF16), struct((3, w3.shape[2]), F32)]
    return small(sums_kernel, (mine, recv, act, gu, dy, x, pack, w3, out_w, up_w, down_w, gub), outs, "sums", 32)


def ride_kernel(grad_ref, vec_ref, o_ref):
    rows = grad_ref.shape[0] - EXTRA
    o_ref[:rows] = grad_ref[:rows]
    o_ref[rows:] = vec_ref[...]


def ride(grad, vec):
    return small(ride_kernel, (grad, vec), [struct(grad.shape, BF16)], "ride")[0]


def place_ride_kernel(mine_ref, other_ref, *refs):
    grad_ref, vec_ref = refs[-2:]
    count, rows, lanes = grad_ref.shape
    value = jnp.where(ctx_flag() == pl.program_id(0), mine_ref[...], other_ref[...]).astype(F32)
    folds = rows // (mine_ref.shape[0] - EXTRA)
    for t in range(count):
        grad_ref[t] = unfold(value, lanes, t, folds)
    at = slice(mine_ref.shape[0] - EXTRA, mine_ref.shape[0])
    vec_ref[...] = mine_ref[at].astype(F32) + other_ref[at].astype(F32)


def rows_kernel(a_ref, b_ref, v_ref, *refs):
    heads_ref = refs[-1]
    held = jnp.concatenate([v_ref[:8], v_ref[8:]], axis=1)
    total = jnp.concatenate([a_ref[:8] + b_ref[:8], a_ref[8:] + b_ref[8:]], axis=1)
    for r, ref in enumerate(refs[:-1]):
        ref[...] = total[r : r + 1] if r < 4 else held[5:6] if r == 5 else held[4:5]
    cols = heads_ref.shape[1]
    for t in range(heads_ref.shape[0]):
        heads_ref[t : t + 1] = held[6:7, t * cols : (t + 1) * cols]


def rows_call(local, a, b, v):
    row = struct((1, 2 * a.shape[1]), F32)
    return small(rows_kernel, (a, b, v), [row] * 7 + [struct((3, local), F32)], "rows")


def place_pair_kernel(mine_ref, other_ref, *refs):
    value = jnp.where(ctx_flag() == pl.program_id(0), mine_ref[...], other_ref[...]).astype(F32)
    heads_ref, out_ref = refs[-2:]
    lanes = heads_ref.shape[2]
    folds = heads_ref.shape[1] // (mine_ref.shape[0] - EXTRA)
    heads_ref[0] = unfold(value, lanes, 0, folds)
    out_ref[...] = unfold(value, lanes, 1, folds).T


def results_kernel(mine_ref, other_ref, x_ref, dy_ref, pack_ref, out_ref, grad_ref):
    rows = x_ref.shape[0] // 2
    bias = pack_ref[5:6] + pack_ref[6:7]
    first = core_flag() == 0
    for i in range(2):
        at = slice(i * rows, (i + 1) * rows)
        here, there = (mine_ref, other_ref) if i == 0 else (other_ref, mine_ref)
        out, grad = [
            jnp.where(first, here[part], there[part]).astype(F32) for part in (slice(0, rows), slice(rows, 2 * rows))
        ]
        x = x_ref[at].astype(F32)
        out_ref[at] = (x + out + bias).astype(BF16)
        xhat, inverse = standard(x)
        mean = jnp.mean(grad, axis=-1, keepdims=True)
        along = jnp.mean(grad * xhat, axis=-1, keepdims=True)
        grad_ref[at] = (dy_ref[at].astype(F32) + inverse * (grad - mean - xhat * along)).astype(BF16)


def results_call(mine, other, x, dy, pack):
    return small(results_kernel, (mine, other, x, dy, pack), [struct(x.shape, BF16)] * 2, "results", 24)


INWARD = [(0, 1), (3, 2)]
MIDDLE = [(1, 2), (2, 1)]
OUTWARD = [(1, 0), (2, 3)]
SWAP = [(0, 1), (1, 0)]
CORES = [(i, i ^ 1) for i in range(4)]
CHIPS = [(i, i ^ 2) for i in range(4)]


class Sequence:
    def __init__(self):
        self.last = None

    def tied(self, operands):
        if self.last is None:
            return operands
        return lax.optimization_barrier((operands, self.last))[0]

    def __call__(self, step, *operands):
        result = step(*self.tied(operands))
        self.last = jax.tree.leaves(result)[0]
        return result

    def send(self, value, axis, perm):
        return lax.ppermute(self.tied(value), axis, perm)

    def arrived(self, value):
        value = self.tied(value)
        self.last = value
        return value


def turn_table(positions):
    half = ROT // 2
    inverse = jnp.exp(jnp.arange(half, dtype=F32) * (-2.0 * jnp.log(10000.0) / ROT))
    angles = inverse[:, None] * positions.astype(F32)[None, :]
    return jnp.concatenate([jnp.cos(angles), jnp.sin(angles)], axis=0)


def line_then_ctx(run, x, finish):
    r = yield "dp", INWARD, run.tied(x)
    x = run(add, x, r)
    r = yield "dp", MIDDLE, x
    x = run(add, x, r)
    r = yield "dp", OUTWARD, x
    x = run(choose, x, r)
    r = yield "ctx", SWAP, x
    finish(x, r)


def over_tensor(run, mine, other, finish):
    r = yield "tensor", CORES, run.tied(other)
    mine = run(add, mine, r)
    r = yield "tensor", CHIPS, mine
    mine = run(add, mine, r)
    r = yield "tensor", CORES, mine
    finish(mine, r)


def vectors_over_tensor(run, local, vec, finish):
    r = yield "tensor", CORES, run.tied(vec)
    x = run(add, vec, r)
    r = yield "tensor", CHIPS, x
    finish(run(functools.partial(rows_call, local), x, r, vec))


def gather_span(run, x, finish):
    half = x.shape[0] // 2
    near = yield "ctx", SWAP, lax.dynamic_slice_in_dim(run.tied(x), lax.axis_index("tensor") % 2 * half, half, 0)
    near = run.arrived(near)
    pair = yield "tensor", CORES, near
    finish(near, pair)


class Unit:
    def __init__(self, run, steps):
        self.run, self.steps, self.message = run, steps, None

    def request(self):
        try:
            return self.steps.send(self.message)
        except StopIteration:
            return None

    def advance(self):
        request = self.request()
        if request:
            axis, perm, value = request
            self.message = lax.ppermute(value, axis, perm)

    def advance_with(self, other):
        (_, _, inward), (_, _, outward) = self.request(), other.request()
        self.message = other.message = lax.ppermute(self.run(choose, outward, inward), "dp", INWARD + OUTWARD)

    def wait(self):
        self.message = self.run.arrived(self.message)


class Held:
    pass


def two_spans(
    tokens, segments, padding, cotangent, norm1_gain, norm1_shift, norm2_gain, norm2_shift,
    qkv_weight, qkv_bias, out_weight, out_bias, up_weight, up_bias, down_weight, down_bias,
):
    x, dy = tokens[0], cotangent[0]
    rows, width = x.shape
    local = qkv_weight.shape[2]
    hidden = up_weight.shape[1]
    lanes = 2 * HEAD_DIM
    row = lambda v: v.reshape(1, -1)
    w3 = jnp.transpose(qkv_weight, (1, 0, 2))
    run = Sequence()
    s, u = Held(), Held()
    dests = {}
    shapes = {"down": (hidden, width), "up": (width, hidden), "qkv": (3, width, local), "out": (local, width),
              "vec": (EXTRA, width // 2)}

    def open_unit(name, steps, *operands):
        setattr(u, name, Unit(run, steps(run, *operands)))

    def placing(names, kernel, count, blocks, indices):
        def finish(a, b):
            held = [n for n in names if n in dests]

            def step(a, b, *old):
                return pl.pallas_call(
                    kernel,
                    grid=(count,),
                    in_specs=[resident()] * 2 + [pl.BlockSpec(memory_space=pl.ANY)] * len(old),
                    out_specs=[pl.BlockSpec(block, index) for block, index in zip(blocks, indices)],
                    out_shape=[struct(shapes[n], F32) for n in names],
                    input_output_aliases={2 + i: names.index(n) for i, n in enumerate(held)},
                    compiler_params=params(24),
                    cost_estimate=cost(0, 0),
                    name="place",
                )(a, b, *old)

            dests.update(zip(names, run(step, a, b, *[dests[n] for n in held])))

        return finish

    open_unit("tk", gather_span, x, lambda *p: s.__dict__.update(tokens=p))
    open_unit("dy", gather_span, dy, lambda *p: s.__dict__.update(dy=p))

    def ids_0():
        ids = jnp.concatenate([segments, padding], axis=0)
        s.ids = ids, run.send(ids, "ctx", SWAP)

    def ids_w():
        s.ids = s.ids[0], run.arrived(s.ids[1])

    def own():
        s.pack = jnp.stack([norm1_gain, norm1_shift, norm2_gain, norm2_shift, up_bias, out_bias, down_bias])
        s.n1, s.n2, s.act, s.gu, s.gub = run(own_call, x, dy, up_weight, down_weight, s.pack)

    def other():
        u.tk.advance()
        s.n1x, s.n2x, *heads, s.actx, s.slope = run(
            other_call, *s.tokens, s.n1, s.pack, w3, qkv_bias, s.table, up_weight)
        s.qkv, s.qkvx = heads[:3], heads[3:]

    def tables():
        s.table = run(turn_table, jnp.arange(2 * rows, dtype=jnp.int32))

    def weights():
        u.dy.advance()
        s.dyx, s.gux, s.ga, *grads = run(
            weights_call, *s.dy, s.act, dy, s.actx, s.slope, down_weight, out_weight)
        for j, grad in enumerate(grads):
            open_unit(f"D{j}", line_then_ctx, grad, placing(
                ["down"], place_halves_kernel, 2, [(hidden // 2, width // 2)], [lambda i, j=j: (i, j)]))

    def attend():
        s.mine, s.theirs, s.qk, vo_grad, *ups = run(
            lambda *a: attend_call(a[:3], a[3:6], *a[6:]),
            *s.qkv, *s.qkvx, s.ga, *s.ids, s.table,
            s.n1, s.n1x, dy, s.dyx, s.n2, s.n2x, s.gu, s.gux)
        open_unit("Q1", line_then_ctx, vo_grad, placing(
            ["qkv", "out"], place_pair_kernel, 2, [(1, width, lanes), (lanes, width)],
            [lambda i: (2, 0, i), lambda i: (i, 0)]))
        for j, grad in enumerate(ups):
            open_unit(f"U{j}", line_then_ctx, grad, placing(
                ["up"], place_halves_kernel, 2, [(width // 2, hidden // 2)], [lambda i, j=j: (j, i)]))

    def gpx_0():
        s.recv = run.send(s.theirs, "ctx", SWAP)

    def gpx_w():
        s.recv = run.arrived(s.recv)

    def sums():
        keep, send, s.vec, _ = run(
            sums_call, s.mine, s.recv, s.act, s.gu, dy, x, s.pack, w3, out_weight, up_weight, down_weight,
            s.gub)

        def finish(a, b):
            s.block_output, s.input_grad = run(lambda a, b: results_call(a, b, x, dy, s.pack), a, b)

        open_unit("both", over_tensor, keep, send, finish)

    def join():
        both = run(ride, s.qk, s.vec)
        put = placing(
            ["qkv", "vec"], place_ride_kernel, 2, [(2, width, lanes), s.vec.shape], [lambda i: (0, 0, i), lambda i: (0, 0)])

        def finish(a, b):
            put(a, b)
            open_unit("vec", vectors_over_tensor, local, dests["vec"], lambda rows: s.__dict__.update(rows=rows))

        open_unit("Q0", line_then_ctx, both, finish)

    u.tk.advance()
    own()
    u.dy.advance()
    tables()
    u.tk.advance()
    ids_0()
    other()
    ids_w()
    u.dy.advance()
    weights()
    u.D0.advance()
    attend()
    u.D1.advance()
    u.D0.wait()
    u.D0.advance()
    gpx_0()
    gpx_w()
    u.D1.wait()
    u.D0.wait()
    u.U0.advance_with(u.D0)
    u.D1.advance()
    sums()
    join()
    u.U0.wait()
    u.Q0.advance_with(u.D1)
    u.D0.advance()
    u.U0.advance()
    u.both.advance()
    u.Q0.wait()
    u.Q1.advance_with(u.U0)
    u.D1.advance()
    u.Q0.advance()
    u.both.advance()
    u.D0.advance()
    u.Q1.wait()
    u.U1.advance_with(u.Q0)
    u.U0.advance()
    u.Q1.advance()
    u.D1.advance()
    u.U1.advance()
    u.Q1.advance()
    u.Q0.advance()
    u.both.advance()
    u.U0.advance()
    u.U1.advance()
    u.Q1.advance()
    u.Q0.advance()
    u.vec.advance()
    u.both.advance()
    u.U1.advance()
    u.Q1.advance()
    u.vec.advance()
    u.vec.advance()
    u.U1.advance()
    *rows, heads_bias = s.rows
    gain1, shift1, gain2, shift2, dy_sum, up_sum, dy_same = [r.reshape(-1) for r in rows]
    return (
        s.block_output[None],
        s.input_grad[None],
        gain1, shift1, gain2, shift2,
        jnp.transpose(dests["qkv"], (1, 0, 2)),
        heads_bias,
        dests["out"],
        dy_sum,
        dests["up"],
        up_sum,
        dests["down"],
        dy_same,
    )


def fits(mesh):
    return dict(mesh.shape) == {"dp": 4, "ctx": 2, "tensor": 4}


def solution(mesh):
    return jax.shard_map(
        two_spans if fits(mesh) else on_device,
        mesh=mesh,
        in_specs=(
            P("dp", "ctx", None),
            P("dp", "ctx"),
            P("dp", "ctx"),
            P("dp", "ctx", None),
            P(),
            P(),
            P(),
            P(),
            P(None, None, "tensor"),
            P(None, "tensor"),
            P("tensor", None),
            P(),
            P(None, "tensor"),
            P("tensor"),
            P("tensor", None),
            P(),
        ),
        out_specs=(
            P("dp", "ctx", None),
            P("dp", "ctx", None),
            P(),
            P(),
            P(),
            P(),
            P(None, None, "tensor"),
            P(None, "tensor"),
            P("tensor", None),
            P(),
            P(None, "tensor"),
            P("tensor"),
            P("tensor", None),
            P(),
        ),
        check_vma=False,
    )
```

```python
import functools

import jax
import jax.numpy as jnp
from jax import lax
from jax.sharding import PartitionSpec as P
from jax.experimental import pallas as pl
from jax.experimental.pallas import tpu as pltpu

HEAD_DIM = 64
ROT = 16
KBLOCK = 512


def layer_norm(values, gain_vec, shift_vec):
    centre = jnp.mean(values, axis=-1, keepdims=True)
    centred = values - centre
    spread = jnp.mean(centred * centred, axis=-1, keepdims=True)
    return centred * lax.rsqrt(spread + 1e-05) * gain_vec + shift_vec


def norm_back(values, gain_vec, shift_vec, upstream):
    outcome, pullback = jax.vjp(layer_norm, values, gain_vec, shift_vec)
    return pullback(upstream)


def gelu_exact(values):
    return jax.nn.gelu(values, approximate=False)


def rotary_tables(positions):
    half_dims = ROT // 2
    freq_index = jnp.arange(half_dims, dtype=jnp.float32)
    inverse = jnp.exp(freq_index * (-2.0 * jnp.log(10000.0) / ROT))
    angles = positions.astype(jnp.float32)[:, None] * inverse[None, :]
    return (jnp.cos(angles)[:, None, :], jnp.sin(angles)[:, None, :])


def rotate(values, cosine_tab, sine_tab):
    half_dims = ROT // 2
    first_half = values[..., :half_dims]
    second_half = values[..., half_dims:ROT]
    return jnp.concatenate(
        [
            first_half * cosine_tab - second_half * sine_tab,
            second_half * cosine_tab + first_half * sine_tab,
            values[..., ROT:],
        ],
        axis=-1,
    )


def score_block(query_block, key_block, query_at, query_doc, key_at, key_doc):
    scores = jnp.einsum(
        "qhd,khd->hqk", query_block, key_block, preferred_element_type=jnp.float32
    ) * HEAD_DIM ** (-0.5)
    visible = (key_at[None, :] <= query_at[:, None]) & (
        (key_doc[None, :] == query_doc[:, None]) | (key_at[None, :] == query_at[:, None])
    )
    return (scores, visible[None])


def grad_scores(
    query_block,
    grad_block,
    query_at,
    query_doc,
    top_block,
    delta_block,
    key_block,
    value_block,
    key_at,
    key_doc,
):
    scores, visible = score_block(query_block, key_block, query_at, query_doc, key_at, key_doc)
    probs_full = jnp.where(
        visible, jnp.exp(jnp.where(visible, scores, -1e30) - top_block[..., None]), 0.0
    )
    probs_grad = jnp.einsum(
        "qhd,khd->hqk", grad_block, value_block, preferred_element_type=jnp.float32
    )
    score_grad = (probs_full * (probs_grad - delta_block[..., None])).astype(jnp.bfloat16)
    return (probs_full.astype(jnp.bfloat16), score_grad)


def on_device(
    tokens,
    segments,
    padding,
    cotangent,
    norm1_gain,
    norm1_shift,
    norm2_gain,
    norm2_shift,
    qkv_weight,
    qkv_bias,
    out_weight,
    out_bias,
    up_weight,
    up_bias,
    down_weight,
    down_bias,
):
    inputs = tokens[0].astype(jnp.float32)
    seg_own = segments[0]
    pad_own = padding[0]
    span_rows = inputs.shape[0]
    local_width = qkv_weight.shape[2]
    heads_loc = local_width // HEAD_DIM
    score_scale = HEAD_DIM ** (-0.5)
    query_pos = lax.axis_index("ctx") * span_rows + jnp.arange(span_rows, dtype=jnp.int32)
    normed1 = layer_norm(inputs, norm1_gain, norm1_shift).astype(jnp.bfloat16)
    normed2 = layer_norm(inputs, norm2_gain, norm2_shift).astype(jnp.bfloat16)
    projected = (
        jnp.einsum("cd,dtf->ctf", normed1, qkv_weight, preferred_element_type=jnp.float32)
        + qkv_bias[None]
    )
    projected = projected.reshape(span_rows, 3, heads_loc, HEAD_DIM)
    cosine_tab, sine_tab = rotary_tables(query_pos)
    queries = rotate(projected[:, 0], cosine_tab, sine_tab).astype(jnp.bfloat16)
    keys_own = rotate(projected[:, 1], cosine_tab, sine_tab).astype(jnp.bfloat16)
    values_own = projected[:, 2].astype(jnp.bfloat16)
    code_own = jnp.where(pad_own == 1, seg_own, -1)
    keys_all, values_all, codes_all = (
        lax.all_gather(keys_own.reshape(span_rows, local_width), "ctx", axis=0, tiled=True),
        lax.all_gather(values_own.reshape(span_rows, local_width), "ctx", axis=0, tiled=True),
        lax.all_gather(code_own, "ctx", axis=0, tiled=True),
    )
    seq_len = keys_all.shape[0]
    block_count = seq_len // KBLOCK
    key_pos = jnp.arange(seq_len, dtype=jnp.int32)
    key_blocks = keys_all.reshape(block_count, KBLOCK, heads_loc, HEAD_DIM)
    value_blocks = values_all.reshape(block_count, KBLOCK, heads_loc, HEAD_DIM)
    code_blocks = codes_all.reshape(block_count, KBLOCK)
    pos_blocks = key_pos.reshape(block_count, KBLOCK)

    def total_step(state_pair, block_data):
        run_top, run_sum = state_pair
        key_block, code_block, pos_block = block_data
        scores, visible = score_block(queries, key_block, query_pos, seg_own, pos_block, code_block)
        masked = jnp.where(visible, scores, -1e30)
        new_top = jnp.maximum(run_top, jnp.max(masked, axis=-1))
        fresh_sum = jnp.sum(jnp.where(visible, jnp.exp(masked - new_top[..., None]), 0.0), axis=-1)
        return ((new_top, run_sum * jnp.exp(run_top - new_top) + fresh_sum), None)

    start_state = (
        jnp.full((heads_loc, span_rows), -1e30, jnp.float32),
        jnp.zeros((heads_loc, span_rows), jnp.float32),
    )
    final_pair, unused = lax.scan(total_step, start_state, (key_blocks, code_blocks, pos_blocks))
    log_total = final_pair[0] + jnp.log(final_pair[1])

    def attend_step(running, block_data):
        key_block, value_block, code_block, pos_block = block_data
        scores, visible = score_block(queries, key_block, query_pos, seg_own, pos_block, code_block)
        weights_low = jnp.where(
            visible, jnp.exp(jnp.where(visible, scores, -1e30) - log_total[..., None]), 0.0
        ).astype(jnp.bfloat16)
        return (
            running
            + jnp.einsum(
                "hqk,khd->qhd", weights_low, value_block, preferred_element_type=jnp.float32
            ),
            None,
        )

    zero_heads = jnp.zeros((span_rows, heads_loc, HEAD_DIM), jnp.float32)
    attended, unused = lax.scan(
        attend_step, zero_heads, (key_blocks, value_blocks, code_blocks, pos_blocks)
    )
    attended_b = attended.reshape(span_rows, local_width).astype(jnp.bfloat16)
    upward = jnp.dot(normed2, up_weight, preferred_element_type=jnp.float32) + up_bias
    activated = gelu_exact(upward).astype(jnp.bfloat16)
    partial_sum = jnp.dot(attended_b, out_weight, preferred_element_type=jnp.float32) + jnp.dot(
        activated, down_weight, preferred_element_type=jnp.float32
    )
    bias_sum = out_bias + down_bias
    summed = lax.psum(partial_sum.astype(jnp.bfloat16), "tensor").astype(jnp.float32)
    block_output = (inputs + summed + bias_sum).astype(jnp.bfloat16)
    grad_in = cotangent[0]
    grad_att_b = jnp.einsum(
        "cd,fd->cf", grad_in, out_weight, preferred_element_type=jnp.float32
    ).astype(jnp.bfloat16)
    grad_act = jnp.einsum("cd,fd->cf", grad_in, down_weight, preferred_element_type=jnp.float32)
    unused, gelu_pull = jax.vjp(gelu_exact, upward)
    grad_up_b = gelu_pull(grad_act)[0].astype(jnp.bfloat16)
    grad_heads = grad_att_b.reshape(span_rows, heads_loc, HEAD_DIM)
    delta_t = jnp.sum(grad_heads.astype(jnp.float32) * attended, axis=-1).T

    def both_step(query_grad, block_data):
        key_block, value_block, code_block, pos_block = block_data
        probs_low, score_grad = grad_scores(
            queries,
            grad_heads,
            query_pos,
            seg_own,
            log_total,
            delta_t,
            key_block,
            value_block,
            pos_block,
            code_block,
        )
        query_grad = query_grad + jnp.einsum(
            "hqk,khd->qhd", score_grad, key_block, preferred_element_type=jnp.float32
        )
        key_grad = jnp.einsum(
            "hqk,qhd->khd", score_grad, queries, preferred_element_type=jnp.float32
        )
        value_grad = jnp.einsum(
            "hqk,qhd->khd", probs_low, grad_heads, preferred_element_type=jnp.float32
        )
        return (query_grad, (key_grad, value_grad))

    query_grad, stacked = lax.scan(
        both_step, zero_heads, (key_blocks, value_blocks, code_blocks, pos_blocks)
    )
    key_grad, value_grad = (
        lax.psum_scatter(
            stacked[0].reshape(seq_len, local_width).astype(jnp.bfloat16),
            "ctx",
            scatter_dimension=0,
            tiled=True,
        ).astype(jnp.float32),
        lax.psum_scatter(
            stacked[1].reshape(seq_len, local_width).astype(jnp.bfloat16),
            "ctx",
            scatter_dimension=0,
            tiled=True,
        ).astype(jnp.float32),
    )
    key_grad = key_grad.reshape(span_rows, heads_loc, HEAD_DIM)
    value_grad = value_grad.reshape(span_rows, heads_loc, HEAD_DIM)
    query_pre = rotate(query_grad * score_scale, cosine_tab, -sine_tab)
    key_pre = rotate(key_grad * score_scale, cosine_tab, -sine_tab)
    grad_proj = (
        jnp.stack([query_pre, key_pre, value_grad], axis=1)
        .reshape(span_rows, 3, local_width)
        .astype(jnp.bfloat16)
    )
    grad_qkv_w = jnp.einsum("cd,ctf->dtf", normed1, grad_proj, preferred_element_type=jnp.float32)
    grad_qkv_b = jnp.sum(grad_proj.astype(jnp.float32), axis=0)
    grad_out_w = jnp.einsum("cf,cd->fd", attended_b, grad_in, preferred_element_type=jnp.float32)
    grad_bias_shared = jnp.sum(grad_in.astype(jnp.float32), axis=0)
    grad_up_w = jnp.einsum("cd,cf->df", normed2, grad_up_b, preferred_element_type=jnp.float32)
    grad_up_bias = jnp.sum(grad_up_b.astype(jnp.float32), axis=0)
    grad_down_w = jnp.einsum("cf,cd->fd", activated, grad_in, preferred_element_type=jnp.float32)
    norm_in1 = jnp.einsum("ctf,dtf->cd", grad_proj, qkv_weight, preferred_element_type=jnp.float32)
    norm_in2 = jnp.einsum("cf,df->cd", grad_up_b, up_weight, preferred_element_type=jnp.float32)
    full_one, full_two = (
        lax.psum(norm_in1.astype(jnp.bfloat16), "tensor").astype(jnp.float32),
        lax.psum(norm_in2.astype(jnp.bfloat16), "tensor").astype(jnp.float32),
    )
    input_one, gain_one, shift_one = norm_back(inputs, norm1_gain, norm1_shift, full_one)
    input_two, gain_two, shift_two = norm_back(inputs, norm2_gain, norm2_shift, full_two)
    input_grad = (grad_in.astype(jnp.float32) + input_one + input_two).astype(jnp.bfloat16)
    summed_grads = lax.psum(
        (
            gain_one,
            shift_one,
            gain_two,
            shift_two,
            grad_qkv_w,
            grad_qkv_b,
            grad_out_w,
            grad_bias_shared,
            grad_up_w,
            grad_up_bias,
            grad_down_w,
        ),
        ("dp", "ctx"),
    )
    return (
        block_output[None],
        input_grad[None],
        summed_grads[0],
        summed_grads[1],
        summed_grads[2],
        summed_grads[3],
        summed_grads[4],
        summed_grads[5],
        summed_grads[6],
        summed_grads[7],
        summed_grads[8],
        summed_grads[9],
        summed_grads[10],
        summed_grads[7],
    )


F32 = jnp.float32
BF16 = jnp.bfloat16
NEG = -1e30
MIB = 1 << 20
CHUNKS = 4


def params(mib=40):
    return pltpu.CompilerParams(vmem_limit_bytes=mib * MIB)


def cost(flops, moved):
    return pl.CostEstimate(flops=1024, bytes_accessed=1024, transcendentals=0)


def dot(a, b):
    return lax.dot_general(a, b, (((1,), (0,)), ((), ())), preferred_element_type=F32)


def dot_nt(a, b):
    return lax.dot_general(a, b, (((1,), (1,)), ((), ())), preferred_element_type=F32)


def dot_tn(a, b):
    return lax.dot_general(a, b, (((0,), (0,)), ((), ())), preferred_element_type=F32)


def whole(shape):
    return pl.BlockSpec(shape, lambda *_: (0,) * len(shape))


def struct(shape, dtype):
    return jax.ShapeDtypeStruct(shape, dtype)


def standard(values):
    centre = jnp.mean(values, axis=-1, keepdims=True)
    centred = values - centre
    spread = jnp.mean(centred * centred, axis=-1, keepdims=True)
    inverse = lax.rsqrt(spread + 1e-05)
    return centred * inverse, inverse


def ctx_flag():
    return lax.axis_index("ctx")


def inner_flag():
    z = lax.axis_index("dp")
    return ((z == 1) | (z == 2)).astype(jnp.int32)


def core_flag():
    return lax.axis_index("tensor") % 2


def halves(flag, values):
    rows = values.shape[0] // 2
    top, low = values[:rows], values[rows:]
    return jnp.where(flag == 0, top, low), jnp.where(flag == 0, low, top)


def resident():
    return pl.BlockSpec(memory_space=pltpu.VMEM)


def small(kernel, arrays, outs, name, mib=16, flops=0):
    return pl.pallas_call(
        kernel,
        in_specs=[resident()] * len(arrays),
        out_specs=[resident()] * len(outs),
        out_shape=list(outs),
        compiler_params=params(mib),
        cost_estimate=cost(flops, 1024),
        name=name,
    )(*arrays)


def fetched(kernel, arrays, outs, name, flops, later=0, scratch=(), mib=48):
    now = len(arrays) - later
    return pl.pallas_call(
        kernel,
        grid=(1,),
        in_specs=[whole(a.shape) for a in arrays[:now]] + [pl.BlockSpec(memory_space=pl.ANY)] * later,
        out_specs=[whole(o.shape) for o in outs],
        out_shape=list(outs),
        scratch_shapes=list(scratch),
        compiler_params=params(mib),
        cost_estimate=cost(flops, 1024),
        name=name,
    )(*arrays)


def add_kernel(a_ref, b_ref, o_ref):
    o_ref[...] = (a_ref[...].astype(F32) + b_ref[...].astype(F32)).astype(o_ref.dtype)


def add(a, b):
    return small(add_kernel, (a, b), [struct(a.shape, a.dtype)], "add")[0]


def choose_kernel(a_ref, b_ref, o_ref):
    o_ref[...] = jnp.where(inner_flag() == 1, a_ref[...], b_ref[...])


def choose(a, b):
    return small(choose_kernel, (a, b), [struct(a.shape, a.dtype)], "choose")[0]


def place_halves_kernel(mine_ref, other_ref, *refs):
    o_ref = refs[-1]
    rows = o_ref.shape[0]
    o_ref[...] = jnp.where(ctx_flag() == pl.program_id(0), mine_ref[:rows], other_ref[:rows]).astype(F32)


def turn_lanes(table):
    half, lanes = ROT // 2, 2 * HEAD_DIM
    row = lax.broadcasted_iota(jnp.int32, (2 * half, lanes), 0)
    lane = lax.broadcasted_iota(jnp.int32, (2 * half, lanes), 1) % HEAD_DIM
    turned = (lane < ROT) & (lane % half == row % half)
    pick_cos = jnp.where(turned & (row < half), 1.0, 0.0)
    pick_sin = jnp.where(turned & (row >= half), jnp.where(lane < half, -1.0, 1.0), 0.0)
    exact = functools.partial(
        lax.dot_general, dimension_numbers=(((0,), (0,)), ((), ())), precision=lax.Precision.HIGHEST,
        preferred_element_type=F32,
    )
    return exact(table, pick_cos) + jnp.where(lane[0:1] < ROT, 0.0, 1.0), exact(table, pick_sin)


def partner(values):
    lane = lax.broadcasted_iota(jnp.int32, values.shape, 1) % HEAD_DIM
    half = ROT // 2
    width = values.shape[1]
    return jnp.where(lane < half, pltpu.roll(values, width - half, 1), pltpu.roll(values, half, 1))


def turn(values, cosine, sine):
    return values * cosine + partner(values) * sine


def activation(up):
    phi = 0.5 * (1.0 + lax.erf(up * 0.7071067811865476))
    return (up * phi).astype(BF16), phi + up * (0.3989422804014327 * jnp.exp(up * up * -0.5))


def early_kernel(x_ref, dy_ref, up_ref, down_ref, pack_ref, n1_ref, n2_ref, act_ref, gu_ref, gub_ref, gd_ref):
    @pl.when(pl.program_id(0) == 0)
    def _():
        xhat, _ = standard(x_ref[...].astype(F32))
        n1_ref[...] = (xhat * pack_ref[0:1] + pack_ref[1:2]).astype(BF16)
        n2_ref[...] = (xhat * pack_ref[2:3] + pack_ref[3:4]).astype(BF16)

    branch(n2_ref, dy_ref, up_ref, down_ref, pack_ref, 0, act_ref, gu_ref, gub_ref, gd_ref)


def own_kernel(n2_ref, dy_ref, up_ref, down_ref, pack_ref, act_in, gu_in, gub_in, act_ref, gu_ref, gub_ref, gd_ref):
    branch(n2_ref, dy_ref, up_ref, down_ref, pack_ref, CHUNKS // 2, act_ref, gu_ref, gub_ref, gd_ref)


def branch(n2_ref, dy_ref, up_ref, down_ref, pack_ref, first, act_ref, gu_ref, gub_ref, gd_ref):
    step = pl.program_id(0)
    size, cols = act_ref.shape[1], gd_ref.shape[1]
    dy = dy_ref[...]
    bias = pack_ref[4:5, pl.ds(pl.multiple_of((first + step) * size, size), size)]
    act, slope = activation(dot(n2_ref[...], up_ref[...]) + bias)
    grad = (dot_nt(dy, down_ref[...]) * slope).astype(BF16)
    act_ref[...] = act
    gu_ref[...] = grad
    gub_ref[...] = jnp.sum(grad.astype(F32), axis=0, keepdims=True)
    gd_ref[pl.ds(pl.multiple_of(step * size, size), size)] = dot_tn(act, dy[:, :cols]).astype(BF16)

    @pl.when(step == CHUNKS // 2 - 1)
    def _():
        gd_ref[gd_ref.shape[0] - EXTRA :] = jnp.zeros((EXTRA, cols), BF16)


def branch_call(kernel, first, before, up_w, down_w, pack, outs, held, name):
    rows, width = before[0].shape
    hidden = up_w.shape[1]
    size = hidden // CHUNKS
    cols = pl.BlockSpec((rows, size), lambda i: (0, first + i))
    grads = unit_struct(hidden // 2, width // 2)
    count = len(before) + 3
    return pl.pallas_call(
        kernel,
        grid=(CHUNKS // 2,),
        in_specs=[whole(a.shape) for a in before] + [
            pl.BlockSpec((width, size), lambda i: (0, first + i)),
            pl.BlockSpec((size, width), lambda i: (first + i, 0)),
            whole(pack.shape),
        ] + [pl.BlockSpec(memory_space=pl.ANY)] * len(held),
        out_specs=[whole(o.shape) for o in outs] + [cols, cols, pl.BlockSpec((1, size), lambda i: (0, first + i))]
        + [whole(grads.shape)],
        out_shape=outs + [struct((rows, hidden), BF16)] * 2 + [struct((1, hidden), F32), grads],
        input_output_aliases={count + i: len(outs) + i for i in range(len(held))},
        compiler_params=params(48),
        cost_estimate=cost(5e9, 1024),
        name=name,
    )(*before, up_w, down_w, pack, *held)


def early_call(x, dy, up_w, down_w, pack):
    return branch_call(early_kernel, 0, (x, dy), up_w, down_w, pack, [struct(x.shape, BF16)] * 2, (), "early")


def own_call(n2, dy, up_w, down_w, pack, *held):
    return branch_call(own_kernel, CHUNKS // 2, (n2, dy), up_w, down_w, pack, [], held, "own")


def half_at(flag, size):
    return pl.ds(pl.multiple_of(flag * size, size), size)


def project(n1, span, w_ref, b_ref, table_ref, q_ref, k_ref, v_ref):
    lanes = q_ref.shape[1]
    mine = half_at(ctx_flag(), lanes)
    cosine, sine = turn_lanes(table_ref[:, half_at(span, n1.shape[0])])
    q_ref[...] = turn(dot(n1, w_ref[0, :, mine]) + b_ref[0:1, mine], cosine, sine).astype(BF16)
    k_ref[...] = turn(dot(n1, w_ref[1, :, mine]) + b_ref[1:2, mine], cosine, sine).astype(BF16)
    v_ref[...] = (dot(n1, w_ref[2, :, mine]) + b_ref[2:3, mine]).astype(BF16)


def pieces(near_ref, pair_ref, step):
    core, size = core_flag(), near_ref.shape[0]
    step(half_at(core, size), near_ref[...])
    step(half_at(1 - core, size), pair_ref[...])


def other_kernel(near_ref, pair_ref, n1_o_ref, pack_ref, w_ref, b_ref, table_ref, up_ref,
                 n1_ref, n2_ref, q_o_ref, k_o_ref, v_o_ref, q_ref, k_ref, v_ref, act_ref, slope_ref):
    def norm(at, x):
        xhat, _ = standard(x.astype(F32))
        n1_ref[at] = (xhat * pack_ref[0:1] + pack_ref[1:2]).astype(BF16)
        n2_ref[at] = (xhat * pack_ref[2:3] + pack_ref[3:4]).astype(BF16)

    pieces(near_ref, pair_ref, norm)
    project(n1_o_ref[...], ctx_flag(), w_ref, b_ref, table_ref, q_o_ref, k_o_ref, v_o_ref)
    project(n1_ref[...], 1 - ctx_flag(), w_ref, b_ref, table_ref, q_ref, k_ref, v_ref)
    size = slope_ref.shape[1] // 2
    for j in range(2):
        mine = pl.ds(pl.multiple_of(ctx_flag() * 2 * size + j * size, size), size)
        at = slice(j * size, (j + 1) * size)
        act_ref[:, at], slope_ref[:, at] = activation(dot(n2_ref[...], up_ref[:, mine]) + pack_ref[4:5, mine])


def other_call(near, pair, n1, pack, w3, bias, table, up_w):
    rows, width = 2 * near.shape[0], near.shape[1]
    half = up_w.shape[1] // 2
    head = struct((rows, 2 * HEAD_DIM), BF16)
    outs = [struct((rows, width), BF16)] * 2 + [head] * 6 + [struct((rows, half), BF16), struct((rows, half), F32)]
    return fetched(other_kernel, (near, pair, n1, pack, w3, bias, table, up_w), outs, "other", 5e9)


EXTRA = 16


def unit_struct(rows, cols):
    return struct((rows + EXTRA, cols), BF16)


def fill(ref, *values):
    rows = ref.shape[0] - EXTRA
    at = 0
    for value in values:
        for first in range(0, value.shape[0], rows):
            ref[:rows, at : at + value.shape[1]] = value[first : first + rows]
            at += value.shape[1]
    ref[rows:] = jnp.zeros((EXTRA, ref.shape[1]), ref.dtype)


def unfold(value, lanes, index, count):
    rows = value.shape[0] - EXTRA
    folds = [value[:rows, (index * count + i) * lanes : (index * count + i + 1) * lanes] for i in range(count)]
    return jnp.concatenate(folds, axis=0)


def weights_kernel(near_ref, pair_ref, act_o_ref, dy_o_ref, act_ref, slope_ref, down_ref, ow_ref,
                   dy_ref, gu_ref, ga_ref, gd_ref):
    hidden = slope_ref.shape[1]

    def put(at, dy):
        dy_ref[at] = dy

    pieces(near_ref, pair_ref, put)
    dy, dy_o = dy_ref[...], dy_o_ref[...]
    rows, lanes = dy.shape[0], ga_ref.shape[1]
    act_o, cols = act_o_ref[:, half_at(ctx_flag(), hidden)], gd_ref.shape[1]
    fill(gd_ref, (dot_tn(act_o, dy_o[:, cols:]) + dot_tn(act_ref[...], dy[:, cols:])).astype(BF16))
    gu_ref[...] = (dot_nt(dy, down_ref[half_at(ctx_flag(), hidden)]) * slope_ref[...]).astype(BF16)
    out_w = ow_ref[half_at(ctx_flag(), lanes)]
    ga_ref[half_at(ctx_flag(), rows)] = dot_nt(dy_o, out_w).astype(BF16)
    ga_ref[half_at(1 - ctx_flag(), rows)] = dot_nt(dy, out_w).astype(BF16)


def weights_call(near, pair, act_o, dy_o, act, slope, down_w, out_w):
    rows, width = dy_o.shape
    hidden = slope.shape[1]
    outs = [struct((rows, width), BF16), struct((rows, hidden), BF16), struct((2 * rows, 2 * HEAD_DIM), BF16)]
    outs.append(unit_struct(hidden, width // 2))
    arrays = (near, pair, act_o, dy_o, act, slope, down_w, out_w)
    return fetched(weights_kernel, arrays, outs, "weights", 4e9)


def in_order(own, other, axis=0):
    first = ctx_flag() == 0
    return jnp.concatenate([jnp.where(first, own, other), jnp.where(first, other, own)], axis=axis)


def attend_head(index, q_o_ref, k_o_ref, v_o_ref, q_x_ref, k_x_ref, v_x_ref, ga_ref, ids_o_ref, ids_x_ref, table_ref,
                q_ref, k_ref, v_ref, dk_ref, dv_ref, att_ref, gp_ref):
    rows, lanes = q_ref.shape
    cosine, sine = turn_lanes(table_ref[...])
    step = 256
    zero = jnp.zeros((), BF16)
    scale = HEAD_DIM ** (-0.5)
    q_ref[...] = in_order(q_o_ref[...], q_x_ref[...]) * jnp.asarray(scale, BF16)
    k_ref[...], v_ref[...] = in_order(k_o_ref[...], k_x_ref[...]), in_order(v_o_ref[...], v_x_ref[...])
    dk_ref[...] = jnp.zeros(dk_ref.shape, F32)
    dv_ref[...] = jnp.zeros(dv_ref.shape, F32)
    ids = in_order(ids_o_ref[...], ids_x_ref[...], axis=1)
    code = jnp.where(ids[1:2] == 1, ids[0:1], -1).astype(F32)
    doc = jnp.broadcast_to(ids[0:1].astype(F32), (8, rows)).T[:, 0:1]
    lane = lax.broadcasted_iota(jnp.int32, (1, lanes), 1)
    head = (lane // HEAD_DIM) == index
    for i in range(rows // step):
        at, upto = slice(i * step, (i + 1) * step), (i + 1) * step
        k, v = k_ref[:upto], v_ref[:upto]
        row = lax.broadcasted_iota(jnp.int32, (step, upto), 0) + i * step
        col = lax.broadcasted_iota(jnp.int32, (step, upto), 1)
        seen = ((col <= row) & (code[:, :upto] == doc[at])) | (col == row)
        bias = jnp.where(seen, 0.0, NEG)
        q, ga = q_ref[at], ga_ref[at]
        qh, gh = jnp.where(head, q, zero), jnp.where(head, ga, zero)
        scores = dot_nt(qh, k) + bias
        e = jnp.exp(scores - jnp.max(scores, axis=1, keepdims=True))
        p = e * (1.0 / jnp.sum(e, axis=1, keepdims=True))
        low = p.astype(BF16)
        att = jnp.where(head, dot(low, v), 0.0)
        delta = jnp.sum(att * gh.astype(F32), axis=1, keepdims=True)
        g = (p * (dot_nt(gh, v) - delta)).astype(BF16)
        query_grad = jnp.where(head, dot(g, k), 0.0)
        att_ref[at] = att.astype(BF16)
        gp_ref[0, at] = turn(query_grad * scale, cosine[at], -sine[at]).astype(BF16)
        dk_ref[:upto] += dot_tn(g, qh)
        dv_ref[:upto] += dot_tn(low, gh)
    gp_ref[1] = turn(dk_ref[...], cosine, -sine).astype(BF16)
    gp_ref[2] = dv_ref[...].astype(BF16)


def head_scratch(rows, lanes):
    return [pltpu.VMEM((rows, lanes), BF16)] * 3 + [pltpu.VMEM((rows, lanes), F32)] * 2


def first_head_kernel(*refs):
    attend_head(0, *refs[:10], *refs[12:], *refs[10:12])


def first_head_call(own, other, ga, ids, ids_x, table):
    arrays = (*own, *other, ga, ids, ids_x, table)
    outs = [struct(ga.shape, BF16), struct((3,) + ga.shape, BF16)]
    return fetched(first_head_kernel, arrays, outs, "first_head", 1024, 0, head_scratch(*ga.shape))


def attend_kernel(*refs):
    heads, (att_in, gp_in), later, outs = refs[:10], refs[10:12], refs[12:20], refs[20:26]
    att_ref, gp_ref, *held, sems = refs[26 + 5 :]
    keep_ref, send_ref, qk_grad_ref, vo_grad_ref, *up_refs = outs
    n1_o_ref, n1_x_ref, dy_o_ref, dy_x_ref, n2_o_ref, n2_x_ref, gu_o_ref, gu_x_ref = held
    span, hidden = n1_o_ref.shape[0], gu_x_ref.shape[1]
    mine, theirs = half_at(ctx_flag(), span), half_at(1 - ctx_flag(), span)
    sources = list(later)
    sources[6] = later[6].at[:, half_at(ctx_flag(), hidden)]
    copies = [pltpu.make_async_copy(src, dst, sems.at[i]) for i, (src, dst) in enumerate(zip(sources, held))]
    for copy in copies:
        copy.start()
    attend_head(1, *heads, *refs[26 : 26 + 5], att_ref, gp_ref)
    for ref, at in ((keep_ref, mine), (send_ref, theirs)):
        ref[0] = att_ref[at] + att_in[at]
        for t in range(3):
            ref[t + 1] = gp_ref[t, at] + gp_in[t, at]
    for copy in copies:
        copy.wait()
    q_grad, k_grad, v_grad = [
        (dot_tn(n1_o_ref[...], keep_ref[t]) + dot_tn(n1_x_ref[...], send_ref[t])).astype(BF16) for t in (1, 2, 3)
    ]
    o_grad = (dot_tn(dy_o_ref[...], keep_ref[0]) + dot_tn(dy_x_ref[...], send_ref[0])).astype(BF16)
    fill(qk_grad_ref, q_grad, k_grad)
    fill(vo_grad_ref, v_grad, o_grad)
    gu_o, gu_x = gu_o_ref[...], gu_x_ref[...]
    for i, ref in enumerate(up_refs):
        at = slice(i * (ref.shape[0] - EXTRA), (i + 1) * (ref.shape[0] - EXTRA))
        fill(ref, (dot_tn(n2_o_ref[:, at], gu_o) + dot_tn(n2_x_ref[:, at], gu_x)).astype(BF16))


def attend_call(own, other, ga, ids, ids_x, table, first, *later):
    arrays = (*own, *other, ga, ids, ids_x, table, *first, *later)
    rows, lanes = ga.shape
    span, width = later[0].shape
    hidden = later[-1].shape[1]
    outs = [struct((4, span, lanes), BF16)] * 2 + [unit_struct(width // 2, 4 * lanes)] * 2 + [unit_struct(width // 2, hidden)] * 2
    scratch = head_scratch(rows, lanes) + [pltpu.VMEM((rows, lanes), BF16), pltpu.VMEM((3, rows, lanes), BF16)]
    scratch += [pltpu.VMEM((span, width), BF16)] * 6 + [pltpu.VMEM((span, hidden), BF16)] * 2
    scratch.append(pltpu.SemaphoreType.DMA((len(later),)))
    return fetched(attend_kernel, arrays, outs, "attend", 1024, len(later), scratch)


def branch_sums_kernel(act_ref, gu_ref, dy_ref, x_ref, up_ref, down_ref, out_ref, grad_ref, sums_ref):
    two = dot_nt(gu_ref[...], up_ref[...])
    xhat, _ = standard(x_ref[...].astype(F32))
    grad_ref[...] = two
    out_ref[...] = dot(act_ref[...], down_ref[...])
    rows = [jnp.sum(v, axis=0, keepdims=True) for v in (two * xhat, two, dy_ref[...].astype(F32))]
    sums_ref[...] = jnp.concatenate(rows + [jnp.zeros((5, two.shape[1]), F32)], axis=0)


def branch_sums_call(act, gu, dy, x, up_w, down_w):
    outs = [struct(x.shape, F32)] * 2 + [struct((8, x.shape[1]), F32)]
    return small(branch_sums_kernel, (act, gu, dy, x, up_w, down_w), outs, "branch_sums", 24)


def sums_kernel(mine_ref, recv_ref, out_ref, grad_ref, sums_ref, x_ref, pack_ref, w_ref, ow_ref, gub_ref,
                keep_ref, send_ref, vec_ref):
    lanes = mine_ref.shape[2]
    heads = [(mine_ref, half_at(ctx_flag(), lanes)), (recv_ref, half_at(1 - ctx_flag(), lanes))]
    out, one = out_ref[...], None
    biases = []
    for ref, at in heads:
        out = out + dot(ref[0], ow_ref[at])
        for t in range(3):
            term = dot_nt(ref[t + 1], w_ref[t, :, at])
            one = term if one is None else one + term
        biases.append([jnp.sum(ref[t + 1].astype(F32), axis=0, keepdims=True) for t in range(3)])
    first = ctx_flag() == 0
    pairs = [(jnp.where(first, m, r), jnp.where(first, r, m)) for m, r in zip(*biases)]
    heads_bias = jnp.concatenate([half for pair in pairs for half in pair], axis=1)
    zeros = jnp.zeros((1, out.shape[1] - heads_bias.shape[1]), F32)
    xhat, _ = standard(x_ref[...].astype(F32))
    sums = sums_ref[...]
    rows = [jnp.sum(one * xhat, axis=0, keepdims=True), jnp.sum(one, axis=0, keepdims=True), sums[0:3], gub_ref[...]]
    rows += [jnp.concatenate([heads_bias, zeros], axis=1), jnp.zeros_like(sums[0:1])]
    vec = jnp.concatenate(rows, axis=0)
    cols = vec_ref.shape[1]
    vec_ref[...] = jnp.concatenate([vec[:, :cols], vec[:, cols:]], axis=0).astype(BF16)
    rows = x_ref.shape[0] // 2
    for at, value in ((0, out), (rows, one * pack_ref[0:1] + grad_ref[...] * pack_ref[2:3])):
        keep_ref[at : at + rows], send_ref[at : at + rows] = halves(core_flag(), value.astype(BF16))


def sums_call(mine, recv, branch, x, pack, w3, out_w, gub):
    rows, width = x.shape
    both = struct((rows, width), BF16)
    outs = [both, both, struct((EXTRA, width // 2), BF16)]
    return small(sums_kernel, (mine, recv, *branch, x, pack, w3, out_w, gub), outs, "sums", 32)


def ride_kernel(grad_ref, vec_ref, o_ref):
    rows = grad_ref.shape[0] - EXTRA
    o_ref[:rows] = grad_ref[:rows]
    o_ref[rows:] = vec_ref[...]


def ride(grad, vec):
    return small(ride_kernel, (grad, vec), [struct(grad.shape, BF16)], "ride")[0]


def place_ride_kernel(mine_ref, other_ref, *refs):
    grad_ref, vec_ref = refs[-2:]
    count, rows, lanes = grad_ref.shape
    value = jnp.where(ctx_flag() == pl.program_id(0), mine_ref[...], other_ref[...]).astype(F32)
    folds = rows // (mine_ref.shape[0] - EXTRA)
    for t in range(count):
        grad_ref[t] = unfold(value, lanes, t, folds)
    at = slice(mine_ref.shape[0] - EXTRA, mine_ref.shape[0])
    vec_ref[...] = mine_ref[at].astype(F32) + other_ref[at].astype(F32)


def rows_kernel(a_ref, b_ref, v_ref, *refs):
    heads_ref = refs[-1]
    held = jnp.concatenate([v_ref[:8], v_ref[8:]], axis=1)
    total = jnp.concatenate([a_ref[:8] + b_ref[:8], a_ref[8:] + b_ref[8:]], axis=1)
    for r, ref in enumerate(refs[:-1]):
        ref[...] = total[r : r + 1] if r < 4 else held[5:6] if r == 5 else held[4:5]
    cols = heads_ref.shape[1]
    for t in range(heads_ref.shape[0]):
        heads_ref[t : t + 1] = held[6:7, t * cols : (t + 1) * cols]


def rows_call(local, a, b, v):
    row = struct((1, 2 * a.shape[1]), F32)
    return small(rows_kernel, (a, b, v), [row] * 7 + [struct((3, local), F32)], "rows")


def place_sum_kernel(mine_ref, other_ref, *refs):
    rows = refs[-1].shape[0]
    refs[-1][...] = mine_ref[:rows].astype(F32) + other_ref[:rows].astype(F32)


def place_pair_kernel(mine_ref, other_ref, *refs):
    value = jnp.where(ctx_flag() == pl.program_id(0), mine_ref[...], other_ref[...]).astype(F32)
    heads_ref, out_ref = refs[-2:]
    lanes = heads_ref.shape[2]
    folds = heads_ref.shape[1] // (mine_ref.shape[0] - EXTRA)
    heads_ref[0] = unfold(value, lanes, 0, folds)
    out_ref[...] = unfold(value, lanes, 1, folds).T


def results_kernel(mine_ref, other_ref, x_ref, dy_ref, pack_ref, out_ref, grad_ref):
    rows = x_ref.shape[0] // 2
    bias = pack_ref[5:6] + pack_ref[6:7]
    first = core_flag() == 0
    for i in range(2):
        at = slice(i * rows, (i + 1) * rows)
        here, there = (mine_ref, other_ref) if i == 0 else (other_ref, mine_ref)
        out, grad = [
            jnp.where(first, here[part], there[part]).astype(F32) for part in (slice(0, rows), slice(rows, 2 * rows))
        ]
        x = x_ref[at].astype(F32)
        out_ref[at] = (x + out + bias).astype(BF16)
        xhat, inverse = standard(x)
        mean = jnp.mean(grad, axis=-1, keepdims=True)
        along = jnp.mean(grad * xhat, axis=-1, keepdims=True)
        grad_ref[at] = (dy_ref[at].astype(F32) + inverse * (grad - mean - xhat * along)).astype(BF16)


def results_call(mine, other, x, dy, pack):
    return small(results_kernel, (mine, other, x, dy, pack), [struct(x.shape, BF16)] * 2, "results", 24)


INWARD = [(0, 1), (3, 2)]
MIDDLE = [(1, 2), (2, 1)]
OUTWARD = [(1, 0), (2, 3)]
SWAP = [(0, 1), (1, 0)]
CORES = [(i, i ^ 1) for i in range(4)]
CHIPS = [(i, i ^ 2) for i in range(4)]


class Sequence:
    def __init__(self):
        self.last = None

    def tied(self, operands):
        if self.last is None:
            return operands
        return lax.optimization_barrier((operands, self.last))[0]

    def __call__(self, step, *operands):
        result = step(*self.tied(operands))
        self.last = jax.tree.leaves(result)[0]
        return result

    def send(self, value, axis, perm):
        return lax.ppermute(self.tied(value), axis, perm)

    def arrived(self, value):
        value = self.tied(value)
        self.last = value
        return value


def turn_table(positions):
    half = ROT // 2
    inverse = jnp.exp(jnp.arange(half, dtype=F32) * (-2.0 * jnp.log(10000.0) / ROT))
    angles = inverse[:, None] * positions.astype(F32)[None, :]
    return jnp.concatenate([jnp.cos(angles), jnp.sin(angles)], axis=0)


def line_then_ctx(run, x, finish):
    r = yield "dp", INWARD, run.tied(x)
    x = run(add, x, r)
    r = yield "dp", MIDDLE, x
    x = run(add, x, r)
    r = yield "dp", OUTWARD, x
    x = run(choose, x, r)
    r = yield "ctx", SWAP, x
    finish(x, r)


def over_tensor(run, mine, other, finish):
    r = yield "tensor", CORES, run.tied(other)
    mine = run(add, mine, r)
    r = yield "tensor", CHIPS, mine
    mine = run(add, mine, r)
    r = yield "tensor", CORES, mine
    finish(mine, r)


def vectors_over_tensor(run, local, vec, finish):
    r = yield "tensor", CORES, run.tied(vec)
    x = run(add, vec, r)
    r = yield "tensor", CHIPS, x
    finish(run(functools.partial(rows_call, local), x, r, vec))


def gather_span(run, x, finish):
    half = x.shape[0] // 2
    near = yield "ctx", SWAP, lax.dynamic_slice_in_dim(run.tied(x), lax.axis_index("tensor") % 2 * half, half, 0)
    near = run.arrived(near)
    pair = yield "tensor", CORES, near
    finish(near, pair)


class Unit:
    def __init__(self, run, steps):
        self.run, self.steps, self.message = run, steps, None

    def request(self):
        try:
            return self.steps.send(self.message)
        except StopIteration:
            return None

    def advance(self):
        request = self.request()
        if request:
            axis, perm, value = request
            self.message = lax.ppermute(value, axis, perm)

    def advance_with(self, other):
        (_, _, inward), (_, _, outward) = self.request(), other.request()
        self.message = other.message = lax.ppermute(self.run(choose, outward, inward), "dp", INWARD + OUTWARD)

    def wait(self):
        self.message = self.run.arrived(self.message)


class Held:
    pass


def two_spans(
    tokens, segments, padding, cotangent, norm1_gain, norm1_shift, norm2_gain, norm2_shift,
    qkv_weight, qkv_bias, out_weight, out_bias, up_weight, up_bias, down_weight, down_bias,
):
    x, dy = tokens[0], cotangent[0]
    rows, width = x.shape
    local = qkv_weight.shape[2]
    hidden = up_weight.shape[1]
    lanes = 2 * HEAD_DIM
    row = lambda v: v.reshape(1, -1)
    w3 = jnp.transpose(qkv_weight, (1, 0, 2))
    run = Sequence()
    s, u = Held(), Held()
    dests = {}
    shapes = {"down": (hidden, width), "up": (width, hidden), "qkv": (3, width, local), "out": (local, width),
              "vec": (EXTRA, width // 2)}

    def open_unit(name, steps, *operands):
        setattr(u, name, Unit(run, steps(run, *operands)))

    def placing(names, kernel, count, blocks, indices):
        def finish(a, b):
            held = [n for n in names if n in dests]

            def step(a, b, *old):
                return pl.pallas_call(
                    kernel,
                    grid=(count,),
                    in_specs=[resident()] * 2 + [pl.BlockSpec(memory_space=pl.ANY)] * len(old),
                    out_specs=[pl.BlockSpec(block, index) for block, index in zip(blocks, indices)],
                    out_shape=[struct(shapes[n], F32) for n in names],
                    input_output_aliases={2 + i: names.index(n) for i, n in enumerate(held)},
                    compiler_params=params(24),
                    cost_estimate=cost(0, 0),
                    name="place",
                )(a, b, *old)

            dests.update(zip(names, run(step, a, b, *[dests[n] for n in held])))

        return finish

    open_unit("tk", gather_span, x, lambda *p: s.__dict__.update(tokens=p))
    open_unit("dy", gather_span, dy, lambda *p: s.__dict__.update(dy=p))

    def ids_0():
        ids = jnp.concatenate([segments, padding], axis=0)
        s.ids = ids, run.send(ids, "ctx", SWAP)

    def ids_w():
        s.ids = s.ids[0], run.arrived(s.ids[1])

    def early():
        s.pack = jnp.stack([norm1_gain, norm1_shift, norm2_gain, norm2_shift, up_bias, out_bias, down_bias])
        s.n1, s.n2, s.act, s.gu, s.gub, grad = run(early_call, x, dy, up_weight, down_weight, s.pack)
        open_early(0, grad)

    def open_early(i, grad):
        open_unit(f"E{i}", line_then_ctx, grad, placing(
            ["down"], place_sum_kernel, 1, [(hidden // 2, width // 2)], [lambda _: (i, 0)]))

    def own():
        s.act, s.gu, s.gub, grad = run(
            own_call, s.n2, dy, up_weight, down_weight, s.pack, s.act, s.gu, s.gub)
        open_early(1, grad)

    def other():
        u.tk.advance()
        s.n1x, s.n2x, *heads, s.actx, s.slope = run(
            other_call, *s.tokens, s.n1, s.pack, w3, qkv_bias, s.table, up_weight)
        s.qkv, s.qkvx = heads[:3], heads[3:]

    def tables():
        s.table = run(turn_table, jnp.arange(2 * rows, dtype=jnp.int32))

    def weights():
        u.dy.advance()
        s.dyx, s.gux, s.ga, grad = run(
            weights_call, *s.dy, s.act, dy, s.actx, s.slope, down_weight, out_weight)
        open_unit("D1", line_then_ctx, grad, placing(
            ["down"], place_halves_kernel, 2, [(hidden // 2, width // 2)], [lambda i: (i, 1)]))

    def first_head():
        s.first = run(lambda *a: first_head_call(a[:3], a[3:6], *a[6:]), *s.qkv, *s.qkvx, s.ga, *s.ids, s.table)

    def attend():
        s.mine, s.theirs, s.qk, vo_grad, *ups = run(
            lambda *a: attend_call(a[:3], a[3:6], *a[6:10], a[10:12], *a[12:]),
            *s.qkv, *s.qkvx, s.ga, *s.ids, s.table, *s.first,
            s.n1, s.n1x, dy, s.dyx, s.n2, s.n2x, s.gu, s.gux)
        open_unit("Q1", line_then_ctx, vo_grad, placing(
            ["qkv", "out"], place_pair_kernel, 2, [(1, width, lanes), (lanes, width)],
            [lambda i: (2, 0, i), lambda i: (i, 0)]))
        for j, grad in enumerate(ups):
            open_unit(f"U{j}", line_then_ctx, grad, placing(
                ["up"], place_halves_kernel, 2, [(width // 2, hidden // 2)], [lambda i, j=j: (j, i)]))

    def gpx_0():
        s.recv = run.send(s.theirs, "ctx", SWAP)

    def gpx_w():
        s.recv = run.arrived(s.recv)

    def branch_sums():
        s.branch = run(branch_sums_call, s.act, s.gu, dy, x, up_weight, down_weight)

    def sums():
        keep, send, s.vec = run(sums_call, s.mine, s.recv, s.branch, x, s.pack, w3, out_weight, s.gub)

        def finish(a, b):
            s.block_output, s.input_grad = run(lambda a, b: results_call(a, b, x, dy, s.pack), a, b)

        open_unit("both", over_tensor, keep, send, finish)

    def join():
        both = run(ride, s.qk, s.vec)
        put = placing(
            ["qkv", "vec"], place_ride_kernel, 2, [(2, width, lanes), s.vec.shape], [lambda i: (0, 0, i), lambda i: (0, 0)])

        def finish(a, b):
            put(a, b)
            open_unit("vec", vectors_over_tensor, local, dests["vec"], lambda rows: s.__dict__.update(rows=rows))

        open_unit("Q0", line_then_ctx, both, finish)

    u.tk.advance()
    early()
    u.E0.advance()
    u.dy.advance()
    own()
    tables()
    u.tk.advance()
    ids_0()
    other()
    u.E0.wait()
    u.E1.advance()
    u.E0.advance()
    u.dy.advance()
    weights()
    u.D1.advance()
    ids_w()
    first_head()
    u.E0.advance()
    u.E1.advance()
    attend()
    gpx_0()
    u.D1.wait()
    u.U0.advance_with(u.E1)
    u.D1.advance()
    branch_sums()
    u.E0.advance()
    gpx_w()
    sums()
    join()
    u.U0.wait()
    u.Q0.advance_with(u.D1)
    u.U0.advance()
    u.E1.advance()
    u.both.advance()
    u.E0.advance()
    u.Q0.wait()
    u.Q1.advance_with(u.U0)
    u.Q0.advance()
    u.D1.advance()
    u.both.advance()
    u.E1.advance()
    u.Q1.wait()
    u.U1.advance_with(u.Q0)
    u.Q1.advance()
    u.U0.advance()
    u.D1.advance()
    u.U1.advance()
    u.Q1.advance()
    u.Q0.advance()
    u.both.advance()
    u.U0.advance()
    u.U1.advance()
    u.Q1.advance()
    u.Q0.advance()
    u.vec.advance()
    u.U1.advance()
    u.both.advance()
    u.Q1.advance()
    u.vec.advance()
    u.vec.advance()
    u.U1.advance()
    *rows, heads_bias = s.rows
    gain1, shift1, gain2, shift2, dy_sum, up_sum, dy_same = [r.reshape(-1) for r in rows]
    return (
        s.block_output[None],
        s.input_grad[None],
        gain1, shift1, gain2, shift2,
        jnp.transpose(dests["qkv"], (1, 0, 2)),
        heads_bias,
        dests["out"],
        dy_sum,
        dests["up"],
        up_sum,
        dests["down"],
        dy_same,
    )


def fits(mesh):
    return dict(mesh.shape) == {"dp": 4, "ctx": 2, "tensor": 4}


def solution(mesh):
    return jax.shard_map(
        two_spans if fits(mesh) else on_device,
        mesh=mesh,
        in_specs=(
            P("dp", "ctx", None),
            P("dp", "ctx"),
            P("dp", "ctx"),
            P("dp", "ctx", None),
            P(),
            P(),
            P(),
            P(),
            P(None, None, "tensor"),
            P(None, "tensor"),
            P("tensor", None),
            P(),
            P(None, "tensor"),
            P("tensor"),
            P("tensor", None),
            P(),
        ),
        out_specs=(
            P("dp", "ctx", None),
            P("dp", "ctx", None),
            P(),
            P(),
            P(),
            P(),
            P(None, None, "tensor"),
            P(None, "tensor"),
            P("tensor", None),
            P(),
            P(None, "tensor"),
            P("tensor"),
            P("tensor", None),
            P(),
        ),
        check_vma=False,
    )
```

```python
import functools

import jax
import jax.numpy as jnp
from jax import lax
from jax.sharding import PartitionSpec as P
from jax.experimental import pallas as pl
from jax.experimental.pallas import tpu as pltpu

HEAD_DIM = 64
ROT = 16
KBLOCK = 512


def layer_norm(values, gain_vec, shift_vec):
    centre = jnp.mean(values, axis=-1, keepdims=True)
    centred = values - centre
    spread = jnp.mean(centred * centred, axis=-1, keepdims=True)
    return centred * lax.rsqrt(spread + 1e-05) * gain_vec + shift_vec


def norm_back(values, gain_vec, shift_vec, upstream):
    outcome, pullback = jax.vjp(layer_norm, values, gain_vec, shift_vec)
    return pullback(upstream)


def gelu_exact(values):
    return jax.nn.gelu(values, approximate=False)


def rotary_tables(positions):
    half_dims = ROT // 2
    freq_index = jnp.arange(half_dims, dtype=jnp.float32)
    inverse = jnp.exp(freq_index * (-2.0 * jnp.log(10000.0) / ROT))
    angles = positions.astype(jnp.float32)[:, None] * inverse[None, :]
    return (jnp.cos(angles)[:, None, :], jnp.sin(angles)[:, None, :])


def rotate(values, cosine_tab, sine_tab):
    half_dims = ROT // 2
    first_half = values[..., :half_dims]
    second_half = values[..., half_dims:ROT]
    return jnp.concatenate(
        [
            first_half * cosine_tab - second_half * sine_tab,
            second_half * cosine_tab + first_half * sine_tab,
            values[..., ROT:],
        ],
        axis=-1,
    )


def score_block(query_block, key_block, query_at, query_doc, key_at, key_doc):
    scores = jnp.einsum(
        "qhd,khd->hqk", query_block, key_block, preferred_element_type=jnp.float32
    ) * HEAD_DIM ** (-0.5)
    visible = (key_at[None, :] <= query_at[:, None]) & (
        (key_doc[None, :] == query_doc[:, None]) | (key_at[None, :] == query_at[:, None])
    )
    return (scores, visible[None])


def grad_scores(
    query_block,
    grad_block,
    query_at,
    query_doc,
    top_block,
    delta_block,
    key_block,
    value_block,
    key_at,
    key_doc,
):
    scores, visible = score_block(query_block, key_block, query_at, query_doc, key_at, key_doc)
    probs_full = jnp.where(
        visible, jnp.exp(jnp.where(visible, scores, -1e30) - top_block[..., None]), 0.0
    )
    probs_grad = jnp.einsum(
        "qhd,khd->hqk", grad_block, value_block, preferred_element_type=jnp.float32
    )
    score_grad = (probs_full * (probs_grad - delta_block[..., None])).astype(jnp.bfloat16)
    return (probs_full.astype(jnp.bfloat16), score_grad)


def on_device(
    tokens,
    segments,
    padding,
    cotangent,
    norm1_gain,
    norm1_shift,
    norm2_gain,
    norm2_shift,
    qkv_weight,
    qkv_bias,
    out_weight,
    out_bias,
    up_weight,
    up_bias,
    down_weight,
    down_bias,
):
    inputs = tokens[0].astype(jnp.float32)
    seg_own = segments[0]
    pad_own = padding[0]
    span_rows = inputs.shape[0]
    local_width = qkv_weight.shape[2]
    heads_loc = local_width // HEAD_DIM
    score_scale = HEAD_DIM ** (-0.5)
    query_pos = lax.axis_index("ctx") * span_rows + jnp.arange(span_rows, dtype=jnp.int32)
    normed1 = layer_norm(inputs, norm1_gain, norm1_shift).astype(jnp.bfloat16)
    normed2 = layer_norm(inputs, norm2_gain, norm2_shift).astype(jnp.bfloat16)
    projected = (
        jnp.einsum("cd,dtf->ctf", normed1, qkv_weight, preferred_element_type=jnp.float32)
        + qkv_bias[None]
    )
    projected = projected.reshape(span_rows, 3, heads_loc, HEAD_DIM)
    cosine_tab, sine_tab = rotary_tables(query_pos)
    queries = rotate(projected[:, 0], cosine_tab, sine_tab).astype(jnp.bfloat16)
    keys_own = rotate(projected[:, 1], cosine_tab, sine_tab).astype(jnp.bfloat16)
    values_own = projected[:, 2].astype(jnp.bfloat16)
    code_own = jnp.where(pad_own == 1, seg_own, -1)
    keys_all, values_all, codes_all = (
        lax.all_gather(keys_own.reshape(span_rows, local_width), "ctx", axis=0, tiled=True),
        lax.all_gather(values_own.reshape(span_rows, local_width), "ctx", axis=0, tiled=True),
        lax.all_gather(code_own, "ctx", axis=0, tiled=True),
    )
    seq_len = keys_all.shape[0]
    block_count = seq_len // KBLOCK
    key_pos = jnp.arange(seq_len, dtype=jnp.int32)
    key_blocks = keys_all.reshape(block_count, KBLOCK, heads_loc, HEAD_DIM)
    value_blocks = values_all.reshape(block_count, KBLOCK, heads_loc, HEAD_DIM)
    code_blocks = codes_all.reshape(block_count, KBLOCK)
    pos_blocks = key_pos.reshape(block_count, KBLOCK)

    def total_step(state_pair, block_data):
        run_top, run_sum = state_pair
        key_block, code_block, pos_block = block_data
        scores, visible = score_block(queries, key_block, query_pos, seg_own, pos_block, code_block)
        masked = jnp.where(visible, scores, -1e30)
        new_top = jnp.maximum(run_top, jnp.max(masked, axis=-1))
        fresh_sum = jnp.sum(jnp.where(visible, jnp.exp(masked - new_top[..., None]), 0.0), axis=-1)
        return ((new_top, run_sum * jnp.exp(run_top - new_top) + fresh_sum), None)

    start_state = (
        jnp.full((heads_loc, span_rows), -1e30, jnp.float32),
        jnp.zeros((heads_loc, span_rows), jnp.float32),
    )
    final_pair, unused = lax.scan(total_step, start_state, (key_blocks, code_blocks, pos_blocks))
    log_total = final_pair[0] + jnp.log(final_pair[1])

    def attend_step(running, block_data):
        key_block, value_block, code_block, pos_block = block_data
        scores, visible = score_block(queries, key_block, query_pos, seg_own, pos_block, code_block)
        weights_low = jnp.where(
            visible, jnp.exp(jnp.where(visible, scores, -1e30) - log_total[..., None]), 0.0
        ).astype(jnp.bfloat16)
        return (
            running
            + jnp.einsum(
                "hqk,khd->qhd", weights_low, value_block, preferred_element_type=jnp.float32
            ),
            None,
        )

    zero_heads = jnp.zeros((span_rows, heads_loc, HEAD_DIM), jnp.float32)
    attended, unused = lax.scan(
        attend_step, zero_heads, (key_blocks, value_blocks, code_blocks, pos_blocks)
    )
    attended_b = attended.reshape(span_rows, local_width).astype(jnp.bfloat16)
    upward = jnp.dot(normed2, up_weight, preferred_element_type=jnp.float32) + up_bias
    activated = gelu_exact(upward).astype(jnp.bfloat16)
    partial_sum = jnp.dot(attended_b, out_weight, preferred_element_type=jnp.float32) + jnp.dot(
        activated, down_weight, preferred_element_type=jnp.float32
    )
    bias_sum = out_bias + down_bias
    summed = lax.psum(partial_sum.astype(jnp.bfloat16), "tensor").astype(jnp.float32)
    block_output = (inputs + summed + bias_sum).astype(jnp.bfloat16)
    grad_in = cotangent[0]
    grad_att_b = jnp.einsum(
        "cd,fd->cf", grad_in, out_weight, preferred_element_type=jnp.float32
    ).astype(jnp.bfloat16)
    grad_act = jnp.einsum("cd,fd->cf", grad_in, down_weight, preferred_element_type=jnp.float32)
    unused, gelu_pull = jax.vjp(gelu_exact, upward)
    grad_up_b = gelu_pull(grad_act)[0].astype(jnp.bfloat16)
    grad_heads = grad_att_b.reshape(span_rows, heads_loc, HEAD_DIM)
    delta_t = jnp.sum(grad_heads.astype(jnp.float32) * attended, axis=-1).T

    def both_step(query_grad, block_data):
        key_block, value_block, code_block, pos_block = block_data
        probs_low, score_grad = grad_scores(
            queries,
            grad_heads,
            query_pos,
            seg_own,
            log_total,
            delta_t,
            key_block,
            value_block,
            pos_block,
            code_block,
        )
        query_grad = query_grad + jnp.einsum(
            "hqk,khd->qhd", score_grad, key_block, preferred_element_type=jnp.float32
        )
        key_grad = jnp.einsum(
            "hqk,qhd->khd", score_grad, queries, preferred_element_type=jnp.float32
        )
        value_grad = jnp.einsum(
            "hqk,qhd->khd", probs_low, grad_heads, preferred_element_type=jnp.float32
        )
        return (query_grad, (key_grad, value_grad))

    query_grad, stacked = lax.scan(
        both_step, zero_heads, (key_blocks, value_blocks, code_blocks, pos_blocks)
    )
    key_grad, value_grad = (
        lax.psum_scatter(
            stacked[0].reshape(seq_len, local_width).astype(jnp.bfloat16),
            "ctx",
            scatter_dimension=0,
            tiled=True,
        ).astype(jnp.float32),
        lax.psum_scatter(
            stacked[1].reshape(seq_len, local_width).astype(jnp.bfloat16),
            "ctx",
            scatter_dimension=0,
            tiled=True,
        ).astype(jnp.float32),
    )
    key_grad = key_grad.reshape(span_rows, heads_loc, HEAD_DIM)
    value_grad = value_grad.reshape(span_rows, heads_loc, HEAD_DIM)
    query_pre = rotate(query_grad * score_scale, cosine_tab, -sine_tab)
    key_pre = rotate(key_grad * score_scale, cosine_tab, -sine_tab)
    grad_proj = (
        jnp.stack([query_pre, key_pre, value_grad], axis=1)
        .reshape(span_rows, 3, local_width)
        .astype(jnp.bfloat16)
    )
    grad_qkv_w = jnp.einsum("cd,ctf->dtf", normed1, grad_proj, preferred_element_type=jnp.float32)
    grad_qkv_b = jnp.sum(grad_proj.astype(jnp.float32), axis=0)
    grad_out_w = jnp.einsum("cf,cd->fd", attended_b, grad_in, preferred_element_type=jnp.float32)
    grad_bias_shared = jnp.sum(grad_in.astype(jnp.float32), axis=0)
    grad_up_w = jnp.einsum("cd,cf->df", normed2, grad_up_b, preferred_element_type=jnp.float32)
    grad_up_bias = jnp.sum(grad_up_b.astype(jnp.float32), axis=0)
    grad_down_w = jnp.einsum("cf,cd->fd", activated, grad_in, preferred_element_type=jnp.float32)
    norm_in1 = jnp.einsum("ctf,dtf->cd", grad_proj, qkv_weight, preferred_element_type=jnp.float32)
    norm_in2 = jnp.einsum("cf,df->cd", grad_up_b, up_weight, preferred_element_type=jnp.float32)
    full_one, full_two = (
        lax.psum(norm_in1.astype(jnp.bfloat16), "tensor").astype(jnp.float32),
        lax.psum(norm_in2.astype(jnp.bfloat16), "tensor").astype(jnp.float32),
    )
    input_one, gain_one, shift_one = norm_back(inputs, norm1_gain, norm1_shift, full_one)
    input_two, gain_two, shift_two = norm_back(inputs, norm2_gain, norm2_shift, full_two)
    input_grad = (grad_in.astype(jnp.float32) + input_one + input_two).astype(jnp.bfloat16)
    summed_grads = lax.psum(
        (
            gain_one,
            shift_one,
            gain_two,
            shift_two,
            grad_qkv_w,
            grad_qkv_b,
            grad_out_w,
            grad_bias_shared,
            grad_up_w,
            grad_up_bias,
            grad_down_w,
        ),
        ("dp", "ctx"),
    )
    return (
        block_output[None],
        input_grad[None],
        summed_grads[0],
        summed_grads[1],
        summed_grads[2],
        summed_grads[3],
        summed_grads[4],
        summed_grads[5],
        summed_grads[6],
        summed_grads[7],
        summed_grads[8],
        summed_grads[9],
        summed_grads[10],
        summed_grads[7],
    )


F32 = jnp.float32
BF16 = jnp.bfloat16
NEG = -1e30
MIB = 1 << 20
CHUNKS = 4


def params(mib=40):
    return pltpu.CompilerParams(vmem_limit_bytes=mib * MIB)


def cost(flops, moved):
    return pl.CostEstimate(flops=1024, bytes_accessed=1024, transcendentals=0)


def dot(a, b):
    return lax.dot_general(a, b, (((1,), (0,)), ((), ())), preferred_element_type=F32)


def dot_nt(a, b):
    return lax.dot_general(a, b, (((1,), (1,)), ((), ())), preferred_element_type=F32)


def dot_tn(a, b):
    return lax.dot_general(a, b, (((0,), (0,)), ((), ())), preferred_element_type=F32)


def whole(shape):
    return pl.BlockSpec(shape, lambda *_: (0,) * len(shape))


def struct(shape, dtype):
    return jax.ShapeDtypeStruct(shape, dtype)


def standard(values):
    centre = jnp.mean(values, axis=-1, keepdims=True)
    centred = values - centre
    spread = jnp.mean(centred * centred, axis=-1, keepdims=True)
    inverse = lax.rsqrt(spread + 1e-05)
    return centred * inverse, inverse


def ctx_flag():
    return lax.axis_index("ctx")


def inner_flag():
    z = lax.axis_index("dp")
    return ((z == 1) | (z == 2)).astype(jnp.int32)


def core_flag():
    return lax.axis_index("tensor") % 2


def halves(flag, values):
    rows = values.shape[0] // 2
    top, low = values[:rows], values[rows:]
    return jnp.where(flag == 0, top, low), jnp.where(flag == 0, low, top)


def resident():
    return pl.BlockSpec(memory_space=pltpu.VMEM)


def small(kernel, arrays, outs, name, mib=16, flops=0):
    return pl.pallas_call(
        kernel,
        in_specs=[resident()] * len(arrays),
        out_specs=[resident()] * len(outs),
        out_shape=list(outs),
        compiler_params=params(mib),
        cost_estimate=cost(flops, 1024),
        name=name,
    )(*arrays)


def fetched(kernel, arrays, outs, name, flops, later=0, scratch=(), mib=48):
    now = len(arrays) - later
    return pl.pallas_call(
        kernel,
        grid=(1,),
        in_specs=[whole(a.shape) for a in arrays[:now]] + [pl.BlockSpec(memory_space=pl.ANY)] * later,
        out_specs=[whole(o.shape) for o in outs],
        out_shape=list(outs),
        scratch_shapes=list(scratch),
        compiler_params=params(mib),
        cost_estimate=cost(flops, 1024),
        name=name,
    )(*arrays)


def add_kernel(a_ref, b_ref, o_ref):
    o_ref[...] = (a_ref[...].astype(F32) + b_ref[...].astype(F32)).astype(o_ref.dtype)


def add(a, b):
    return small(add_kernel, (a, b), [struct(a.shape, a.dtype)], "add")[0]


def choose_kernel(a_ref, b_ref, o_ref):
    o_ref[...] = jnp.where(inner_flag() == 1, a_ref[...], b_ref[...])


def choose(a, b):
    return small(choose_kernel, (a, b), [struct(a.shape, a.dtype)], "choose")[0]


def place_halves_kernel(mine_ref, other_ref, *refs):
    o_ref = refs[-1]
    rows = o_ref.shape[0]
    o_ref[...] = jnp.where(ctx_flag() == pl.program_id(0), mine_ref[:rows], other_ref[:rows]).astype(F32)


def turn_lanes(table):
    half, lanes = ROT // 2, 2 * HEAD_DIM
    row = lax.broadcasted_iota(jnp.int32, (2 * half, lanes), 0)
    lane = lax.broadcasted_iota(jnp.int32, (2 * half, lanes), 1) % HEAD_DIM
    turned = (lane < ROT) & (lane % half == row % half)
    pick_cos = jnp.where(turned & (row < half), 1.0, 0.0)
    pick_sin = jnp.where(turned & (row >= half), jnp.where(lane < half, -1.0, 1.0), 0.0)
    exact = functools.partial(
        lax.dot_general, dimension_numbers=(((0,), (0,)), ((), ())), precision=lax.Precision.HIGHEST,
        preferred_element_type=F32,
    )
    return exact(table, pick_cos) + jnp.where(lane[0:1] < ROT, 0.0, 1.0), exact(table, pick_sin)


def partner(values):
    lane = lax.broadcasted_iota(jnp.int32, values.shape, 1) % HEAD_DIM
    half = ROT // 2
    width = values.shape[1]
    return jnp.where(lane < half, pltpu.roll(values, width - half, 1), pltpu.roll(values, half, 1))


def turn(values, cosine, sine):
    return values * cosine + partner(values) * sine


def activation(up):
    phi = 0.5 * (1.0 + lax.erf(up * 0.7071067811865476))
    return (up * phi).astype(BF16), phi + up * (0.3989422804014327 * jnp.exp(up * up * -0.5))


def early_kernel(x_ref, dy_ref, up_ref, down_ref, pack_ref, n1_ref, n2_ref, act_ref, gu_ref, gub_ref, gd_ref):
    @pl.when(pl.program_id(0) == 0)
    def _():
        xhat, _ = standard(x_ref[...].astype(F32))
        n1_ref[...] = (xhat * pack_ref[0:1] + pack_ref[1:2]).astype(BF16)
        n2_ref[...] = (xhat * pack_ref[2:3] + pack_ref[3:4]).astype(BF16)

    branch(n2_ref, dy_ref, up_ref, down_ref, pack_ref, 0, act_ref, gu_ref, gub_ref, gd_ref)


def own_kernel(n2_ref, dy_ref, up_ref, down_ref, pack_ref, act_in, gu_in, gub_in, act_ref, gu_ref, gub_ref, gd_ref):
    branch(n2_ref, dy_ref, up_ref, down_ref, pack_ref, CHUNKS // 2, act_ref, gu_ref, gub_ref, gd_ref)


def branch(n2_ref, dy_ref, up_ref, down_ref, pack_ref, first, act_ref, gu_ref, gub_ref, gd_ref):
    step = pl.program_id(0)
    size, cols = act_ref.shape[1], gd_ref.shape[1]
    dy = dy_ref[...]
    bias = pack_ref[4:5, pl.ds(pl.multiple_of((first + step) * size, size), size)]
    act, slope = activation(dot(n2_ref[...], up_ref[...]) + bias)
    grad = (dot_nt(dy, down_ref[...]) * slope).astype(BF16)
    act_ref[...] = act
    gu_ref[...] = grad
    gub_ref[...] = jnp.sum(grad.astype(F32), axis=0, keepdims=True)
    gd_ref[pl.ds(pl.multiple_of(step * size, size), size)] = dot_tn(act, dy[:, :cols]).astype(BF16)

    @pl.when(step == CHUNKS // 2 - 1)
    def _():
        gd_ref[gd_ref.shape[0] - EXTRA :] = jnp.zeros((EXTRA, cols), BF16)


def branch_call(kernel, first, before, up_w, down_w, pack, outs, held, name):
    rows, width = before[0].shape
    hidden = up_w.shape[1]
    size = hidden // CHUNKS
    cols = pl.BlockSpec((rows, size), lambda i: (0, first + i))
    grads = unit_struct(hidden // 2, width // 2)
    count = len(before) + 3
    return pl.pallas_call(
        kernel,
        grid=(CHUNKS // 2,),
        in_specs=[whole(a.shape) for a in before] + [
            pl.BlockSpec((width, size), lambda i: (0, first + i)),
            pl.BlockSpec((size, width), lambda i: (first + i, 0)),
            whole(pack.shape),
        ] + [pl.BlockSpec(memory_space=pl.ANY)] * len(held),
        out_specs=[whole(o.shape) for o in outs] + [cols, cols, pl.BlockSpec((1, size), lambda i: (0, first + i))]
        + [whole(grads.shape)],
        out_shape=outs + [struct((rows, hidden), BF16)] * 2 + [struct((1, hidden), F32), grads],
        input_output_aliases={count + i: len(outs) + i for i in range(len(held))},
        compiler_params=params(48),
        cost_estimate=cost(5e9, 1024),
        name=name,
    )(*before, up_w, down_w, pack, *held)


def early_call(x, dy, up_w, down_w, pack):
    return branch_call(early_kernel, 0, (x, dy), up_w, down_w, pack, [struct(x.shape, BF16)] * 2, (), "early")


def own_call(n2, dy, up_w, down_w, pack, *held):
    return branch_call(own_kernel, CHUNKS // 2, (n2, dy), up_w, down_w, pack, [], held, "own")


def half_at(flag, size):
    return pl.ds(pl.multiple_of(flag * size, size), size)


def project(n1, span, w_ref, b_ref, table_ref, q_ref, k_ref, v_ref):
    lanes = q_ref.shape[1]
    mine = half_at(ctx_flag(), lanes)
    cosine, sine = turn_lanes(table_ref[:, half_at(span, n1.shape[0])])
    q_ref[...] = turn(dot(n1, w_ref[0, :, mine]) + b_ref[0:1, mine], cosine, sine).astype(BF16)
    k_ref[...] = turn(dot(n1, w_ref[1, :, mine]) + b_ref[1:2, mine], cosine, sine).astype(BF16)
    v_ref[...] = (dot(n1, w_ref[2, :, mine]) + b_ref[2:3, mine]).astype(BF16)


def pieces(near_ref, pair_ref, step):
    core, size = core_flag(), near_ref.shape[0]
    step(half_at(core, size), near_ref[...])
    step(half_at(1 - core, size), pair_ref[...])


def other_kernel(near_ref, pair_ref, n1_o_ref, pack_ref, w_ref, b_ref, table_ref, up_ref,
                 n1_ref, n2_ref, q_o_ref, k_o_ref, v_o_ref, q_ref, k_ref, v_ref, act_ref, slope_ref):
    def norm(at, x):
        xhat, _ = standard(x.astype(F32))
        n1_ref[at] = (xhat * pack_ref[0:1] + pack_ref[1:2]).astype(BF16)
        n2_ref[at] = (xhat * pack_ref[2:3] + pack_ref[3:4]).astype(BF16)

    pieces(near_ref, pair_ref, norm)
    project(n1_o_ref[...], ctx_flag(), w_ref, b_ref, table_ref, q_o_ref, k_o_ref, v_o_ref)
    project(n1_ref[...], 1 - ctx_flag(), w_ref, b_ref, table_ref, q_ref, k_ref, v_ref)
    size = slope_ref.shape[1] // 2
    for j in range(2):
        mine = pl.ds(pl.multiple_of(ctx_flag() * 2 * size + j * size, size), size)
        at = slice(j * size, (j + 1) * size)
        act_ref[:, at], slope_ref[:, at] = activation(dot(n2_ref[...], up_ref[:, mine]) + pack_ref[4:5, mine])


def other_call(near, pair, n1, pack, w3, bias, table, up_w):
    rows, width = 2 * near.shape[0], near.shape[1]
    half = up_w.shape[1] // 2
    head = struct((rows, 2 * HEAD_DIM), BF16)
    outs = [struct((rows, width), BF16)] * 2 + [head] * 6 + [struct((rows, half), BF16), struct((rows, half), F32)]
    return fetched(other_kernel, (near, pair, n1, pack, w3, bias, table, up_w), outs, "other", 5e9)


EXTRA = 16


def unit_struct(rows, cols):
    return struct((rows + EXTRA, cols), BF16)


def fill(ref, *values):
    rows = ref.shape[0] - EXTRA
    at = 0
    for value in values:
        for first in range(0, value.shape[0], rows):
            ref[:rows, at : at + value.shape[1]] = value[first : first + rows]
            at += value.shape[1]
    ref[rows:] = jnp.zeros((EXTRA, ref.shape[1]), ref.dtype)


def unfold(value, lanes, index, count):
    rows = value.shape[0] - EXTRA
    folds = [value[:rows, (index * count + i) * lanes : (index * count + i + 1) * lanes] for i in range(count)]
    return jnp.concatenate(folds, axis=0)


def weights_kernel(near_ref, pair_ref, act_o_ref, dy_o_ref, act_ref, slope_ref, down_ref, ow_ref,
                   dy_ref, gu_ref, ga_ref, gd_ref):
    hidden = slope_ref.shape[1]

    def put(at, dy):
        dy_ref[at] = dy

    pieces(near_ref, pair_ref, put)
    dy, dy_o = dy_ref[...], dy_o_ref[...]
    rows, lanes = dy.shape[0], ga_ref.shape[1]
    act_o, cols = act_o_ref[:, half_at(ctx_flag(), hidden)], gd_ref.shape[1]
    fill(gd_ref, (dot_tn(act_o, dy_o[:, cols:]) + dot_tn(act_ref[...], dy[:, cols:])).astype(BF16))
    gu_ref[...] = (dot_nt(dy, down_ref[half_at(ctx_flag(), hidden)]) * slope_ref[...]).astype(BF16)
    out_w = ow_ref[half_at(ctx_flag(), lanes)]
    ga_ref[half_at(ctx_flag(), rows)] = dot_nt(dy_o, out_w).astype(BF16)
    ga_ref[half_at(1 - ctx_flag(), rows)] = dot_nt(dy, out_w).astype(BF16)


def weights_call(near, pair, act_o, dy_o, act, slope, down_w, out_w):
    rows, width = dy_o.shape
    hidden = slope.shape[1]
    outs = [struct((rows, width), BF16), struct((rows, hidden), BF16), struct((2 * rows, 2 * HEAD_DIM), BF16)]
    outs.append(unit_struct(hidden, width // 2))
    arrays = (near, pair, act_o, dy_o, act, slope, down_w, out_w)
    return fetched(weights_kernel, arrays, outs, "weights", 4e9)


def in_order(own, other, axis=0):
    first = ctx_flag() == 0
    return jnp.concatenate([jnp.where(first, own, other), jnp.where(first, other, own)], axis=axis)


def attend_head(index, q_o_ref, k_o_ref, v_o_ref, q_x_ref, k_x_ref, v_x_ref, ga_ref, ids_o_ref, ids_x_ref, table_ref,
                q_ref, k_ref, v_ref, dk_ref, dv_ref, att_ref, gp_ref):
    rows, lanes = q_ref.shape
    cosine, sine = turn_lanes(table_ref[...])
    step = 256
    zero = jnp.zeros((), BF16)
    scale = HEAD_DIM ** (-0.5)
    q_ref[...] = in_order(q_o_ref[...], q_x_ref[...]) * jnp.asarray(scale, BF16)
    k_ref[...], v_ref[...] = in_order(k_o_ref[...], k_x_ref[...]), in_order(v_o_ref[...], v_x_ref[...])
    dk_ref[...] = jnp.zeros(dk_ref.shape, F32)
    dv_ref[...] = jnp.zeros(dv_ref.shape, F32)
    ids = in_order(ids_o_ref[...], ids_x_ref[...], axis=1)
    code = jnp.where(ids[1:2] == 1, ids[0:1], -1).astype(F32)
    doc = jnp.broadcast_to(ids[0:1].astype(F32), (8, rows)).T[:, 0:1]
    lane = lax.broadcasted_iota(jnp.int32, (1, lanes), 1)
    head = (lane // HEAD_DIM) == index
    for i in range(rows // step):
        at, upto = slice(i * step, (i + 1) * step), (i + 1) * step
        k, v = k_ref[:upto], v_ref[:upto]
        row = lax.broadcasted_iota(jnp.int32, (step, upto), 0) + i * step
        col = lax.broadcasted_iota(jnp.int32, (step, upto), 1)
        seen = ((col <= row) & (code[:, :upto] == doc[at])) | (col == row)
        bias = jnp.where(seen, 0.0, NEG)
        q, ga = q_ref[at], ga_ref[at]
        qh, gh = jnp.where(head, q, zero), jnp.where(head, ga, zero)
        scores = dot_nt(qh, k) + bias
        e = jnp.exp(scores - jnp.max(scores, axis=1, keepdims=True))
        p = e * (1.0 / jnp.sum(e, axis=1, keepdims=True))
        low = p.astype(BF16)
        att = jnp.where(head, dot(low, v), 0.0)
        delta = jnp.sum(att * gh.astype(F32), axis=1, keepdims=True)
        g = (p * (dot_nt(gh, v) - delta)).astype(BF16)
        query_grad = jnp.where(head, dot(g, k), 0.0)
        att_ref[at] = att.astype(BF16)
        gp_ref[0, at] = turn(query_grad * scale, cosine[at], -sine[at]).astype(BF16)
        dk_ref[:upto] += dot_tn(g, qh)
        dv_ref[:upto] += dot_tn(low, gh)
    gp_ref[1] = turn(dk_ref[...], cosine, -sine).astype(BF16)
    gp_ref[2] = dv_ref[...].astype(BF16)


def head_scratch(rows, lanes):
    return [pltpu.VMEM((rows, lanes), BF16)] * 3 + [pltpu.VMEM((rows, lanes), F32)] * 2


def first_head_kernel(*refs):
    attend_head(0, *refs[:10], *refs[12:], *refs[10:12])


def first_head_call(own, other, ga, ids, ids_x, table):
    arrays = (*own, *other, ga, ids, ids_x, table)
    outs = [struct(ga.shape, BF16), struct((3,) + ga.shape, BF16)]
    return fetched(first_head_kernel, arrays, outs, "first_head", 1024, 0, head_scratch(*ga.shape))


def attend_kernel(*refs):
    heads, (att_in, gp_in), later, outs = refs[:10], refs[10:12], refs[12:20], refs[20:26]
    att_ref, gp_ref, *held, sems = refs[26 + 5 :]
    keep_ref, send_ref, qk_grad_ref, vo_grad_ref, *up_refs = outs
    n1_o_ref, n1_x_ref, dy_o_ref, dy_x_ref, n2_o_ref, n2_x_ref, gu_o_ref, gu_x_ref = held
    span, hidden = n1_o_ref.shape[0], gu_x_ref.shape[1]
    mine, theirs = half_at(ctx_flag(), span), half_at(1 - ctx_flag(), span)
    sources = list(later)
    sources[6] = later[6].at[:, half_at(ctx_flag(), hidden)]
    copies = [pltpu.make_async_copy(src, dst, sems.at[i]) for i, (src, dst) in enumerate(zip(sources, held))]
    for copy in copies:
        copy.start()
    attend_head(1, *heads, *refs[26 : 26 + 5], att_ref, gp_ref)
    for ref, at in ((keep_ref, mine), (send_ref, theirs)):
        ref[0] = att_ref[at] + att_in[at]
        for t in range(3):
            ref[t + 1] = gp_ref[t, at] + gp_in[t, at]
    for copy in copies:
        copy.wait()
    q_grad, k_grad, v_grad = [
        (dot_tn(n1_o_ref[...], keep_ref[t]) + dot_tn(n1_x_ref[...], send_ref[t])).astype(BF16) for t in (1, 2, 3)
    ]
    o_grad = (dot_tn(dy_o_ref[...], keep_ref[0]) + dot_tn(dy_x_ref[...], send_ref[0])).astype(BF16)
    fill(qk_grad_ref, q_grad, k_grad)
    fill(vo_grad_ref, v_grad, o_grad)
    gu_o, gu_x = gu_o_ref[...], gu_x_ref[...]
    for i, ref in enumerate(up_refs):
        at = slice(i * (ref.shape[0] - EXTRA), (i + 1) * (ref.shape[0] - EXTRA))
        fill(ref, (dot_tn(n2_o_ref[:, at], gu_o) + dot_tn(n2_x_ref[:, at], gu_x)).astype(BF16))


def attend_call(own, other, ga, ids, ids_x, table, first, *later):
    arrays = (*own, *other, ga, ids, ids_x, table, *first, *later)
    rows, lanes = ga.shape
    span, width = later[0].shape
    hidden = later[-1].shape[1]
    outs = [struct((4, span, lanes), BF16)] * 2 + [unit_struct(width // 2, 4 * lanes)] * 2 + [unit_struct(width // 2, hidden)] * 2
    scratch = head_scratch(rows, lanes) + [pltpu.VMEM((rows, lanes), BF16), pltpu.VMEM((3, rows, lanes), BF16)]
    scratch += [pltpu.VMEM((span, width), BF16)] * 6 + [pltpu.VMEM((span, hidden), BF16)] * 2
    scratch.append(pltpu.SemaphoreType.DMA((len(later),)))
    return fetched(attend_kernel, arrays, outs, "attend", 1024, len(later), scratch)


def branch_sums_kernel(act_ref, gu_ref, dy_ref, x_ref, up_ref, down_ref, out_ref, grad_ref, sums_ref):
    two = dot_nt(gu_ref[...], up_ref[...])
    xhat, _ = standard(x_ref[...].astype(F32))
    grad_ref[...] = two
    out_ref[...] = dot(act_ref[...], down_ref[...])
    rows = [jnp.sum(v, axis=0, keepdims=True) for v in (two * xhat, two, dy_ref[...].astype(F32))]
    sums_ref[...] = jnp.concatenate(rows + [jnp.zeros((5, two.shape[1]), F32)], axis=0)


def branch_sums_call(act, gu, dy, x, up_w, down_w):
    outs = [struct(x.shape, F32)] * 2 + [struct((8, x.shape[1]), F32)]
    return small(branch_sums_kernel, (act, gu, dy, x, up_w, down_w), outs, "branch_sums", 24)


def sums_kernel(mine_ref, recv_ref, out_ref, grad_ref, sums_ref, x_ref, pack_ref, w_ref, ow_ref, gub_ref,
                keep_ref, send_ref, vec_ref):
    lanes = mine_ref.shape[2]
    heads = [(mine_ref, half_at(ctx_flag(), lanes)), (recv_ref, half_at(1 - ctx_flag(), lanes))]
    out, one = out_ref[...], None
    biases = []
    for ref, at in heads:
        out = out + dot(ref[0], ow_ref[at])
        for t in range(3):
            term = dot_nt(ref[t + 1], w_ref[t, :, at])
            one = term if one is None else one + term
        biases.append([jnp.sum(ref[t + 1].astype(F32), axis=0, keepdims=True) for t in range(3)])
    first = ctx_flag() == 0
    pairs = [(jnp.where(first, m, r), jnp.where(first, r, m)) for m, r in zip(*biases)]
    heads_bias = jnp.concatenate([half for pair in pairs for half in pair], axis=1)
    zeros = jnp.zeros((1, out.shape[1] - heads_bias.shape[1]), F32)
    xhat, _ = standard(x_ref[...].astype(F32))
    sums = sums_ref[...]
    rows = [jnp.sum(one * xhat, axis=0, keepdims=True), jnp.sum(one, axis=0, keepdims=True), sums[0:3], gub_ref[...]]
    rows += [jnp.concatenate([heads_bias, zeros], axis=1), jnp.zeros_like(sums[0:1])]
    vec = jnp.concatenate(rows, axis=0)
    cols = vec_ref.shape[1]
    vec_ref[...] = jnp.concatenate([vec[:, :cols], vec[:, cols:]], axis=0).astype(BF16)
    rows = x_ref.shape[0] // 2
    for at, value in ((0, out), (rows, one * pack_ref[0:1] + grad_ref[...] * pack_ref[2:3])):
        keep_ref[at : at + rows], send_ref[at : at + rows] = halves(core_flag(), value.astype(BF16))


def sums_call(mine, recv, branch, x, pack, w3, out_w, gub):
    rows, width = x.shape
    both = struct((rows, width), BF16)
    outs = [both, both, struct((EXTRA, width // 2), BF16)]
    return small(sums_kernel, (mine, recv, *branch, x, pack, w3, out_w, gub), outs, "sums", 32)


def ride_kernel(grad_ref, vec_ref, o_ref):
    rows = grad_ref.shape[0] - EXTRA
    o_ref[:rows] = grad_ref[:rows]
    o_ref[rows:] = vec_ref[...]


def ride(grad, vec):
    return small(ride_kernel, (grad, vec), [struct(grad.shape, BF16)], "ride")[0]


def place_ride_kernel(mine_ref, other_ref, *refs):
    grad_ref, vec_ref = refs[-2:]
    count, rows, lanes = grad_ref.shape
    value = jnp.where(ctx_flag() == pl.program_id(0), mine_ref[...], other_ref[...]).astype(F32)
    folds = rows // (mine_ref.shape[0] - EXTRA)
    for t in range(count):
        grad_ref[t] = unfold(value, lanes, t, folds)
    at = slice(mine_ref.shape[0] - EXTRA, mine_ref.shape[0])
    vec_ref[...] = mine_ref[at].astype(F32) + other_ref[at].astype(F32)


def rows_kernel(a_ref, b_ref, v_ref, *refs):
    heads_ref = refs[-1]
    held = jnp.concatenate([v_ref[:8], v_ref[8:]], axis=1)
    total = jnp.concatenate([a_ref[:8] + b_ref[:8], a_ref[8:] + b_ref[8:]], axis=1)
    for r, ref in enumerate(refs[:-1]):
        ref[...] = total[r : r + 1] if r < 4 else held[5:6] if r == 5 else held[4:5]
    cols = heads_ref.shape[1]
    for t in range(heads_ref.shape[0]):
        heads_ref[t : t + 1] = held[6:7, t * cols : (t + 1) * cols]


def rows_call(local, a, b, v):
    row = struct((1, 2 * a.shape[1]), F32)
    return small(rows_kernel, (a, b, v), [row] * 7 + [struct((3, local), F32)], "rows")


def place_sum_kernel(mine_ref, other_ref, *refs):
    rows = refs[-1].shape[0]
    refs[-1][...] = mine_ref[:rows].astype(F32) + other_ref[:rows].astype(F32)


def place_pair_kernel(mine_ref, other_ref, *refs):
    value = jnp.where(ctx_flag() == pl.program_id(0), mine_ref[...], other_ref[...]).astype(F32)
    heads_ref, out_ref = refs[-2:]
    lanes = heads_ref.shape[2]
    folds = heads_ref.shape[1] // (mine_ref.shape[0] - EXTRA)
    heads_ref[0] = unfold(value, lanes, 0, folds)
    out_ref[...] = unfold(value, lanes, 1, folds).T


def results_kernel(mine_ref, other_ref, x_ref, dy_ref, pack_ref, out_ref, grad_ref):
    rows = x_ref.shape[0] // 2
    bias = pack_ref[5:6] + pack_ref[6:7]
    first = core_flag() == 0
    for i in range(2):
        at = slice(i * rows, (i + 1) * rows)
        here, there = (mine_ref, other_ref) if i == 0 else (other_ref, mine_ref)
        out, grad = [
            jnp.where(first, here[part], there[part]).astype(F32) for part in (slice(0, rows), slice(rows, 2 * rows))
        ]
        x = x_ref[at].astype(F32)
        out_ref[at] = (x + out + bias).astype(BF16)
        xhat, inverse = standard(x)
        mean = jnp.mean(grad, axis=-1, keepdims=True)
        along = jnp.mean(grad * xhat, axis=-1, keepdims=True)
        grad_ref[at] = (dy_ref[at].astype(F32) + inverse * (grad - mean - xhat * along)).astype(BF16)


def results_call(mine, other, x, dy, pack):
    return small(results_kernel, (mine, other, x, dy, pack), [struct(x.shape, BF16)] * 2, "results", 24)


INWARD = [(0, 1), (3, 2)]
MIDDLE = [(1, 2), (2, 1)]
OUTWARD = [(1, 0), (2, 3)]
SWAP = [(0, 1), (1, 0)]
CORES = [(i, i ^ 1) for i in range(4)]
CHIPS = [(i, i ^ 2) for i in range(4)]


class Sequence:
    def __init__(self):
        self.last = None

    def tied(self, operands):
        if self.last is None:
            return operands
        return lax.optimization_barrier((operands, self.last))[0]

    def __call__(self, step, *operands):
        result = step(*self.tied(operands))
        self.last = jax.tree.leaves(result)[0]
        return result

    def send(self, value, axis, perm):
        return lax.ppermute(self.tied(value), axis, perm)

    def arrived(self, value):
        value = self.tied(value)
        self.last = value
        return value


def turn_table(positions):
    half = ROT // 2
    inverse = jnp.exp(jnp.arange(half, dtype=F32) * (-2.0 * jnp.log(10000.0) / ROT))
    angles = inverse[:, None] * positions.astype(F32)[None, :]
    return jnp.concatenate([jnp.cos(angles), jnp.sin(angles)], axis=0)


def line_then_ctx(run, x, finish):
    r = yield "dp", INWARD, run.tied(x)
    x = run(add, x, r)
    r = yield "dp", MIDDLE, x
    x = run(add, x, r)
    r = yield "dp", OUTWARD, x
    x = run(choose, x, r)
    r = yield "ctx", SWAP, x
    finish(x, r)


def over_tensor(run, mine, other, finish):
    r = yield "tensor", CORES, run.tied(other)
    mine = run(add, mine, r)
    r = yield "tensor", CHIPS, mine
    mine = run(add, mine, r)
    r = yield "tensor", CORES, mine
    finish(mine, r)


def vectors_over_tensor(run, local, vec, finish):
    r = yield "tensor", CORES, run.tied(vec)
    x = run(add, vec, r)
    r = yield "tensor", CHIPS, x
    finish(run(functools.partial(rows_call, local), x, r, vec))


def gather_span(run, x, finish):
    half = x.shape[0] // 2
    near = yield "ctx", SWAP, lax.dynamic_slice_in_dim(run.tied(x), lax.axis_index("tensor") % 2 * half, half, 0)
    near = run.arrived(near)
    pair = yield "tensor", CORES, near
    finish(near, pair)


class Unit:
    def __init__(self, run, steps):
        self.run, self.steps, self.message = run, steps, None

    def request(self):
        try:
            return self.steps.send(self.message)
        except StopIteration:
            return None

    def advance(self):
        request = self.request()
        if request:
            axis, perm, value = request
            self.message = lax.ppermute(value, axis, perm)

    def advance_with(self, other):
        (_, _, inward), (_, _, outward) = self.request(), other.request()
        self.message = other.message = lax.ppermute(self.run(choose, outward, inward), "dp", INWARD + OUTWARD)

    def wait(self):
        self.message = self.run.arrived(self.message)


class Held:
    pass


def two_spans(
    tokens, segments, padding, cotangent, norm1_gain, norm1_shift, norm2_gain, norm2_shift,
    qkv_weight, qkv_bias, out_weight, out_bias, up_weight, up_bias, down_weight, down_bias,
):
    x, dy = tokens[0], cotangent[0]
    rows, width = x.shape
    local = qkv_weight.shape[2]
    hidden = up_weight.shape[1]
    lanes = 2 * HEAD_DIM
    row = lambda v: v.reshape(1, -1)
    w3 = jnp.transpose(qkv_weight, (1, 0, 2))
    run = Sequence()
    s, u = Held(), Held()
    dests = {}
    shapes = {"down": (hidden, width), "up": (width, hidden), "qkv": (3, width, local), "out": (local, width),
              "vec": (EXTRA, width // 2)}

    def open_unit(name, steps, *operands):
        setattr(u, name, Unit(run, steps(run, *operands)))

    def placing(names, kernel, count, blocks, indices):
        def finish(a, b):
            held = [n for n in names if n in dests]

            def step(a, b, *old):
                return pl.pallas_call(
                    kernel,
                    grid=(count,),
                    in_specs=[resident()] * 2 + [pl.BlockSpec(memory_space=pl.ANY)] * len(old),
                    out_specs=[pl.BlockSpec(block, index) for block, index in zip(blocks, indices)],
                    out_shape=[struct(shapes[n], F32) for n in names],
                    input_output_aliases={2 + i: names.index(n) for i, n in enumerate(held)},
                    compiler_params=params(24),
                    cost_estimate=cost(0, 0),
                    name="place",
                )(a, b, *old)

            dests.update(zip(names, run(step, a, b, *[dests[n] for n in held])))

        return finish

    open_unit("tk", gather_span, x, lambda *p: s.__dict__.update(tokens=p))
    open_unit("dy", gather_span, dy, lambda *p: s.__dict__.update(dy=p))

    def ids_0():
        ids = jnp.concatenate([segments, padding], axis=0)
        s.ids = ids, run.send(ids, "ctx", SWAP)

    def ids_w():
        s.ids = s.ids[0], run.arrived(s.ids[1])

    def early():
        s.pack = jnp.stack([norm1_gain, norm1_shift, norm2_gain, norm2_shift, up_bias, out_bias, down_bias])
        s.n1, s.n2, s.act, s.gu, s.gub, grad = run(early_call, x, dy, up_weight, down_weight, s.pack)
        open_early(0, grad)

    def open_early(i, grad):
        open_unit(f"E{i}", line_then_ctx, grad, placing(
            ["down"], place_sum_kernel, 1, [(hidden // 2, width // 2)], [lambda _: (i, 0)]))

    def own():
        s.act, s.gu, s.gub, grad = run(
            own_call, s.n2, dy, up_weight, down_weight, s.pack, s.act, s.gu, s.gub)
        open_early(1, grad)

    def other():
        u.tk.advance()
        s.n1x, s.n2x, *heads, s.actx, s.slope = run(
            other_call, *s.tokens, s.n1, s.pack, w3, qkv_bias, s.table, up_weight)
        s.qkv, s.qkvx = heads[:3], heads[3:]

    def tables():
        s.table = run(turn_table, jnp.arange(2 * rows, dtype=jnp.int32))

    def weights():
        u.dy.advance()
        s.dyx, s.gux, s.ga, grad = run(
            weights_call, *s.dy, s.act, dy, s.actx, s.slope, down_weight, out_weight)
        open_unit("D1", line_then_ctx, grad, placing(
            ["down"], place_halves_kernel, 2, [(hidden // 2, width // 2)], [lambda i: (i, 1)]))

    def first_head():
        s.first = run(lambda *a: first_head_call(a[:3], a[3:6], *a[6:]), *s.qkv, *s.qkvx, s.ga, *s.ids, s.table)

    def attend():
        s.mine, s.theirs, s.qk, vo_grad, *ups = run(
            lambda *a: attend_call(a[:3], a[3:6], *a[6:10], a[10:12], *a[12:]),
            *s.qkv, *s.qkvx, s.ga, *s.ids, s.table, *s.first,
            s.n1, s.n1x, dy, s.dyx, s.n2, s.n2x, s.gu, s.gux)
        open_unit("Q1", line_then_ctx, vo_grad, placing(
            ["qkv", "out"], place_pair_kernel, 2, [(1, width, lanes), (lanes, width)],
            [lambda i: (2, 0, i), lambda i: (i, 0)]))
        for j, grad in enumerate(ups):
            open_unit(f"U{j}", line_then_ctx, grad, placing(
                ["up"], place_halves_kernel, 2, [(width // 2, hidden // 2)], [lambda i, j=j: (j, i)]))

    def gpx_0():
        s.recv = run.send(s.theirs, "ctx", SWAP)

    def gpx_w():
        s.recv = run.arrived(s.recv)

    def branch_sums():
        s.branch = run(branch_sums_call, s.act, s.gu, dy, x, up_weight, down_weight)

    def sums():
        keep, send, s.vec = run(sums_call, s.mine, s.recv, s.branch, x, s.pack, w3, out_weight, s.gub)

        def finish(a, b):
            s.block_output, s.input_grad = run(lambda a, b: results_call(a, b, x, dy, s.pack), a, b)

        open_unit("both", over_tensor, keep, send, finish)

    def join():
        both = run(ride, s.qk, s.vec)
        put = placing(
            ["qkv", "vec"], place_ride_kernel, 2, [(2, width, lanes), s.vec.shape], [lambda i: (0, 0, i), lambda i: (0, 0)])

        def finish(a, b):
            put(a, b)
            open_unit("vec", vectors_over_tensor, local, dests["vec"], lambda rows: s.__dict__.update(rows=rows))

        open_unit("Q0", line_then_ctx, both, finish)

    u.tk.advance()
    early()
    u.E0.advance()
    u.dy.advance()
    own()
    tables()
    u.tk.advance()
    ids_0()
    other()
    u.E0.wait()
    u.E1.advance()
    u.E0.advance()
    u.dy.advance()
    weights()
    u.D1.advance()
    first_head()
    ids_w()
    u.E0.advance()
    u.E1.advance()
    attend()
    gpx_0()
    u.D1.wait()
    u.U0.advance_with(u.E1)
    u.D1.advance()
    branch_sums()
    u.E0.wait()
    u.E0.advance()
    gpx_w()
    sums()
    join()
    u.U0.wait()
    u.Q0.advance_with(u.D1)
    u.U0.advance()
    u.E1.advance()
    u.both.advance()
    u.E0.advance()
    u.Q0.wait()
    u.Q1.advance_with(u.U0)
    u.Q0.advance()
    u.D1.advance()
    u.both.advance()
    u.E1.advance()
    u.Q1.wait()
    u.U1.advance_with(u.Q0)
    u.Q1.advance()
    u.U0.advance()
    u.D1.advance()
    u.U1.wait()
    u.U1.advance()
    u.Q1.advance()
    u.Q0.advance()
    u.both.advance()
    u.U0.advance()
    u.Q0.advance()
    u.U1.advance()
    u.Q1.advance()
    u.vec.advance()
    u.U1.advance()
    u.both.advance()
    u.Q1.advance()
    u.vec.advance()
    u.vec.advance()
    u.U1.advance()
    *rows, heads_bias = s.rows
    gain1, shift1, gain2, shift2, dy_sum, up_sum, dy_same = [r.reshape(-1) for r in rows]
    return (
        s.block_output[None],
        s.input_grad[None],
        gain1, shift1, gain2, shift2,
        jnp.transpose(dests["qkv"], (1, 0, 2)),
        heads_bias,
        dests["out"],
        dy_sum,
        dests["up"],
        up_sum,
        dests["down"],
        dy_same,
    )


def fits(mesh):
    return dict(mesh.shape) == {"dp": 4, "ctx": 2, "tensor": 4}


def solution(mesh):
    return jax.shard_map(
        two_spans if fits(mesh) else on_device,
        mesh=mesh,
        in_specs=(
            P("dp", "ctx", None),
            P("dp", "ctx"),
            P("dp", "ctx"),
            P("dp", "ctx", None),
            P(),
            P(),
            P(),
            P(),
            P(None, None, "tensor"),
            P(None, "tensor"),
            P("tensor", None),
            P(),
            P(None, "tensor"),
            P("tensor"),
            P("tensor", None),
            P(),
        ),
        out_specs=(
            P("dp", "ctx", None),
            P("dp", "ctx", None),
            P(),
            P(),
            P(),
            P(),
            P(None, None, "tensor"),
            P(None, "tensor"),
            P("tensor", None),
            P(),
            P(None, "tensor"),
            P("tensor"),
            P("tensor", None),
            P(),
        ),
        check_vma=False,
    )
```

```python
import functools

import jax
import jax.numpy as jnp
from jax import lax
from jax.sharding import PartitionSpec as P
from jax.experimental import pallas as pl
from jax.experimental.pallas import tpu as pltpu

HEAD_DIM = 64
ROT = 16
KBLOCK = 512


def layer_norm(values, gain_vec, shift_vec):
    centre = jnp.mean(values, axis=-1, keepdims=True)
    centred = values - centre
    spread = jnp.mean(centred * centred, axis=-1, keepdims=True)
    return centred * lax.rsqrt(spread + 1e-05) * gain_vec + shift_vec


def norm_back(values, gain_vec, shift_vec, upstream):
    outcome, pullback = jax.vjp(layer_norm, values, gain_vec, shift_vec)
    return pullback(upstream)


def gelu_exact(values):
    return jax.nn.gelu(values, approximate=False)


def rotary_tables(positions):
    half_dims = ROT // 2
    freq_index = jnp.arange(half_dims, dtype=jnp.float32)
    inverse = jnp.exp(freq_index * (-2.0 * jnp.log(10000.0) / ROT))
    angles = positions.astype(jnp.float32)[:, None] * inverse[None, :]
    return (jnp.cos(angles)[:, None, :], jnp.sin(angles)[:, None, :])


def rotate(values, cosine_tab, sine_tab):
    half_dims = ROT // 2
    first_half = values[..., :half_dims]
    second_half = values[..., half_dims:ROT]
    return jnp.concatenate(
        [
            first_half * cosine_tab - second_half * sine_tab,
            second_half * cosine_tab + first_half * sine_tab,
            values[..., ROT:],
        ],
        axis=-1,
    )


def score_block(query_block, key_block, query_at, query_doc, key_at, key_doc):
    scores = jnp.einsum(
        "qhd,khd->hqk", query_block, key_block, preferred_element_type=jnp.float32
    ) * HEAD_DIM ** (-0.5)
    visible = (key_at[None, :] <= query_at[:, None]) & (
        (key_doc[None, :] == query_doc[:, None]) | (key_at[None, :] == query_at[:, None])
    )
    return (scores, visible[None])


def grad_scores(
    query_block,
    grad_block,
    query_at,
    query_doc,
    top_block,
    delta_block,
    key_block,
    value_block,
    key_at,
    key_doc,
):
    scores, visible = score_block(query_block, key_block, query_at, query_doc, key_at, key_doc)
    probs_full = jnp.where(
        visible, jnp.exp(jnp.where(visible, scores, -1e30) - top_block[..., None]), 0.0
    )
    probs_grad = jnp.einsum(
        "qhd,khd->hqk", grad_block, value_block, preferred_element_type=jnp.float32
    )
    score_grad = (probs_full * (probs_grad - delta_block[..., None])).astype(jnp.bfloat16)
    return (probs_full.astype(jnp.bfloat16), score_grad)


def on_device(
    tokens,
    segments,
    padding,
    cotangent,
    norm1_gain,
    norm1_shift,
    norm2_gain,
    norm2_shift,
    qkv_weight,
    qkv_bias,
    out_weight,
    out_bias,
    up_weight,
    up_bias,
    down_weight,
    down_bias,
):
    inputs = tokens[0].astype(jnp.float32)
    seg_own = segments[0]
    pad_own = padding[0]
    span_rows = inputs.shape[0]
    local_width = qkv_weight.shape[2]
    heads_loc = local_width // HEAD_DIM
    score_scale = HEAD_DIM ** (-0.5)
    query_pos = lax.axis_index("ctx") * span_rows + jnp.arange(span_rows, dtype=jnp.int32)
    normed1 = layer_norm(inputs, norm1_gain, norm1_shift).astype(jnp.bfloat16)
    normed2 = layer_norm(inputs, norm2_gain, norm2_shift).astype(jnp.bfloat16)
    projected = (
        jnp.einsum("cd,dtf->ctf", normed1, qkv_weight, preferred_element_type=jnp.float32)
        + qkv_bias[None]
    )
    projected = projected.reshape(span_rows, 3, heads_loc, HEAD_DIM)
    cosine_tab, sine_tab = rotary_tables(query_pos)
    queries = rotate(projected[:, 0], cosine_tab, sine_tab).astype(jnp.bfloat16)
    keys_own = rotate(projected[:, 1], cosine_tab, sine_tab).astype(jnp.bfloat16)
    values_own = projected[:, 2].astype(jnp.bfloat16)
    code_own = jnp.where(pad_own == 1, seg_own, -1)
    keys_all, values_all, codes_all = (
        lax.all_gather(keys_own.reshape(span_rows, local_width), "ctx", axis=0, tiled=True),
        lax.all_gather(values_own.reshape(span_rows, local_width), "ctx", axis=0, tiled=True),
        lax.all_gather(code_own, "ctx", axis=0, tiled=True),
    )
    seq_len = keys_all.shape[0]
    block_count = seq_len // KBLOCK
    key_pos = jnp.arange(seq_len, dtype=jnp.int32)
    key_blocks = keys_all.reshape(block_count, KBLOCK, heads_loc, HEAD_DIM)
    value_blocks = values_all.reshape(block_count, KBLOCK, heads_loc, HEAD_DIM)
    code_blocks = codes_all.reshape(block_count, KBLOCK)
    pos_blocks = key_pos.reshape(block_count, KBLOCK)

    def total_step(state_pair, block_data):
        run_top, run_sum = state_pair
        key_block, code_block, pos_block = block_data
        scores, visible = score_block(queries, key_block, query_pos, seg_own, pos_block, code_block)
        masked = jnp.where(visible, scores, -1e30)
        new_top = jnp.maximum(run_top, jnp.max(masked, axis=-1))
        fresh_sum = jnp.sum(jnp.where(visible, jnp.exp(masked - new_top[..., None]), 0.0), axis=-1)
        return ((new_top, run_sum * jnp.exp(run_top - new_top) + fresh_sum), None)

    start_state = (
        jnp.full((heads_loc, span_rows), -1e30, jnp.float32),
        jnp.zeros((heads_loc, span_rows), jnp.float32),
    )
    final_pair, unused = lax.scan(total_step, start_state, (key_blocks, code_blocks, pos_blocks))
    log_total = final_pair[0] + jnp.log(final_pair[1])

    def attend_step(running, block_data):
        key_block, value_block, code_block, pos_block = block_data
        scores, visible = score_block(queries, key_block, query_pos, seg_own, pos_block, code_block)
        weights_low = jnp.where(
            visible, jnp.exp(jnp.where(visible, scores, -1e30) - log_total[..., None]), 0.0
        ).astype(jnp.bfloat16)
        return (
            running
            + jnp.einsum(
                "hqk,khd->qhd", weights_low, value_block, preferred_element_type=jnp.float32
            ),
            None,
        )

    zero_heads = jnp.zeros((span_rows, heads_loc, HEAD_DIM), jnp.float32)
    attended, unused = lax.scan(
        attend_step, zero_heads, (key_blocks, value_blocks, code_blocks, pos_blocks)
    )
    attended_b = attended.reshape(span_rows, local_width).astype(jnp.bfloat16)
    upward = jnp.dot(normed2, up_weight, preferred_element_type=jnp.float32) + up_bias
    activated = gelu_exact(upward).astype(jnp.bfloat16)
    partial_sum = jnp.dot(attended_b, out_weight, preferred_element_type=jnp.float32) + jnp.dot(
        activated, down_weight, preferred_element_type=jnp.float32
    )
    bias_sum = out_bias + down_bias
    summed = lax.psum(partial_sum.astype(jnp.bfloat16), "tensor").astype(jnp.float32)
    block_output = (inputs + summed + bias_sum).astype(jnp.bfloat16)
    grad_in = cotangent[0]
    grad_att_b = jnp.einsum(
        "cd,fd->cf", grad_in, out_weight, preferred_element_type=jnp.float32
    ).astype(jnp.bfloat16)
    grad_act = jnp.einsum("cd,fd->cf", grad_in, down_weight, preferred_element_type=jnp.float32)
    unused, gelu_pull = jax.vjp(gelu_exact, upward)
    grad_up_b = gelu_pull(grad_act)[0].astype(jnp.bfloat16)
    grad_heads = grad_att_b.reshape(span_rows, heads_loc, HEAD_DIM)
    delta_t = jnp.sum(grad_heads.astype(jnp.float32) * attended, axis=-1).T

    def both_step(query_grad, block_data):
        key_block, value_block, code_block, pos_block = block_data
        probs_low, score_grad = grad_scores(
            queries,
            grad_heads,
            query_pos,
            seg_own,
            log_total,
            delta_t,
            key_block,
            value_block,
            pos_block,
            code_block,
        )
        query_grad = query_grad + jnp.einsum(
            "hqk,khd->qhd", score_grad, key_block, preferred_element_type=jnp.float32
        )
        key_grad = jnp.einsum(
            "hqk,qhd->khd", score_grad, queries, preferred_element_type=jnp.float32
        )
        value_grad = jnp.einsum(
            "hqk,qhd->khd", probs_low, grad_heads, preferred_element_type=jnp.float32
        )
        return (query_grad, (key_grad, value_grad))

    query_grad, stacked = lax.scan(
        both_step, zero_heads, (key_blocks, value_blocks, code_blocks, pos_blocks)
    )
    key_grad, value_grad = (
        lax.psum_scatter(
            stacked[0].reshape(seq_len, local_width).astype(jnp.bfloat16),
            "ctx",
            scatter_dimension=0,
            tiled=True,
        ).astype(jnp.float32),
        lax.psum_scatter(
            stacked[1].reshape(seq_len, local_width).astype(jnp.bfloat16),
            "ctx",
            scatter_dimension=0,
            tiled=True,
        ).astype(jnp.float32),
    )
    key_grad = key_grad.reshape(span_rows, heads_loc, HEAD_DIM)
    value_grad = value_grad.reshape(span_rows, heads_loc, HEAD_DIM)
    query_pre = rotate(query_grad * score_scale, cosine_tab, -sine_tab)
    key_pre = rotate(key_grad * score_scale, cosine_tab, -sine_tab)
    grad_proj = (
        jnp.stack([query_pre, key_pre, value_grad], axis=1)
        .reshape(span_rows, 3, local_width)
        .astype(jnp.bfloat16)
    )
    grad_qkv_w = jnp.einsum("cd,ctf->dtf", normed1, grad_proj, preferred_element_type=jnp.float32)
    grad_qkv_b = jnp.sum(grad_proj.astype(jnp.float32), axis=0)
    grad_out_w = jnp.einsum("cf,cd->fd", attended_b, grad_in, preferred_element_type=jnp.float32)
    grad_bias_shared = jnp.sum(grad_in.astype(jnp.float32), axis=0)
    grad_up_w = jnp.einsum("cd,cf->df", normed2, grad_up_b, preferred_element_type=jnp.float32)
    grad_up_bias = jnp.sum(grad_up_b.astype(jnp.float32), axis=0)
    grad_down_w = jnp.einsum("cf,cd->fd", activated, grad_in, preferred_element_type=jnp.float32)
    norm_in1 = jnp.einsum("ctf,dtf->cd", grad_proj, qkv_weight, preferred_element_type=jnp.float32)
    norm_in2 = jnp.einsum("cf,df->cd", grad_up_b, up_weight, preferred_element_type=jnp.float32)
    full_one, full_two = (
        lax.psum(norm_in1.astype(jnp.bfloat16), "tensor").astype(jnp.float32),
        lax.psum(norm_in2.astype(jnp.bfloat16), "tensor").astype(jnp.float32),
    )
    input_one, gain_one, shift_one = norm_back(inputs, norm1_gain, norm1_shift, full_one)
    input_two, gain_two, shift_two = norm_back(inputs, norm2_gain, norm2_shift, full_two)
    input_grad = (grad_in.astype(jnp.float32) + input_one + input_two).astype(jnp.bfloat16)
    summed_grads = lax.psum(
        (
            gain_one,
            shift_one,
            gain_two,
            shift_two,
            grad_qkv_w,
            grad_qkv_b,
            grad_out_w,
            grad_bias_shared,
            grad_up_w,
            grad_up_bias,
            grad_down_w,
        ),
        ("dp", "ctx"),
    )
    return (
        block_output[None],
        input_grad[None],
        summed_grads[0],
        summed_grads[1],
        summed_grads[2],
        summed_grads[3],
        summed_grads[4],
        summed_grads[5],
        summed_grads[6],
        summed_grads[7],
        summed_grads[8],
        summed_grads[9],
        summed_grads[10],
        summed_grads[7],
    )


F32 = jnp.float32
BF16 = jnp.bfloat16
NEG = -1e30
MIB = 1 << 20
CHUNKS = 4


def params(mib=40):
    return pltpu.CompilerParams(vmem_limit_bytes=mib * MIB)


def cost(flops, moved):
    return pl.CostEstimate(flops=1024, bytes_accessed=1024, transcendentals=0)


def dot(a, b):
    return lax.dot_general(a, b, (((1,), (0,)), ((), ())), preferred_element_type=F32)


def dot_nt(a, b):
    return lax.dot_general(a, b, (((1,), (1,)), ((), ())), preferred_element_type=F32)


def dot_tn(a, b):
    return lax.dot_general(a, b, (((0,), (0,)), ((), ())), preferred_element_type=F32)


def whole(shape):
    return pl.BlockSpec(shape, lambda *_: (0,) * len(shape))


def struct(shape, dtype):
    return jax.ShapeDtypeStruct(shape, dtype)


def standard(values):
    centre = jnp.mean(values, axis=-1, keepdims=True)
    centred = values - centre
    spread = jnp.mean(centred * centred, axis=-1, keepdims=True)
    inverse = lax.rsqrt(spread + 1e-05)
    return centred * inverse, inverse


def ctx_flag():
    return lax.axis_index("ctx")


def inner_flag():
    z = lax.axis_index("dp")
    return ((z == 1) | (z == 2)).astype(jnp.int32)


def core_flag():
    return lax.axis_index("tensor") % 2


def halves(flag, values):
    rows = values.shape[0] // 2
    top, low = values[:rows], values[rows:]
    return jnp.where(flag == 0, top, low), jnp.where(flag == 0, low, top)


def resident():
    return pl.BlockSpec(memory_space=pltpu.VMEM)


def small(kernel, arrays, outs, name, mib=16, flops=0):
    return pl.pallas_call(
        kernel,
        in_specs=[resident()] * len(arrays),
        out_specs=[resident()] * len(outs),
        out_shape=list(outs),
        compiler_params=params(mib),
        cost_estimate=cost(flops, 1024),
        name=name,
    )(*arrays)


def fetched(kernel, arrays, outs, name, flops, later=0, scratch=(), mib=48):
    now = len(arrays) - later
    return pl.pallas_call(
        kernel,
        grid=(1,),
        in_specs=[whole(a.shape) for a in arrays[:now]] + [pl.BlockSpec(memory_space=pl.ANY)] * later,
        out_specs=[whole(o.shape) for o in outs],
        out_shape=list(outs),
        scratch_shapes=list(scratch),
        compiler_params=params(mib),
        cost_estimate=cost(flops, 1024),
        name=name,
    )(*arrays)


def add_kernel(a_ref, b_ref, o_ref):
    o_ref[...] = (a_ref[...].astype(F32) + b_ref[...].astype(F32)).astype(o_ref.dtype)


def add(a, b):
    return small(add_kernel, (a, b), [struct(a.shape, a.dtype)], "add")[0]


def choose_kernel(a_ref, b_ref, o_ref):
    o_ref[...] = jnp.where(inner_flag() == 1, a_ref[...], b_ref[...])


def choose(a, b):
    return small(choose_kernel, (a, b), [struct(a.shape, a.dtype)], "choose")[0]


def place_halves_kernel(mine_ref, other_ref, *refs):
    o_ref = refs[-1]
    rows = o_ref.shape[0]
    o_ref[...] = jnp.where(ctx_flag() == pl.program_id(0), mine_ref[:rows], other_ref[:rows]).astype(F32)


def turn_lanes(table):
    half, lanes = ROT // 2, 2 * HEAD_DIM
    row = lax.broadcasted_iota(jnp.int32, (2 * half, lanes), 0)
    lane = lax.broadcasted_iota(jnp.int32, (2 * half, lanes), 1) % HEAD_DIM
    turned = (lane < ROT) & (lane % half == row % half)
    pick_cos = jnp.where(turned & (row < half), 1.0, 0.0)
    pick_sin = jnp.where(turned & (row >= half), jnp.where(lane < half, -1.0, 1.0), 0.0)
    exact = functools.partial(
        lax.dot_general, dimension_numbers=(((0,), (0,)), ((), ())), precision=lax.Precision.HIGHEST,
        preferred_element_type=F32,
    )
    return exact(table, pick_cos) + jnp.where(lane[0:1] < ROT, 0.0, 1.0), exact(table, pick_sin)


def partner(values):
    lane = lax.broadcasted_iota(jnp.int32, values.shape, 1) % HEAD_DIM
    half = ROT // 2
    width = values.shape[1]
    return jnp.where(lane < half, pltpu.roll(values, width - half, 1), pltpu.roll(values, half, 1))


def turn(values, cosine, sine):
    return values * cosine + partner(values) * sine


def activation(up):
    phi = 0.5 * (1.0 + lax.erf(up * 0.7071067811865476))
    return (up * phi).astype(BF16), phi + up * (0.3989422804014327 * jnp.exp(up * up * -0.5))


def early_kernel(x_ref, dy_ref, up_ref, down_ref, pack_ref, n1_ref, n2_ref, act_ref, gu_ref, gub_ref, gd_ref):
    @pl.when(pl.program_id(0) == 0)
    def _():
        xhat, _ = standard(x_ref[...].astype(F32))
        n1_ref[...] = (xhat * pack_ref[0:1] + pack_ref[1:2]).astype(BF16)
        n2_ref[...] = (xhat * pack_ref[2:3] + pack_ref[3:4]).astype(BF16)

    branch(n2_ref, dy_ref, up_ref, down_ref, pack_ref, 0, act_ref, gu_ref, gub_ref, gd_ref)


def own_kernel(n2_ref, dy_ref, up_ref, down_ref, pack_ref, act_in, gu_in, gub_in, act_ref, gu_ref, gub_ref, gd_ref):
    branch(n2_ref, dy_ref, up_ref, down_ref, pack_ref, CHUNKS // 2, act_ref, gu_ref, gub_ref, gd_ref)


def branch(n2_ref, dy_ref, up_ref, down_ref, pack_ref, first, act_ref, gu_ref, gub_ref, gd_ref):
    step = pl.program_id(0)
    size, cols = act_ref.shape[1], gd_ref.shape[1]
    dy = dy_ref[...]
    bias = pack_ref[4:5, pl.ds(pl.multiple_of((first + step) * size, size), size)]
    act, slope = activation(dot(n2_ref[...], up_ref[...]) + bias)
    grad = (dot_nt(dy, down_ref[...]) * slope).astype(BF16)
    act_ref[...] = act
    gu_ref[...] = grad
    gub_ref[...] = jnp.sum(grad.astype(F32), axis=0, keepdims=True)
    gd_ref[pl.ds(pl.multiple_of(step * size, size), size)] = dot_tn(act, dy[:, :cols]).astype(BF16)

    @pl.when(step == CHUNKS // 2 - 1)
    def _():
        gd_ref[gd_ref.shape[0] - EXTRA :] = jnp.zeros((EXTRA, cols), BF16)


def branch_call(kernel, first, before, up_w, down_w, pack, outs, held, name):
    rows, width = before[0].shape
    hidden = up_w.shape[1]
    size = hidden // CHUNKS
    cols = pl.BlockSpec((rows, size), lambda i: (0, first + i))
    grads = unit_struct(hidden // 2, width // 2)
    count = len(before) + 3
    return pl.pallas_call(
        kernel,
        grid=(CHUNKS // 2,),
        in_specs=[whole(a.shape) for a in before] + [
            pl.BlockSpec((width, size), lambda i: (0, first + i)),
            pl.BlockSpec((size, width), lambda i: (first + i, 0)),
            whole(pack.shape),
        ] + [pl.BlockSpec(memory_space=pl.ANY)] * len(held),
        out_specs=[whole(o.shape) for o in outs] + [cols, cols, pl.BlockSpec((1, size), lambda i: (0, first + i))]
        + [whole(grads.shape)],
        out_shape=outs + [struct((rows, hidden), BF16)] * 2 + [struct((1, hidden), F32), grads],
        input_output_aliases={count + i: len(outs) + i for i in range(len(held))},
        compiler_params=params(48),
        cost_estimate=cost(5e9, 1024),
        name=name,
    )(*before, up_w, down_w, pack, *held)


def early_call(x, dy, up_w, down_w, pack):
    return branch_call(early_kernel, 0, (x, dy), up_w, down_w, pack, [struct(x.shape, BF16)] * 2, (), "early")


def own_call(n2, dy, up_w, down_w, pack, *held):
    return branch_call(own_kernel, CHUNKS // 2, (n2, dy), up_w, down_w, pack, [], held, "own")


def half_at(flag, size):
    return pl.ds(pl.multiple_of(flag * size, size), size)


def project(n1, span, w_ref, b_ref, table_ref, q_ref, k_ref, v_ref):
    lanes = q_ref.shape[1]
    mine = half_at(ctx_flag(), lanes)
    cosine, sine = turn_lanes(table_ref[:, half_at(span, n1.shape[0])])
    q_ref[...] = turn(dot(n1, w_ref[0, :, mine]) + b_ref[0:1, mine], cosine, sine).astype(BF16)
    k_ref[...] = turn(dot(n1, w_ref[1, :, mine]) + b_ref[1:2, mine], cosine, sine).astype(BF16)
    v_ref[...] = (dot(n1, w_ref[2, :, mine]) + b_ref[2:3, mine]).astype(BF16)


def pieces(near_ref, pair_ref, step):
    core, size = core_flag(), near_ref.shape[0]
    step(half_at(core, size), near_ref[...])
    step(half_at(1 - core, size), pair_ref[...])


def other_kernel(near_ref, pair_ref, n1_o_ref, pack_ref, w_ref, b_ref, table_ref, up_ref,
                 n1_ref, n2_ref, q_o_ref, k_o_ref, v_o_ref, q_ref, k_ref, v_ref, act_ref, slope_ref):
    def norm(at, x):
        xhat, _ = standard(x.astype(F32))
        n1_ref[at] = (xhat * pack_ref[0:1] + pack_ref[1:2]).astype(BF16)
        n2_ref[at] = (xhat * pack_ref[2:3] + pack_ref[3:4]).astype(BF16)

    pieces(near_ref, pair_ref, norm)
    project(n1_o_ref[...], ctx_flag(), w_ref, b_ref, table_ref, q_o_ref, k_o_ref, v_o_ref)
    project(n1_ref[...], 1 - ctx_flag(), w_ref, b_ref, table_ref, q_ref, k_ref, v_ref)
    size = slope_ref.shape[1] // 2
    for j in range(2):
        mine = pl.ds(pl.multiple_of(ctx_flag() * 2 * size + j * size, size), size)
        at = slice(j * size, (j + 1) * size)
        act_ref[:, at], slope_ref[:, at] = activation(dot(n2_ref[...], up_ref[:, mine]) + pack_ref[4:5, mine])


def other_call(near, pair, n1, pack, w3, bias, table, up_w):
    rows, width = 2 * near.shape[0], near.shape[1]
    half = up_w.shape[1] // 2
    head = struct((rows, 2 * HEAD_DIM), BF16)
    outs = [struct((rows, width), BF16)] * 2 + [head] * 6 + [struct((rows, half), BF16), struct((rows, half), F32)]
    return fetched(other_kernel, (near, pair, n1, pack, w3, bias, table, up_w), outs, "other", 5e9)


EXTRA = 16


def unit_struct(rows, cols, extra=EXTRA):
    return struct((rows + extra, cols), BF16)


def own_rows(message):
    return message.shape[0] - message.shape[0] % (2 * EXTRA)


def fill(ref, *values):
    rows = own_rows(ref)
    at = 0
    for value in values:
        for first in range(0, value.shape[0], rows):
            ref[:rows, at : at + value.shape[1]] = value[first : first + rows]
            at += value.shape[1]
    if rows < ref.shape[0]:
        ref[rows:] = jnp.zeros((EXTRA, ref.shape[1]), ref.dtype)


def unfold(value, lanes, index, count):
    rows = own_rows(value)
    folds = [value[:rows, (index * count + i) * lanes : (index * count + i + 1) * lanes] for i in range(count)]
    return jnp.concatenate(folds, axis=0)


def weights_kernel(near_ref, pair_ref, act_o_ref, dy_o_ref, act_ref, slope_ref, down_ref, ow_ref,
                   gu_ref, ga_ref, gd_ref, dy_ref):
    hidden = slope_ref.shape[1]

    def put(at, dy):
        dy_ref[at] = dy

    pieces(near_ref, pair_ref, put)
    dy, dy_o = dy_ref[...], dy_o_ref[...]
    rows, lanes = dy.shape[0], ga_ref.shape[1]
    act_o, cols = act_o_ref[:, half_at(ctx_flag(), hidden)], gd_ref.shape[1]
    fill(gd_ref, (dot_tn(act_o, dy_o[:, cols:]) + dot_tn(act_ref[...], dy[:, cols:])).astype(BF16))
    gu_ref[...] = (dot_nt(dy, down_ref[half_at(ctx_flag(), hidden)]) * slope_ref[...]).astype(BF16)
    out_w = ow_ref[half_at(ctx_flag(), lanes)]
    ga_ref[half_at(ctx_flag(), rows)] = dot_nt(dy_o, out_w).astype(BF16)
    ga_ref[half_at(1 - ctx_flag(), rows)] = dot_nt(dy, out_w).astype(BF16)


def weights_call(near, pair, act_o, dy_o, act, slope, down_w, out_w):
    rows, width = dy_o.shape
    hidden = slope.shape[1]
    outs = [struct((rows, hidden), BF16), struct((2 * rows, 2 * HEAD_DIM), BF16)]
    outs.append(unit_struct(hidden, width // 2, EXTRA))
    arrays = (near, pair, act_o, dy_o, act, slope, down_w, out_w)
    return fetched(weights_kernel, arrays, outs, "weights", 4e9, 0, [pltpu.VMEM((rows, width), BF16)])


def in_order(own, other, axis=0):
    first = ctx_flag() == 0
    return jnp.concatenate([jnp.where(first, own, other), jnp.where(first, other, own)], axis=axis)


def attend_head(index, q_o_ref, k_o_ref, v_o_ref, q_x_ref, k_x_ref, v_x_ref, ga_ref, ids_o_ref, ids_x_ref, table_ref,
                q_ref, k_ref, v_ref, dk_ref, dv_ref, att_ref, gp_ref):
    rows, lanes = q_ref.shape
    cosine, sine = turn_lanes(table_ref[...])
    step = 256
    zero = jnp.zeros((), BF16)
    scale = HEAD_DIM ** (-0.5)
    q_ref[...] = in_order(q_o_ref[...], q_x_ref[...]) * jnp.asarray(scale, BF16)
    k_ref[...], v_ref[...] = in_order(k_o_ref[...], k_x_ref[...]), in_order(v_o_ref[...], v_x_ref[...])
    dk_ref[...] = jnp.zeros(dk_ref.shape, F32)
    dv_ref[...] = jnp.zeros(dv_ref.shape, F32)
    ids = in_order(ids_o_ref[...], ids_x_ref[...], axis=1)
    code = jnp.where(ids[1:2] == 1, ids[0:1], -1).astype(F32)
    doc = jnp.broadcast_to(ids[0:1].astype(F32), (8, rows)).T[:, 0:1]
    lane = lax.broadcasted_iota(jnp.int32, (1, lanes), 1)
    head = (lane // HEAD_DIM) == index
    for i in range(rows // step):
        at, upto = slice(i * step, (i + 1) * step), (i + 1) * step
        k, v = k_ref[:upto], v_ref[:upto]
        row = lax.broadcasted_iota(jnp.int32, (step, upto), 0) + i * step
        col = lax.broadcasted_iota(jnp.int32, (step, upto), 1)
        seen = ((col <= row) & (code[:, :upto] == doc[at])) | (col == row)
        bias = jnp.where(seen, 0.0, NEG)
        q, ga = q_ref[at], ga_ref[at]
        qh, gh = jnp.where(head, q, zero), jnp.where(head, ga, zero)
        scores = dot_nt(qh, k) + bias
        e = jnp.exp(scores - jnp.max(scores, axis=1, keepdims=True))
        p = e * (1.0 / jnp.sum(e, axis=1, keepdims=True))
        low = p.astype(BF16)
        att = jnp.where(head, dot(low, v), 0.0)
        delta = jnp.sum(att * gh.astype(F32), axis=1, keepdims=True)
        g = (p * (dot_nt(gh, v) - delta)).astype(BF16)
        query_grad = jnp.where(head, dot(g, k), 0.0)
        att_ref[at] = att.astype(BF16)
        gp_ref[0, at] = turn(query_grad * scale, cosine[at], -sine[at]).astype(BF16)
        dk_ref[:upto] += dot_tn(g, qh)
        dv_ref[:upto] += dot_tn(low, gh)
    gp_ref[1] = turn(dk_ref[...], cosine, -sine).astype(BF16)
    gp_ref[2] = dv_ref[...].astype(BF16)


def head_scratch(rows, lanes):
    return [pltpu.VMEM((rows, lanes), BF16)] * 3 + [pltpu.VMEM((rows, lanes), F32)] * 2


def first_head_kernel(*refs):
    attend_head(0, *refs[:10], *refs[12:], *refs[10:12])


def first_head_call(own, other, ga, ids, ids_x, table):
    arrays = (*own, *other, ga, ids, ids_x, table)
    outs = [struct(ga.shape, BF16), struct((3,) + ga.shape, BF16)]
    return fetched(first_head_kernel, arrays, outs, "first_head", 1024, 0, head_scratch(*ga.shape))


def attend_kernel(*refs):
    heads, (att_in, gp_in), later, outs = refs[:10], refs[10:12], refs[12:21], refs[21:27]
    att_ref, gp_ref, *held, sems = refs[27 + 5 :]
    keep_ref, send_ref, qk_grad_ref, vo_grad_ref, *up_refs = outs
    n1_o_ref, n1_x_ref, dy_o_ref, dy_x_ref, n2_o_ref, n2_x_ref, gu_o_ref, gu_x_ref = held
    span, hidden = n1_o_ref.shape[0], gu_x_ref.shape[1]
    mine, theirs = half_at(ctx_flag(), span), half_at(1 - ctx_flag(), span)
    n1_o, n1_x, dy_o, near, pair, n2_o, n2_x, gu_o, gu_x = later
    core, half = core_flag(), span // 2
    copies = [
        pltpu.make_async_copy(src, dst, sems.at[i])
        for i, (src, dst) in enumerate((
            (n1_o, n1_o_ref), (n1_x, n1_x_ref), (dy_o, dy_o_ref),
            (near, dy_x_ref.at[half_at(core, half)]), (pair, dy_x_ref.at[half_at(1 - core, half)]),
            (n2_o, n2_o_ref), (n2_x, n2_x_ref), (gu_o.at[:, half_at(ctx_flag(), hidden)], gu_o_ref), (gu_x, gu_x_ref),
        ))
    ]
    for copy in copies:
        copy.start()
    attend_head(1, *heads, *refs[27 : 27 + 5], att_ref, gp_ref)
    for ref, at in ((keep_ref, mine), (send_ref, theirs)):
        ref[0] = att_ref[at] + att_in[at]
        for t in range(3):
            ref[t + 1] = gp_ref[t, at] + gp_in[t, at]
    for copy in copies:
        copy.wait()
    q_grad, k_grad, v_grad = [
        (dot_tn(n1_o_ref[...], keep_ref[t]) + dot_tn(n1_x_ref[...], send_ref[t])).astype(BF16) for t in (1, 2, 3)
    ]
    o_grad = (dot_tn(dy_o_ref[...], keep_ref[0]) + dot_tn(dy_x_ref[...], send_ref[0])).astype(BF16)
    fill(qk_grad_ref, q_grad, k_grad)
    fill(vo_grad_ref, v_grad, o_grad)
    gu_o, gu_x = gu_o_ref[...], gu_x_ref[...]
    for i, ref in enumerate(up_refs):
        at = slice(i * own_rows(ref), (i + 1) * own_rows(ref))
        fill(ref, (dot_tn(n2_o_ref[:, at], gu_o) + dot_tn(n2_x_ref[:, at], gu_x)).astype(BF16))


def attend_call(own, other, ga, ids, ids_x, table, first, *later):
    arrays = (*own, *other, ga, ids, ids_x, table, *first, *later)
    rows, lanes = ga.shape
    span, width = later[0].shape
    hidden = later[-1].shape[1]
    outs = [struct((4, span, lanes), BF16)] * 2 + [unit_struct(width // 2, 4 * lanes) for _ in range(2)]
    outs += [unit_struct(width // 2, hidden) for _ in range(2)]
    scratch = head_scratch(rows, lanes) + [pltpu.VMEM((rows, lanes), BF16), pltpu.VMEM((3, rows, lanes), BF16)]
    scratch += [pltpu.VMEM((span, width), BF16)] * 6 + [pltpu.VMEM((span, hidden), BF16)] * 2
    scratch.append(pltpu.SemaphoreType.DMA((len(later),)))
    return fetched(attend_kernel, arrays, outs, "attend", 1024, len(later), scratch)


def branch_sums_kernel(act_ref, gu_ref, dy_ref, x_ref, up_ref, down_ref, out_ref, grad_ref, sums_ref):
    two = dot_nt(gu_ref[...], up_ref[...])
    xhat, _ = standard(x_ref[...].astype(F32))
    grad_ref[...] = two
    out_ref[...] = dot(act_ref[...], down_ref[...])
    rows = [jnp.sum(v, axis=0, keepdims=True) for v in (two * xhat, two, dy_ref[...].astype(F32))]
    sums_ref[...] = jnp.concatenate(rows + [jnp.zeros((5, two.shape[1]), F32)], axis=0)


def branch_sums_call(act, gu, dy, x, up_w, down_w):
    outs = [struct(x.shape, F32)] * 2 + [struct((8, x.shape[1]), F32)]
    return small(branch_sums_kernel, (act, gu, dy, x, up_w, down_w), outs, "branch_sums", 24)


def sums_kernel(mine_ref, recv_ref, out_ref, grad_ref, sums_ref, x_ref, pack_ref, w_ref, ow_ref, gub_ref,
                keep_ref, send_ref, vec_ref):
    lanes = mine_ref.shape[2]
    heads = [(mine_ref, half_at(ctx_flag(), lanes)), (recv_ref, half_at(1 - ctx_flag(), lanes))]
    out, one = out_ref[...], None
    biases = []
    for ref, at in heads:
        out = out + dot(ref[0], ow_ref[at])
        for t in range(3):
            term = dot_nt(ref[t + 1], w_ref[t, :, at])
            one = term if one is None else one + term
        biases.append([jnp.sum(ref[t + 1].astype(F32), axis=0, keepdims=True) for t in range(3)])
    first = ctx_flag() == 0
    pairs = [(jnp.where(first, m, r), jnp.where(first, r, m)) for m, r in zip(*biases)]
    heads_bias = jnp.concatenate([half for pair in pairs for half in pair], axis=1)
    zeros = jnp.zeros((1, out.shape[1] - heads_bias.shape[1]), F32)
    xhat, _ = standard(x_ref[...].astype(F32))
    sums = sums_ref[...]
    rows = [jnp.sum(one * xhat, axis=0, keepdims=True), jnp.sum(one, axis=0, keepdims=True), sums[0:3], gub_ref[...]]
    rows += [jnp.concatenate([heads_bias, zeros], axis=1), jnp.zeros_like(sums[0:1])]
    vec = jnp.concatenate(rows, axis=0)
    cols = vec_ref.shape[1]
    vec_ref[...] = jnp.concatenate([vec[:, :cols], vec[:, cols:]], axis=0).astype(BF16)
    rows = x_ref.shape[0] // 2
    for at, value in ((0, out), (rows, one * pack_ref[0:1] + grad_ref[...] * pack_ref[2:3])):
        keep_ref[at : at + rows], send_ref[at : at + rows] = halves(core_flag(), value.astype(BF16))


def sums_call(mine, recv, branch, x, pack, w3, out_w, gub):
    rows, width = x.shape
    both = struct((rows, width), BF16)
    outs = [both, both, struct((EXTRA, width // 2), BF16)]
    return small(sums_kernel, (mine, recv, *branch, x, pack, w3, out_w, gub), outs, "sums", 32)


def ride_kernel(grad_ref, vec_ref, o_ref):
    rows = grad_ref.shape[0] - EXTRA
    o_ref[:rows] = grad_ref[:rows]
    o_ref[rows:] = vec_ref[...]


def ride(grad, vec):
    return small(ride_kernel, (grad, vec), [struct(grad.shape, BF16)], "ride")[0]


def place_ride_kernel(mine_ref, other_ref, *refs):
    grad_ref, vec_ref = refs[-2:]
    count, rows, lanes = grad_ref.shape
    value = jnp.where(ctx_flag() == pl.program_id(0), mine_ref[...], other_ref[...]).astype(F32)
    folds = rows // own_rows(mine_ref)
    for t in range(count):
        grad_ref[t] = unfold(value, lanes, t, folds)
    at = slice(mine_ref.shape[0] - EXTRA, mine_ref.shape[0])
    vec_ref[...] = mine_ref[at].astype(F32) + other_ref[at].astype(F32)


def rows_kernel(a_ref, b_ref, v_ref, *refs):
    heads_ref = refs[-1]
    held = jnp.concatenate([v_ref[:8], v_ref[8:]], axis=1)
    total = jnp.concatenate([a_ref[:8] + b_ref[:8], a_ref[8:] + b_ref[8:]], axis=1)
    for r, ref in enumerate(refs[:-1]):
        ref[...] = total[r : r + 1] if r < 4 else held[5:6] if r == 5 else held[4:5]
    cols = heads_ref.shape[1]
    for t in range(heads_ref.shape[0]):
        heads_ref[t : t + 1] = held[6:7, t * cols : (t + 1) * cols]


def rows_call(local, a, b, v):
    row = struct((1, 2 * a.shape[1]), F32)
    return small(rows_kernel, (a, b, v), [row] * 7 + [struct((3, local), F32)], "rows")


def place_sum_kernel(mine_ref, other_ref, *refs):
    rows = refs[-1].shape[0]
    refs[-1][...] = mine_ref[:rows].astype(F32) + other_ref[:rows].astype(F32)


def place_pair_kernel(mine_ref, other_ref, *refs):
    value = jnp.where(ctx_flag() == pl.program_id(0), mine_ref[...], other_ref[...]).astype(F32)
    heads_ref, out_ref = refs[-2:]
    lanes = heads_ref.shape[2]
    folds = heads_ref.shape[1] // own_rows(mine_ref)
    heads_ref[0] = unfold(value, lanes, 0, folds)
    out_ref[...] = unfold(value, lanes, 1, folds).T


def results_kernel(mine_ref, other_ref, x_ref, dy_ref, pack_ref, out_ref, grad_ref):
    rows = x_ref.shape[0] // 2
    bias = pack_ref[5:6] + pack_ref[6:7]
    first = core_flag() == 0
    for i in range(2):
        at = slice(i * rows, (i + 1) * rows)
        here, there = (mine_ref, other_ref) if i == 0 else (other_ref, mine_ref)
        out, grad = [
            jnp.where(first, here[part], there[part]).astype(F32) for part in (slice(0, rows), slice(rows, 2 * rows))
        ]
        x = x_ref[at].astype(F32)
        out_ref[at] = (x + out + bias).astype(BF16)
        xhat, inverse = standard(x)
        mean = jnp.mean(grad, axis=-1, keepdims=True)
        along = jnp.mean(grad * xhat, axis=-1, keepdims=True)
        grad_ref[at] = (dy_ref[at].astype(F32) + inverse * (grad - mean - xhat * along)).astype(BF16)


def results_call(mine, other, x, dy, pack):
    return small(results_kernel, (mine, other, x, dy, pack), [struct(x.shape, BF16)] * 2, "results", 24)


INWARD = [(0, 1), (3, 2)]
MIDDLE = [(1, 2), (2, 1)]
OUTWARD = [(1, 0), (2, 3)]
SWAP = [(0, 1), (1, 0)]
CORES = [(i, i ^ 1) for i in range(4)]
CHIPS = [(i, i ^ 2) for i in range(4)]


class Sequence:
    def __init__(self):
        self.last = None

    def tied(self, operands):
        if self.last is None:
            return operands
        return lax.optimization_barrier((operands, self.last))[0]

    def __call__(self, step, *operands):
        result = step(*self.tied(operands))
        self.last = jax.tree.leaves(result)[0]
        return result

    def send(self, value, axis, perm):
        return lax.ppermute(self.tied(value), axis, perm)

    def arrived(self, value):
        value = self.tied(value)
        self.last = value
        return value


def turn_table(positions):
    half = ROT // 2
    inverse = jnp.exp(jnp.arange(half, dtype=F32) * (-2.0 * jnp.log(10000.0) / ROT))
    angles = inverse[:, None] * positions.astype(F32)[None, :]
    return jnp.concatenate([jnp.cos(angles), jnp.sin(angles)], axis=0)


def line_then_ctx(run, x, finish):
    r = yield "dp", INWARD, run.tied(x)
    x = run(add, x, r)
    r = yield "dp", MIDDLE, x
    x = run(add, x, r)
    r = yield "dp", OUTWARD, x
    x = run(choose, x, r)
    r = yield "ctx", SWAP, x
    finish(x, r)


def over_tensor(run, mine, other, finish):
    r = yield "tensor", CORES, run.tied(other)
    mine = run(add, mine, r)
    r = yield "tensor", CHIPS, mine
    mine = run(add, mine, r)
    r = yield "tensor", CORES, mine
    finish(mine, r)


def vectors_over_tensor(run, local, vec, finish):
    r = yield "tensor", CORES, run.tied(vec)
    x = run(add, vec, r)
    r = yield "tensor", CHIPS, x
    finish(run(functools.partial(rows_call, local), x, r, vec))


def gather_span(run, x, finish):
    half = x.shape[0] // 2
    near = yield "ctx", SWAP, lax.dynamic_slice_in_dim(run.tied(x), lax.axis_index("tensor") % 2 * half, half, 0)
    near = run.arrived(near)
    pair = yield "tensor", CORES, near
    finish(near, pair)


class Unit:
    def __init__(self, run, steps):
        self.run, self.steps, self.message = run, steps, None

    def request(self):
        try:
            return self.steps.send(self.message)
        except StopIteration:
            return None

    def advance(self):
        request = self.request()
        if request:
            axis, perm, value = request
            self.message = lax.ppermute(value, axis, perm)

    def advance_with(self, other):
        (_, _, inward), (_, _, outward) = self.request(), other.request()
        self.message = other.message = lax.ppermute(self.run(choose, outward, inward), "dp", INWARD + OUTWARD)

    def wait(self):
        self.message = self.run.arrived(self.message)


class Held:
    pass


def two_spans(
    tokens, segments, padding, cotangent, norm1_gain, norm1_shift, norm2_gain, norm2_shift,
    qkv_weight, qkv_bias, out_weight, out_bias, up_weight, up_bias, down_weight, down_bias,
):
    x, dy = tokens[0], cotangent[0]
    rows, width = x.shape
    local = qkv_weight.shape[2]
    hidden = up_weight.shape[1]
    lanes = 2 * HEAD_DIM
    row = lambda v: v.reshape(1, -1)
    w3 = jnp.transpose(qkv_weight, (1, 0, 2))
    run = Sequence()
    s, u = Held(), Held()
    dests = {}
    shapes = {"down": (hidden, width), "up": (width, hidden), "qkv": (3, width, local), "out": (local, width),
              "vec": (EXTRA, width // 2)}

    def open_unit(name, steps, *operands):
        setattr(u, name, Unit(run, steps(run, *operands)))

    def placing(names, kernel, count, blocks, indices):
        def finish(a, b):
            held = [n for n in names if n in dests]

            def step(a, b, *old):
                return pl.pallas_call(
                    kernel,
                    grid=(count,),
                    in_specs=[resident()] * 2 + [pl.BlockSpec(memory_space=pl.ANY)] * len(old),
                    out_specs=[pl.BlockSpec(block, index) for block, index in zip(blocks, indices)],
                    out_shape=[struct(shapes[n], F32) for n in names],
                    input_output_aliases={2 + i: names.index(n) for i, n in enumerate(held)},
                    compiler_params=params(24),
                    cost_estimate=cost(0, 0),
                    name="place",
                )(a, b, *old)

            dests.update(zip(names, run(step, a, b, *[dests[n] for n in held])))

        return finish

    open_unit("tk", gather_span, x, lambda *p: s.__dict__.update(tokens=p))
    open_unit("dy", gather_span, dy, lambda *p: s.__dict__.update(dy=p))

    def ids_0():
        ids = jnp.concatenate([segments, padding], axis=0)
        s.ids = ids, run.send(ids, "ctx", SWAP)

    def ids_w():
        s.ids = s.ids[0], run.arrived(s.ids[1])

    def early():
        s.pack = jnp.stack([norm1_gain, norm1_shift, norm2_gain, norm2_shift, up_bias, out_bias, down_bias])
        s.n1, s.n2, s.act, s.gu, s.gub, grad = run(early_call, x, dy, up_weight, down_weight, s.pack)
        open_early(0, grad)

    def open_early(i, grad):
        open_unit(f"E{i}", line_then_ctx, grad, placing(
            ["down"], place_sum_kernel, 1, [(hidden // 2, width // 2)], [lambda _: (i, 0)]))

    def own():
        s.act, s.gu, s.gub, grad = run(
            own_call, s.n2, dy, up_weight, down_weight, s.pack, s.act, s.gu, s.gub)
        open_early(1, grad)

    def other():
        u.tk.advance()
        s.n1x, s.n2x, *heads, s.actx, s.slope = run(
            other_call, *s.tokens, s.n1, s.pack, w3, qkv_bias, s.table, up_weight)
        s.qkv, s.qkvx = heads[:3], heads[3:]

    def tables():
        s.table = run(turn_table, jnp.arange(2 * rows, dtype=jnp.int32))

    def weights():
        u.dy.advance()
        s.gux, s.ga, grad = run(
            weights_call, *s.dy, s.act, dy, s.actx, s.slope, down_weight, out_weight)
        open_unit("D1", line_then_ctx, grad, placing(
            ["down"], place_halves_kernel, 2, [(hidden // 2, width // 2)], [lambda i: (i, 1)]))

    def first_head():
        s.first = run(lambda *a: first_head_call(a[:3], a[3:6], *a[6:]), *s.qkv, *s.qkvx, s.ga, *s.ids, s.table)

    def attend():
        s.mine, s.theirs, s.qk, vo_grad, *ups = run(
            lambda *a: attend_call(a[:3], a[3:6], *a[6:10], a[10:12], *a[12:]),
            *s.qkv, *s.qkvx, s.ga, *s.ids, s.table, *s.first,
            s.n1, s.n1x, dy, *s.dy, s.n2, s.n2x, s.gu, s.gux)
        open_unit("Q1", line_then_ctx, vo_grad, placing(
            ["qkv", "out"], place_pair_kernel, 2, [(1, width, lanes), (lanes, width)],
            [lambda i: (2, 0, i), lambda i: (i, 0)]))
        for j, grad in enumerate(ups):
            open_unit(f"U{j}", line_then_ctx, grad, placing(
                ["up"], place_halves_kernel, 2, [(width // 2, hidden // 2)], [lambda i, j=j: (j, i)]))

    def gpx_0():
        s.recv = run.send(s.theirs, "ctx", SWAP)

    def gpx_w():
        s.recv = run.arrived(s.recv)

    def branch_sums():
        s.branch = run(branch_sums_call, s.act, s.gu, dy, x, up_weight, down_weight)

    def sums():
        keep, send, s.vec = run(sums_call, s.mine, s.recv, s.branch, x, s.pack, w3, out_weight, s.gub)

        def finish(a, b):
            s.block_output, s.input_grad = run(lambda a, b: results_call(a, b, x, dy, s.pack), a, b)

        open_unit("both", over_tensor, keep, send, finish)

    def join():
        both = run(ride, s.qk, s.vec)
        put = placing(
            ["qkv", "vec"], place_ride_kernel, 2, [(2, width, lanes), s.vec.shape], [lambda i: (0, 0, i), lambda i: (0, 0)])

        def finish(a, b):
            put(a, b)
            open_unit("vec", vectors_over_tensor, local, dests["vec"], lambda rows: s.__dict__.update(rows=rows))

        open_unit("Q0", line_then_ctx, both, finish)

    u.tk.advance()
    early()
    u.E0.advance()
    u.dy.advance()
    own()
    tables()
    u.tk.advance()
    ids_0()
    other()
    u.E0.wait()
    u.E1.advance()
    u.E0.advance()
    u.dy.advance()
    weights()
    u.D1.advance()
    first_head()
    ids_w()
    u.E0.advance()
    u.E1.advance()
    attend()
    gpx_0()
    u.D1.wait()
    u.U0.advance_with(u.E1)
    u.D1.advance()
    branch_sums()
    u.E0.wait()
    u.E0.advance()
    gpx_w()
    sums()
    join()
    u.U0.wait()
    u.Q0.advance_with(u.D1)
    u.U0.advance()
    u.E1.advance()
    u.both.advance()
    u.E0.advance()
    u.Q0.wait()
    u.Q1.advance_with(u.U0)
    u.Q0.advance()
    u.D1.advance()
    u.both.advance()
    u.E1.advance()
    u.Q1.wait()
    u.U1.advance_with(u.Q0)
    u.Q1.advance()
    u.U0.advance()
    u.D1.advance()
    u.U1.wait()
    u.U1.advance()
    u.Q1.advance()
    u.Q0.advance()
    u.both.advance()
    u.U0.advance()
    u.Q0.advance()
    u.U1.advance()
    u.Q1.advance()
    u.vec.advance()
    u.U1.advance()
    u.both.advance()
    u.Q1.advance()
    u.vec.advance()
    u.vec.advance()
    u.U1.advance()
    *rows, heads_bias = s.rows
    gain1, shift1, gain2, shift2, dy_sum, up_sum, dy_same = [r.reshape(-1) for r in rows]
    return (
        s.block_output[None],
        s.input_grad[None],
        gain1, shift1, gain2, shift2,
        jnp.transpose(dests["qkv"], (1, 0, 2)),
        heads_bias,
        dests["out"],
        dy_sum,
        dests["up"],
        up_sum,
        dests["down"],
        dy_same,
    )


def fits(mesh):
    return dict(mesh.shape) == {"dp": 4, "ctx": 2, "tensor": 4}


def solution(mesh):
    return jax.shard_map(
        two_spans if fits(mesh) else on_device,
        mesh=mesh,
        in_specs=(
            P("dp", "ctx", None),
            P("dp", "ctx"),
            P("dp", "ctx"),
            P("dp", "ctx", None),
            P(),
            P(),
            P(),
            P(),
            P(None, None, "tensor"),
            P(None, "tensor"),
            P("tensor", None),
            P(),
            P(None, "tensor"),
            P("tensor"),
            P("tensor", None),
            P(),
        ),
        out_specs=(
            P("dp", "ctx", None),
            P("dp", "ctx", None),
            P(),
            P(),
            P(),
            P(),
            P(None, None, "tensor"),
            P(None, "tensor"),
            P("tensor", None),
            P(),
            P(None, "tensor"),
            P("tensor"),
            P("tensor", None),
            P(),
        ),
        check_vma=False,
    )
```
